32 devices in a mesh: ctx: 8 (over y, x, core), fsdp: 4 (over z).
Axes of the slice: x: 2, y: 2, z: 4, core: 2. Of those that a mesh axis runs over, the one named last changes fastest.
Arguments:
- states: bfloat16 [4, 4096, 1024], P('fsdp', 'ctx'), may hold values from -6 to 6
- positions: int32 [4, 4096], P('fsdp', 'ctx'), may hold values from 0 to 2303, as said below
- segments: int32 [4, 4096], P('fsdp', 'ctx'), may hold values from 0 to 8, as said below
- encoded: bfloat16 [4, 512, 1024], P('fsdp', 'ctx'), may hold values from -6 to 6
- cotangent: bfloat16 [4, 4096, 1024], P('fsdp', 'ctx'), may hold values from -6 to 6
- self_gain: bfloat16 [1024], P('fsdp'), may hold values from 0.099609375 to 1.8984375
- self_query: bfloat16 [1024, 1024], P('fsdp'), may hold values from -0.0234375 to 0.0234375
- self_key: bfloat16 [1024, 1024], P('fsdp'), may hold values from -0.1875 to 0.1875
- self_value: bfloat16 [1024, 1024], P('fsdp'), may hold values from -0.1875 to 0.1875
- self_output: bfloat16 [1024, 1024], P('fsdp'), may hold values from -3 to 3
- bias_table: bfloat16 [32, 16], P('fsdp'), may hold values from -4 to 4
- cross_gain: bfloat16 [1024], P('fsdp'), may hold values from 0.099609375 to 1.8984375
- cross_query: bfloat16 [1024, 1024], P('fsdp'), may hold values from -0.0234375 to 0.0234375
- cross_key: bfloat16 [1024, 1024], P('fsdp'), may hold values from -0.1875 to 0.1875
- cross_value: bfloat16 [1024, 1024], P('fsdp'), may hold values from -0.1875 to 0.1875
- cross_output: bfloat16 [1024, 1024], P('fsdp'), may hold values from -2 to 2
- feed_gain: bfloat16 [1024], P('fsdp'), may hold values from 0.099609375 to 1.8984375
- gate_weight: bfloat16 [1024, 2816], P('fsdp'), may hold values from -0.1875 to 0.1875
- up_weight: bfloat16 [1024, 2816], P('fsdp'), may hold values from -0.1875 to 0.1875
- down_weight: bfloat16 [2816, 1024], P('fsdp'), may hold values from -0.109375 to 0.109375
Outputs:
- layer_out: bfloat16 [4, 4096, 1024], P('fsdp', 'ctx')
- states_grad: float32 [4, 4096, 1024], P('fsdp', 'ctx')
- encoded_grad: float32 [4, 512, 1024], P('fsdp', 'ctx')
- self_gain_grad: float32 [1024], P('fsdp')
- self_query_grad: float32 [1024, 1024], P('fsdp')
- self_key_grad: float32 [1024, 1024], P('fsdp')
- self_value_grad: float32 [1024, 1024], P('fsdp')
- self_output_grad: float32 [1024, 1024], P('fsdp')
- bias_table_grad: float32 [32, 16], P('fsdp')
- cross_gain_grad: float32 [1024], P('fsdp')
- cross_query_grad: float32 [1024, 1024], P('fsdp')
- cross_key_grad: float32 [1024, 1024], P('fsdp')
- cross_value_grad: float32 [1024, 1024], P('fsdp')
- cross_output_grad: float32 [1024, 1024], P('fsdp')
- feed_gain_grad: float32 [1024], P('fsdp')
- gate_weight_grad: float32 [1024, 2816], P('fsdp')
- up_weight_grad: float32 [1024, 2816], P('fsdp')
- down_weight_grad: float32 [2816, 1024], P('fsdp')
The draws below stay inside these ranges and needn't reach their ends.
Inputs may be any that keep to these rules, and one draw needn't show every extreme that they name: In each group the 4096 tokens come in aligned blocks of 128; a block holds 128 consecutive tokens of the prompt (segment 0, positions 0 to 2047) or of one continuation c (segment c, positions 2048 to 2303); every block of the group occurs once, in an order drawn from the seed, and the first and the last block are prompt blocks. `segments`: the segment of each token, laid out as described for positions.
All inputs are finite; a program needn't handle non-finite values.
Results may differ from the reference program's by a relative error of at most 0.028.
Values may be sent and summed in bfloat16 or wider, within the bound.
No kernel may reach another device: no remote copies, remote signals or barrier semaphores. Data moves between devices by JAX's collectives and lax.ppermute only.
A program may use at most 320 MiB of HBM per device.

```python
import math
import jax
import jax.numpy as jnp
from jax import lax

D = 1024
H = 16
DK = 64
FF = 2816
BUCKETS = 32
DISTANCE = 128
PROMPT = 2048
CLEN = 256
BLOCK = 128
ENC = 512
HD = 1024
GROUP_TOK = 4096
GROUPS = 4


def block_layout(key):
    count = GROUP_TOK // BLOCK
    prompt_blocks = PROMPT // BLOCK

    def arrange(group_key):
        first_key, second_key, third_key = jax.random.split(group_key, 3)
        middle = jax.random.permutation(first_key, count - 2) + 1
        marks = jnp.zeros((count,), jnp.int32)
        marks = marks.at[0].set(1).at[count - 1].set(1)
        marks = marks.at[middle[:prompt_blocks - 2]].set(1)
        slots = jnp.arange(count, dtype=jnp.int32)
        order = jnp.argsort((1 - marks) * count + slots)
        chosen = jnp.concatenate([jax.random.permutation(second_key, prompt_blocks), jax.random.permutation(third_key, count - prompt_blocks) + prompt_blocks]).astype(jnp.int32)
        owner = jnp.zeros((count,), jnp.int32).at[order].set(chosen)
        index = (owner[:, None] * BLOCK + jnp.arange(BLOCK, dtype=jnp.int32)[None, :]).reshape(-1)
        later = index - PROMPT
        place = jnp.where(index < PROMPT, index, PROMPT + later % CLEN)
        label = jnp.where(index < PROMPT, 0, 1 + later // CLEN)
        return (place.astype(jnp.int32), label.astype(jnp.int32))
    return jax.vmap(arrange)(jax.random.split(key, GROUPS))


def draw_positions(key, part):
    place, label = block_layout(key)
    return place


def draw_segments(key, part):
    place, label = block_layout(key)
    return label


def block_levels(stream_key, extent, shards, low, high):
    level, own = 1.0, jax.random.fold_in(stream_key, 6)
    for position, shards_of in shards:
        steps = jnp.exp(jax.random.uniform(jax.random.fold_in(own, position), (shards_of,), jnp.float32, low / len(shards), high / len(shards)))
        level = level * jnp.repeat(steps, extent[position] // shards_of).reshape([-1 if axis == position else 1 for axis in range(len(extent))])
    return level


def normal_values(own_key, extent, deviation, bound, shards=(), held_as=jnp.bfloat16):
    drawn = jax.random.normal(own_key, extent, jnp.float32) * deviation
    if len(shards) > 0:
        drawn = block_levels(own_key, extent, shards, -0.22, 0.18) * drawn
    return jnp.clip(drawn, min=-bound, max=bound).astype(held_as)


def setup_inputs(seed: int = 0) -> dict:
    seeds = jax.random.split(jax.random.key(seed), 21)
    states = normal_values(seeds[0], (GROUPS, GROUP_TOK, D), 1.0, 6.0, ((0, 4), (1, 8)))
    positions = draw_positions(jax.random.fold_in(seeds[20], 71), 0)
    segments = draw_segments(jax.random.fold_in(seeds[20], 71), 0)
    encoded = normal_values(seeds[3], (GROUPS, ENC, D), 1.0, 6.0, ((0, 4), (1, 8)))
    cotangent = normal_values(seeds[4], (GROUPS, GROUP_TOK, D), 1.0, 6.0, ((0, 4), (1, 8)))
    self_gain = jnp.clip(1.0 + 0.18 * jax.random.normal(seeds[5], (D,), jnp.float32), 0.099609375, 1.8984375).astype(jnp.bfloat16)
    self_query = normal_values(seeds[6], (D, HD), (D * DK) ** -0.5, 0.0234375, ((0, 4),))
    self_key = normal_values(seeds[7], (D, HD), D ** -0.5, 0.1875, ((0, 4),))
    self_value = normal_values(seeds[8], (D, HD), D ** -0.5, 0.1875, ((0, 4),))
    self_output = normal_values(seeds[9], (HD, D), (max(HD // 256, 1)) ** -0.5, 3.0, ((0, 4),))
    bias_table = normal_values(seeds[10], (BUCKETS, H), 1.0, 4.0, ((0, 4),))
    cross_gain = jnp.clip(1.0 + 0.18 * jax.random.normal(seeds[11], (D,), jnp.float32), 0.099609375, 1.8984375).astype(jnp.bfloat16)
    cross_query = normal_values(seeds[12], (D, HD), (D * DK) ** -0.5, 0.0234375, ((0, 4),))
    cross_key = normal_values(seeds[13], (D, HD), D ** -0.5, 0.1875, ((0, 4),))
    cross_value = normal_values(seeds[14], (D, HD), D ** -0.5, 0.1875, ((0, 4),))
    cross_output = normal_values(seeds[15], (HD, D), (max(HD // 128, 1)) ** -0.5, 2.0, ((0, 4),))
    feed_gain = jnp.clip(1.0 + 0.18 * jax.random.normal(seeds[16], (D,), jnp.float32), 0.099609375, 1.8984375).astype(jnp.bfloat16)
    gate_weight = normal_values(seeds[17], (D, FF), D ** -0.5, 0.1875, ((0, 4),))
    up_weight = normal_values(seeds[18], (D, FF), D ** -0.5, 0.1875, ((0, 4),))
    down_weight = normal_values(seeds[19], (FF, D), FF ** -0.5, 0.109375, ((0, 4),))
    return {"states": states, "positions": positions, "segments": segments, "encoded": encoded, "cotangent": cotangent, "self_gain": self_gain, "self_query": self_query, "self_key": self_key, "self_value": self_value, "self_output": self_output, "bias_table": bias_table, "cross_gain": cross_gain, "cross_query": cross_query, "cross_key": cross_key, "cross_value": cross_value, "cross_output": cross_output, "feed_gain": feed_gain, "gate_weight": gate_weight, "up_weight": up_weight, "down_weight": down_weight}


@jax.custom_vjp
def low(v):
    return lax.optimization_barrier(v.astype(jnp.bfloat16)).astype(jnp.float32)

@jax.custom_vjp
def low_back(v):
    return v

def low_keep(v):
    return (low(v), None)

def low_pass(kept, grad):
    return (grad,)

def back_keep(v):
    return (v, None)

def back_low(kept, grad):
    return (low(grad),)
low.defvjp(low_keep, low_pass)
low_back.defvjp(back_keep, back_low)
highest = lax.Precision.HIGHEST
epsilon = 1e-06
masked_value = -1e+30
gelu_scale = math.sqrt(2.0 / math.pi)

def rounded_both(value):
    return low(low_back(value))

def product(left, right):
    return jnp.dot(left, right, precision=highest)

def norm_rows(value, gain):
    return value * lax.rsqrt(lax.optimization_barrier(jnp.mean(value * value, axis=-1, keepdims=True)) + epsilon) * gain

def gelu_tanh(value):
    return 0.5 * value * (1.0 + jnp.tanh(gelu_scale * (value + 0.044715 * value * value * value)))

def bucket_edges():
    half_count = BUCKETS // 2
    return [math.ceil(half_count * (DISTANCE / half_count) ** (edge_number / half_count)) for edge_number in range(1, half_count)]

def relative_bucket(distance):
    bucket = jnp.minimum(distance, BUCKETS // 2)
    for edge_value in bucket_edges():
        bucket = bucket + (distance >= edge_value).astype(jnp.int32)
    return bucket

def softmax_rows(scores):
    highest_score = lax.optimization_barrier(jnp.max(scores, axis=-1, keepdims=True))
    expo = jnp.exp(scores - highest_score)
    return expo / lax.optimization_barrier(jnp.sum(expo, axis=-1, keepdims=True))

def self_attention(queries, keys, values, places, labels, table):
    length = queries.shape[0]
    stride = math.gcd(256, length)

    def block_rows(offset):
        block_queries = lax.dynamic_slice_in_dim(queries, offset, stride, 0)
        block_places = lax.dynamic_slice_in_dim(places, offset, stride, 0)
        block_labels = lax.dynamic_slice_in_dim(labels, offset, stride, 0)
        scores = jnp.einsum('qhd,khd->hqk', block_queries, keys, precision=highest)
        distance = jnp.maximum(block_places[:, None] - places[None, :], 0)
        scores = scores + jnp.transpose(jnp.take(table, relative_bucket(distance), axis=0), (2, 0, 1))
        scores = low_back(scores)
        allowed = ((labels[None, :] == 0) | (labels[None, :] == block_labels[:, None])) & (places[None, :] <= block_places[:, None])
        weights = low(softmax_rows(jnp.where(allowed[None], scores, masked_value)))
        return jnp.einsum('hqk,khd->qhd', weights, values, precision=highest)
    offsets = jnp.arange(length // stride, dtype=jnp.int32) * stride
    blocks = lax.map(jax.checkpoint(block_rows), offsets)
    return blocks.reshape(length, -1)

def cross_attention(queries, keys, values):
    length = queries.shape[0]
    stride = math.gcd(256, length)

    def block_rows(offset):
        block_queries = lax.dynamic_slice_in_dim(queries, offset, stride, 0)
        scores = low_back(jnp.einsum('qhd,khd->hqk', block_queries, keys, precision=highest))
        weights = low(softmax_rows(scores))
        return jnp.einsum('hqk,khd->qhd', weights, values, precision=highest)
    offsets = jnp.arange(length // stride, dtype=jnp.int32) * stride
    blocks = lax.map(jax.checkpoint(block_rows), offsets)
    return blocks.reshape(length, -1)

def layer_forward(inputs, sources, places, labels, weights):
    gain_first, query_matrix, key_matrix, value_matrix, output_matrix, table, gain_second, cross_query_matrix, cross_key_matrix, cross_value_matrix, cross_output_matrix, gain_third, gate_matrix, up_matrix, down_matrix = weights
    head_count = table.shape[1]
    head_size = query_matrix.shape[1] // head_count

    def split_heads(value):
        return value.reshape(value.shape[0], head_count, head_size)
    first = low(norm_rows(inputs, gain_first))
    queries = split_heads(rounded_both(product(first, query_matrix)))
    keys = split_heads(rounded_both(product(first, key_matrix)))
    values = split_heads(rounded_both(product(first, value_matrix)))
    attended = rounded_both(self_attention(queries, keys, values, places, labels, table))
    after_self = inputs + low_back(product(attended, output_matrix))
    second = low(norm_rows(after_self, gain_second))
    cross_queries = split_heads(rounded_both(product(second, cross_query_matrix)))
    cross_keys = split_heads(rounded_both(product(sources, cross_key_matrix)))
    cross_values = split_heads(rounded_both(product(sources, cross_value_matrix)))
    cross_out = rounded_both(cross_attention(cross_queries, cross_keys, cross_values))
    after_cross = after_self + low_back(product(cross_out, cross_output_matrix))
    third = low(norm_rows(after_cross, gain_third))
    gate = low_back(product(third, gate_matrix))
    up_part = low_back(product(third, up_matrix))
    hidden = low(gelu_tanh(gate) * up_part)
    return after_cross + low_back(product(hidden, down_matrix))

def reference(states, positions, segments, encoded, cotangent, self_gain, self_query, self_key, self_value, self_output, bias_table, cross_gain, cross_query, cross_key, cross_value, cross_output, feed_gain, gate_weight, up_weight, down_weight):
    weights = tuple((weight.astype(jnp.float32) for weight in (self_gain, self_query, self_key, self_value, self_output, bias_table, cross_gain, cross_query, cross_key, cross_value, cross_output, feed_gain, gate_weight, up_weight, down_weight)))
    inputs = states.astype(jnp.float32)
    sources = encoded.astype(jnp.float32)

    def whole_layer(inputs, sources, weights):

        def one_group(group_in, group_src, places, labels):
            return layer_forward(group_in, group_src, places, labels, weights)
        checked = jax.checkpoint(one_group)

        def scan_step(carried, member):
            return (carried, checked(member[0], member[1], member[2], member[3]))
        unused, outputs = lax.scan(scan_step, jnp.zeros((), jnp.float32), (inputs, sources, positions, segments))
        return outputs
    result, pullback = jax.vjp(whole_layer, inputs, sources, weights)
    grad_states, grad_sources, grad_weights = pullback(cotangent.astype(jnp.float32))
    return (result.astype(jnp.bfloat16), grad_states, grad_sources, grad_weights[0], grad_weights[1], grad_weights[2], grad_weights[3], grad_weights[4], grad_weights[5], grad_weights[6], grad_weights[7], grad_weights[8], grad_weights[9], grad_weights[10], grad_weights[11], grad_weights[12], grad_weights[13], grad_weights[14])
```

```python
import functools
import math

import jax
import jax.numpy as jnp
from jax import lax
from jax.experimental import pallas as pl
from jax.experimental.pallas import tpu as pltpu
from jax.sharding import Mesh
from jax.sharding import PartitionSpec as P

BUCKETS = 32
DISTANCE = 128
PROMPT = 2048
CLEN = 256
BLK = 128
TILE = 256
NEG = -1e30
F32 = jnp.float32
BF = jnp.bfloat16
epsilon = 1e-06
gelu_scale = math.sqrt(2.0 / math.pi)
VMEM_LIMIT = 56 * 1024 * 1024


def bucket_starts():
    half=BUCKETS//2
    edges=[math.ceil(half*(DISTANCE/half)**(e/half)) for e in range(1,half)]
    return list(range(half+1))+edges

def nt(a,b):
    return lax.dot_general(a,b,(((1,),(1,)),((),())),preferred_element_type=F32)
def nn(a,b):
    return lax.dot_general(a,b,(((1,),(0,)),((),())),preferred_element_type=F32)

def head_mask(value,head,heads):
    if heads==1: return value
    size=value.shape[-1]//heads
    lane=lax.broadcasted_iota(jnp.int32,value.shape,1)
    return jnp.where((lane>=head*size)&(lane<(head+1)*size),value,jnp.zeros_like(value))

def build_bias(tab_ref,bias_ref,heads):
    starts=bucket_starts()
    key=lax.broadcasted_iota(jnp.int32,(BLK,BLK),0)
    query=lax.broadcasted_iota(jnp.int32,(BLK,BLK),1)
    for h in range(heads):
        last=tab_ref[(BUCKETS-1)*heads+h]
        for sub in (0,1):
            dist=query-key+BLK*sub
            val=jnp.full((BLK,BLK),tab_ref[h]-last,F32)
            for b in range(1,BUCKETS):
                val=jnp.where(dist>=starts[b],tab_ref[b*heads+h]-last,val)
            if sub==0:
                val=jnp.where(dist>=0,val,NEG)
                bias_ref[h,0:BLK,0:BLK]=val
                bias_ref[h,BLK:,BLK:]=val
            else:
                bias_ref[h,0:BLK,BLK:]=val
        bias_ref[h,BLK:,0:BLK]=jnp.full((BLK,BLK),NEG,F32)

def load_tile(src,slots,tile,lo,hi):
    a=src[slots[2*tile],:,lo:hi]
    b=src[slots[2*tile+1],:,lo:hi]
    return jnp.concatenate([a,b],axis=0)

def fwd_kernel(heads,prompt_tiles,slots,tab,qkv,o_ref,ot_ref,lse_ref,bias,kc,vt,qm,s_scr):
    tiles=kc.shape[0]//TILE
    width=kc.shape[1]
    size=width//heads
    build_bias(tab,bias,heads)
    def arrange(t,_):
        rows=pl.ds(pl.multiple_of(t*TILE,TILE),TILE)
        kc[rows,:]=load_tile(qkv,slots,t,width,2*width)
        vt[t]=jnp.transpose(load_tile(qkv,slots,t,2*width,3*width),(1,0))
        return 0
    lax.fori_loop(0,tiles,arrange,0)

    def scores(t_rows,h,kind,qh):
        s=nt(kc[t_rows,:],qh)
        if kind=="own":
            s=s+bias[h]
        elif kind=="prev":
            top=s[:BLK]
            low=jnp.concatenate([s[BLK:,:BLK]+bias[h,0:BLK,BLK:],s[BLK:,BLK:]],axis=1)
            s=jnp.concatenate([top,low],axis=0)
        return s

    def tile_body(t,n_far,own_static):
        q=load_tile(qkv,slots,t,0,width)
        outs=[]
        for h in range(heads):
            qh=head_mask(q,h,heads)
            m=None
            for j in range(n_far+1):
                if j<n_far:
                    rows=pl.ds(j*TILE,TILE); kind="prev" if j==n_far-1 else "far"
                else:
                    rows=pl.ds(pl.multiple_of(t*TILE,TILE),TILE) if not own_static else pl.ds(t*TILE,TILE); kind="own"
                s=scores(rows,h,kind,qh)
                s_scr[h,j]=s
                part=jnp.max(s.reshape(TILE//8,8,TILE),axis=0)
                m=part if m is None else jnp.maximum(m,part)
            m=jnp.max(m,axis=0,keepdims=True)
            l=None; acc=None
            for j in range(n_far+1):
                p=jnp.exp(s_scr[h,j]-m)
                part=jnp.sum(p.reshape(TILE//8,8,TILE),axis=0)
                l=part if l is None else l+part
                vrow=j if j<n_far else t
                a=nn(vt[vrow,h*size:(h+1)*size,:],p.astype(BF))
                acc=a if acc is None else acc+a
            l=jnp.sum(l,axis=0,keepdims=True)
            o=acc*(1.0/l)
            cols=pl.ds(t*TILE if own_static else pl.multiple_of(t*TILE,TILE),TILE)
            ot_ref[h*size:(h+1)*size,cols]=o
            lse_ref[h:h+1,cols]=m+jnp.log(l)
            outs.append(o)
        o=jnp.concatenate(outs,axis=0) if heads>1 else outs[0]
        o=jnp.transpose(o,(1,0)).astype(BF)
        o_ref[slots[2*t]]=o[:BLK]
        o_ref[slots[2*t+1]]=o[BLK:]
    for t in range(prompt_tiles):
        tile_body(t,t,True)
    def cont(c,_):
        tile_body(c,prompt_tiles,False)
        return 0
    lax.fori_loop(prompt_tiles,tiles,cont,0)

def sa_fwd(slots,tab,qkv,heads,prompt_tiles):
    nb,_,w3=qkv.shape; w=w3//3; n=nb*BLK; tiles=n//TILE
    return pl.pallas_call(
        functools.partial(fwd_kernel,heads,prompt_tiles),
        out_shape=(jax.ShapeDtypeStruct((nb,BLK,w),BF),jax.ShapeDtypeStruct((w,n),F32),jax.ShapeDtypeStruct((heads,n),F32)),
        in_specs=[pl.BlockSpec(memory_space=pltpu.SMEM),pl.BlockSpec(memory_space=pltpu.SMEM),pl.BlockSpec(memory_space=pltpu.VMEM)],
        out_specs=[pl.BlockSpec(memory_space=pltpu.VMEM)]*3,
        scratch_shapes=[pltpu.VMEM((heads,TILE,TILE),F32),pltpu.VMEM((n,w),BF),pltpu.VMEM((tiles,w,TILE),BF),pltpu.VMEM((8,128),F32),pltpu.VMEM((heads,prompt_tiles+1,TILE,TILE),F32)],
        compiler_params=pltpu.CompilerParams(vmem_limit_bytes=VMEM_LIMIT),
        name="self_attention_forward",
    )(slots,tab,qkv)

def bwd_kernel(heads,prompt_tiles,unroll,slots,tab,qkv,do_ref,ot_ref,lse_ref,dqkv_ref,dtab_ref,bias,kc,vc,kt,dkv,dqt,near,far):
    tiles=kc.shape[0]//TILE
    width=kc.shape[1]
    size=width//heads
    build_bias(tab,bias,heads)
    near[...]=jnp.zeros_like(near)
    far[...]=jnp.zeros_like(far)
    dkv[...]=jnp.zeros_like(dkv)
    def arrange(t,_):
        rows=pl.ds(pl.multiple_of(t*TILE,TILE),TILE)
        k=load_tile(qkv,slots,t,width,2*width)
        kc[rows,:]=k
        kt[t]=jnp.transpose(k,(1,0))
        vc[rows,:]=load_tile(qkv,slots,t,2*width,3*width)
        return 0
    lax.fori_loop(0,tiles,arrange,0)

    def query_tile(t,_):
        cols=pl.ds(pl.multiple_of(t*TILE,TILE),TILE)
        q=load_tile(qkv,slots,t,0,width)
        do=load_tile(do_ref,slots,t,0,width)
        dot=jnp.transpose(do.astype(F32),(1,0))*ot_ref[:,cols]
        qh=[head_mask(q,h,heads) for h in range(heads)]
        doh=[head_mask(do,h,heads) for h in range(heads)]
        lse=[lse_ref[h:h+1,cols] for h in range(heads)]
        delta=[jnp.sum(dot[h*size:(h+1)*size],axis=0,keepdims=True) for h in range(heads)]
        dqt[...]=jnp.zeros_like(dqt)

        def piece(j,kind):
            rows=pl.ds(pl.multiple_of(j*TILE,TILE),TILE)
            k=kc[rows,:]; v=vc[rows,:]
            dv=None; dk=None
            for h in range(heads):
                s=nt(k,qh[h])
                if kind=="own":
                    s=s+bias[h]
                elif kind=="prev":
                    low=jnp.concatenate([s[BLK:,:BLK]+bias[h,0:BLK,BLK:],s[BLK:,BLK:]],axis=1)
                    s=jnp.concatenate([s[:BLK],low],axis=0)
                p=jnp.exp(s-lse[h])
                dp=nt(v,doh[h])
                ds=p*(dp-delta[h])
                if kind=="own":
                    near[h,0]+=ds[:BLK,:BLK]+ds[BLK:,BLK:]
                    near[h,1]+=ds[:BLK,BLK:]
                elif kind=="prev":
                    near[h,1]+=ds[BLK:,:BLK]
                    f=jnp.sum(ds[:BLK].reshape(BLK//8,8,TILE),axis=0)
                    f2=jnp.sum(ds[BLK:,BLK:].reshape(BLK//8,8,BLK),axis=0)
                    far[h]+=f
                    far[h,:,BLK:]+=f2
                else:
                    far[h]+=jnp.sum(ds.reshape(TILE//8,8,TILE),axis=0)
                pb=p.astype(BF); db=ds.astype(BF)
                a=nn(pb,doh[h]); dv=a if dv is None else dv+a
                b=nn(db,qh[h]); dk=b if dk is None else dk+b
                dqt[h*size:(h+1)*size,:]+=nn(kt[j,h*size:(h+1)*size,:],db)
            dkv[rows,0:width]+=dk
            dkv[rows,width:2*width]+=dv
        n_far=jnp.minimum(t,prompt_tiles)-1
        def far_step(j,_):
            piece(j,"far"); return 0
        def far_many(j,_):
            for u in range(unroll): piece(j*unroll+u,"far")
            return 0
        if unroll>1:
            lax.fori_loop(0,n_far//unroll,far_many,0)
            lax.fori_loop((n_far//unroll)*unroll,n_far,far_step,0)
        else:
            lax.fori_loop(0,n_far,far_step,0)
        @pl.when(t>0)
        def _():
            piece(n_far,"prev")
        piece(t,"own")
        dq=jnp.transpose(dqt[...],(1,0)).astype(BF)
        dqkv_ref[slots[2*t],:,0:width]=dq[:BLK]
        dqkv_ref[slots[2*t+1],:,0:width]=dq[BLK:]
        return 0
    lax.fori_loop(0,tiles,query_tile,0)
    def finish(t,_):
        g=dkv[pl.ds(pl.multiple_of(t*TILE,TILE),TILE),:].astype(BF)
        dqkv_ref[slots[2*t],:,width:3*width]=g[:BLK]
        dqkv_ref[slots[2*t+1],:,width:3*width]=g[BLK:]
        return 0
    lax.fori_loop(0,tiles,finish,0)
    starts=bucket_starts()
    key=lax.broadcasted_iota(jnp.int32,(BLK,BLK),0)
    query=lax.broadcasted_iota(jnp.int32,(BLK,BLK),1)
    for h in range(heads):
        for b in range(BUCKETS):
            total=jnp.zeros((8,BLK),F32)
            for sub in (0,1):
                dist=query-key+BLK*sub
                inside=dist>=starts[b]
                if b<BUCKETS-1: inside=inside&(dist<starts[b+1])
                total=total+jnp.sum(jnp.where(inside,near[h,sub],0.0).reshape(BLK//8,8,BLK),axis=0)
            if b==BUCKETS-1:
                total=total+far[h,:,0:BLK]+far[h,:,BLK:]
            row=jnp.sum(total,axis=0,keepdims=True)
            dtab_ref[h,b:b+1,:]=jnp.broadcast_to(jnp.sum(row,axis=1,keepdims=True),(1,BLK))

def sa_bwd(slots,tab,qkv,do,ot,lse,heads,prompt_tiles,unroll=1):
    nb,_,w3=qkv.shape; w=w3//3; n=nb*BLK; tiles=n//TILE
    return pl.pallas_call(
        functools.partial(bwd_kernel,heads,prompt_tiles,unroll),
        out_shape=(jax.ShapeDtypeStruct((nb,BLK,w3),BF),jax.ShapeDtypeStruct((heads,BUCKETS,BLK),F32)),
        in_specs=[pl.BlockSpec(memory_space=pltpu.SMEM)]*2+[pl.BlockSpec(memory_space=pltpu.VMEM)]*4,
        out_specs=[pl.BlockSpec(memory_space=pltpu.VMEM)]*2,
        scratch_shapes=[pltpu.VMEM((heads,TILE,TILE),F32),pltpu.VMEM((n,w),BF),pltpu.VMEM((n,w),BF),pltpu.VMEM((tiles,w,TILE),BF),pltpu.VMEM((n,2*w),F32),pltpu.VMEM((w,TILE),F32),pltpu.VMEM((heads,2,BLK,BLK),F32),pltpu.VMEM((heads,8,TILE),F32)],
        compiler_params=pltpu.CompilerParams(vmem_limit_bytes=VMEM_LIMIT),
        name="self_attention_backward",
    )(slots,tab,qkv,do,ot,lse)


def first_kernel(states_ref, gain_ref, w_ref, out_ref):
    x = states_ref[...].astype(F32)
    r = lax.rsqrt(jnp.mean(x * x, axis=-1, keepdims=True) + epsilon)
    n = (x * r * gain_ref[...]).astype(BF)
    out_ref[...] = nn(n, w_ref[...]).astype(BF)


def first_projection(states_all, gain, weight, rows=512):
    tokens, width = states_all.shape
    cols = weight.shape[1]
    return pl.pallas_call(
        first_kernel,
        grid=(tokens // rows,),
        out_shape=jax.ShapeDtypeStruct((tokens, cols), BF),
        in_specs=[
            pl.BlockSpec((rows, width), lambda i: (i, 0)),
            pl.BlockSpec((1, width), lambda i: (0, 0)),
            pl.BlockSpec((width, cols), lambda i: (0, 0)),
        ],
        out_specs=pl.BlockSpec((rows, cols), lambda i: (i, 0)),
        compiler_params=pltpu.CompilerParams(vmem_limit_bytes=VMEM_LIMIT),
        cost_estimate=pl.CostEstimate(
            flops=2 * tokens * width * cols, bytes_accessed=2 * tokens * (width + cols), transcendentals=0
        ),
        name="first_projection",
    )(states_all, gain, weight)


def last_kernel(states_ref, gain_ref, w_ref, d_ref, dn_ref, gw_ref, acc_ref):
    step = pl.program_id(0)
    x = states_ref[...].astype(F32)
    r = lax.rsqrt(jnp.mean(x * x, axis=-1, keepdims=True) + epsilon)
    n = (x * r * gain_ref[...]).astype(BF)
    d = d_ref[...]
    dn_ref[...] = nt(d, w_ref[...]).astype(BF)
    g = lax.dot_general(n, d, (((0,), (0,)), ((), ())), preferred_element_type=F32)

    @pl.when(step == 0)
    def _():
        acc_ref[...] = g

    @pl.when(step > 0)
    def _():
        acc_ref[...] += g

    @pl.when(step == pl.num_programs(0) - 1)
    def _():
        gw_ref[...] = acc_ref[...].astype(BF)


def last_projection(states_all, gain, weight, grads, rows=512):
    tokens, width = states_all.shape
    cols = weight.shape[1]
    return pl.pallas_call(
        last_kernel,
        grid=(tokens // rows,),
        out_shape=(jax.ShapeDtypeStruct((tokens, width), BF), jax.ShapeDtypeStruct((width, cols), BF)),
        in_specs=[
            pl.BlockSpec((rows, width), lambda i: (i, 0)),
            pl.BlockSpec((1, width), lambda i: (0, 0)),
            pl.BlockSpec((width, cols), lambda i: (0, 0)),
            pl.BlockSpec((rows, cols), lambda i: (i, 0)),
        ],
        out_specs=[
            pl.BlockSpec((rows, width), lambda i: (i, 0)),
            pl.BlockSpec((width, cols), lambda i: (0, 0)),
        ],
        scratch_shapes=[pltpu.VMEM((width, cols), F32)],
        compiler_params=pltpu.CompilerParams(vmem_limit_bytes=VMEM_LIMIT),
        cost_estimate=pl.CostEstimate(
            flops=4 * tokens * width * cols, bytes_accessed=2 * tokens * (2 * width + cols), transcendentals=0
        ),
        name="last_projection",
    )(states_all, gain, weight, grads)


def norm_rows(value, gain):
    return value * lax.rsqrt(jnp.mean(value * value, axis=-1, keepdims=True) + epsilon) * gain


def geglu(gate, up_part):
    return 0.5 * gate * (1.0 + jnp.tanh(gelu_scale * (gate + 0.044715 * gate * gate * gate))) * up_part


def project(left, right):
    return jnp.einsum("td,de->te", left, right, preferred_element_type=F32)


def project_back(left, right):
    return jnp.einsum("te,de->td", left, right, preferred_element_type=F32)


def weight_grad(left, right):
    return jnp.einsum("td,te->de", left, right, preferred_element_type=F32).astype(BF)


CTX = ("plane", "core")


def gather_all(shard):
    parts = lax.axis_size(CTX)
    own = shard.shape[0] // parts
    piece = lax.dynamic_slice_in_dim(shard, lax.axis_index(CTX) * own, own, 0)
    return lax.all_gather(piece, ("fsdp",) + CTX, axis=0, tiled=True)


def reduce_all(grad):
    parts, shards = lax.axis_size(CTX), lax.axis_size("fsdp")
    own = grad.shape[0] // (parts * shards)
    g = grad.reshape(shards, parts, own, grad.shape[1]).transpose(1, 0, 2, 3)
    g = lax.psum_scatter(g, CTX, scatter_dimension=0, tiled=True)
    g = lax.psum_scatter(g.reshape(shards, own, grad.shape[1]), "fsdp", scatter_dimension=0, tiled=True)
    return lax.all_gather(g[0], CTX, axis=0, tiled=True).astype(F32)


def on_device(
    states, positions, segments, encoded, cotangent,
    self_gain, self_query, self_key, self_value, self_output, bias_table,
    cross_gain, cross_query, cross_key, cross_value, cross_output,
    feed_gain, gate_weight, up_weight, down_weight,
):
    parts, shards = lax.axis_size(CTX), lax.axis_size("fsdp")
    place = lax.axis_index(CTX)
    local, width = states.shape[1:]
    head_count = bias_table.shape[1]
    size = width // head_count
    heads = head_count // parts
    inner = heads * size
    blocks = local // BLK
    table_rows = bias_table.shape[0]
    shard_width = self_gain.shape[0]

    states_all = lax.all_gather(states[0], CTX, axis=0, tiled=True)
    columns = lax.dynamic_slice_in_dim(
        jnp.stack([self_query, self_key, self_value], axis=1), place * inner, inner, 2
    ).reshape(self_query.shape[0], 3 * inner)
    qkv_weight = lax.all_gather(columns, "fsdp", axis=0, tiled=True)
    small = jnp.concatenate([self_gain, cross_gain, feed_gain, bias_table.reshape(-1)])
    small = lax.all_gather(small, "fsdp", axis=0, tiled=False).astype(F32)
    gains = [small[:, i * shard_width : (i + 1) * shard_width].reshape(1, width) for i in range(3)]
    table = small[:, 3 * shard_width :].reshape(BUCKETS, head_count)
    own_table = lax.dynamic_slice_in_dim(table, place * heads, heads, 1).reshape(-1)
    first_pos, first_seg = positions[0, ::BLK], segments[0, ::BLK]
    canon = jnp.where(
        first_seg == 0,
        first_pos // BLK,
        PROMPT // BLK + (first_seg - 1) * (CLEN // BLK) + (first_pos - PROMPT) // BLK,
    )
    canon_all = lax.all_gather(canon, CTX, axis=0, tiled=True)
    slots = jnp.argmax(canon_all[None, :] == jnp.arange(blocks * parts)[:, None], axis=1).astype(jnp.int32)
    encoded_all = lax.all_gather(encoded[0], CTX, axis=0, tiled=True)
    out_full = gather_all(self_output)
    cq_full, ck_full, cv_full, co_full = [gather_all(w) for w in (cross_query, cross_key, cross_value, cross_output)]
    gate_full, up_full, down_full = gather_all(gate_weight), gather_all(up_weight), gather_all(down_weight)

    prompt_tiles = PROMPT // TILE
    qkv = first_projection(states_all, gains[0], qkv_weight).reshape(parts * blocks, BLK, 3 * inner)
    o, ot, lse = sa_fwd(slots, own_table, qkv, heads, prompt_tiles)
    o = lax.all_to_all(o.reshape(parts, local, inner), CTX, 0, 0, tiled=True)
    attended_low = o.transpose(1, 0, 2).reshape(local, width)

    inputs = states[0].astype(F32)
    cot = cotangent[0]
    after_self = inputs + project(attended_low, out_full)
    second_norm, second_back = jax.vjp(norm_rows, after_self, gains[1][0])
    second_low = second_norm.astype(BF)
    heads_of = lambda v: v.reshape(v.shape[0], head_count, size)
    cross_queries = project(second_low, cq_full).astype(BF)
    cross_keys = project(encoded_all, ck_full).astype(BF)
    cross_values = project(encoded_all, cv_full).astype(BF)
    scores = jnp.einsum("qhd,khd->hqk", heads_of(cross_queries), heads_of(cross_keys), preferred_element_type=F32)
    expo = jnp.exp(scores - jnp.max(scores, axis=-1, keepdims=True))
    probs = expo / jnp.sum(expo, axis=-1, keepdims=True)
    probs_low = probs.astype(BF)
    cross_attended = jnp.einsum("hqk,khd->qhd", probs_low, heads_of(cross_values), preferred_element_type=F32)
    cross_low = cross_attended.reshape(local, width).astype(BF)
    after_cross = after_self + project(cross_low, co_full)
    third_norm, third_back = jax.vjp(norm_rows, after_cross, gains[2][0])
    third_low = third_norm.astype(BF)
    gate = project(third_low, gate_full)
    up_part = project(third_low, up_full)
    hidden, hidden_back = jax.vjp(geglu, gate, up_part)
    hidden_low = hidden.astype(BF)
    layer_out = (after_cross + project(hidden_low, down_full)).astype(BF)
    grad_gate, grad_up = hidden_back(project_back(cot, down_full))
    gate_low, up_low = grad_gate.astype(BF), grad_up.astype(BF)
    g_down = reduce_all(weight_grad(hidden_low, cot))
    g_gate = reduce_all(weight_grad(third_low, gate_low))
    g_up = reduce_all(weight_grad(third_low, up_low))
    third_in, feed_gain_part = third_back(project_back(gate_low, gate_full) + project_back(up_low, up_full))
    carry_two = cot.astype(F32) + third_in
    branch_two = carry_two.astype(BF)
    g_cross_output = reduce_all(weight_grad(cross_low, branch_two))
    cross_dout = heads_of(project_back(branch_two, co_full).astype(BF))
    cross_delta = jnp.sum(cross_dout.astype(F32) * cross_attended, axis=-1).T
    dprob = jnp.einsum("qhd,khd->hqk", cross_dout, heads_of(cross_values), preferred_element_type=F32)
    dscore = (probs * (dprob - cross_delta[..., None])).astype(BF)
    dcq = jnp.einsum("hqk,khd->qhd", dscore, heads_of(cross_keys), preferred_element_type=F32)
    dcq = dcq.reshape(local, width).astype(BF)
    dck = jnp.einsum("hqk,qhd->khd", dscore, heads_of(cross_queries), preferred_element_type=F32)
    dcv = jnp.einsum("hqk,qhd->khd", probs_low, cross_dout, preferred_element_type=F32)
    dck = dck.reshape(-1, width).astype(BF)
    dcv = dcv.reshape(-1, width).astype(BF)
    g_cross_key = reduce_all(weight_grad(encoded_all, dck))
    g_cross_value = reduce_all(weight_grad(encoded_all, dcv))
    encoded_part = (project_back(dck, ck_full) + project_back(dcv, cv_full)).astype(BF)
    encoded_grad = lax.psum_scatter(encoded_part, CTX, scatter_dimension=0, tiled=True).astype(F32)
    g_cross_query = reduce_all(weight_grad(second_low, dcq))
    second_in, cross_gain_part = second_back(project_back(dcq, cq_full))
    carry_one = carry_two + second_in
    branch_one = carry_one.astype(BF)
    g_self_output = reduce_all(weight_grad(attended_low, branch_one))
    dso = project_back(branch_one, out_full).astype(BF)

    dso = dso.reshape(local, parts, inner).transpose(1, 0, 2)
    dso = lax.all_to_all(dso, CTX, 0, 0, tiled=True).reshape(parts * blocks, BLK, inner)
    dqkv, dtable = sa_bwd(slots, own_table, qkv, dso, ot, lse, heads, prompt_tiles)
    dn1, g_qkv = last_projection(states_all, gains[0], qkv_weight, dqkv.reshape(parts * local, 3 * inner))
    dn1 = lax.psum_scatter(dn1, CTX, scatter_dimension=0, tiled=True).astype(F32)
    first_back = jax.vjp(norm_rows, inputs, gains[0][0])[1]
    first_in, self_gain_part = first_back(dn1)
    states_grad = carry_one + first_in
    g_qkv = lax.psum_scatter(g_qkv, "fsdp", scatter_dimension=0, tiled=True)
    g_qkv = lax.all_gather(g_qkv, CTX, axis=0, tiled=False).astype(F32)
    g_qkv = g_qkv.reshape(parts, -1, 3, inner).transpose(2, 1, 0, 3).reshape(3, -1, width)

    table_part = jnp.zeros((BUCKETS, head_count), F32)
    table_part = lax.dynamic_update_slice_in_dim(table_part, dtable[:, :, 0].T, place * heads, 1)
    sums = jnp.concatenate([self_gain_part, cross_gain_part, feed_gain_part, table_part.reshape(-1)])
    sums = lax.psum(sums, CTX + ("fsdp",))
    mine = lax.axis_index("fsdp")
    gain_grads = [lax.dynamic_slice_in_dim(sums, i * width + mine * shard_width, shard_width) for i in range(3)]
    table_grad = lax.dynamic_slice_in_dim(sums[3 * width :].reshape(BUCKETS, head_count), mine * table_rows, table_rows, 0)
    return (
        layer_out[None], states_grad[None], encoded_grad[None],
        gain_grads[0], g_qkv[0], g_qkv[1], g_qkv[2], g_self_output, table_grad,
        gain_grads[1], g_cross_query, g_cross_key, g_cross_value, g_cross_output,
        gain_grads[2], g_gate, g_up, g_down,
    )


def solution(mesh):
    ctx, fsdp = mesh.devices.shape
    split = Mesh(mesh.devices.reshape(ctx // 2, 2, fsdp), ("plane", "core", "fsdp"))
    tokens, matrix, vector = P("fsdp", CTX, None), P("fsdp", None), P("fsdp")
    place = P("fsdp", CTX)
    return jax.shard_map(
        on_device,
        mesh=split,
        in_specs=(tokens, place, place, tokens, tokens)
        + (vector, matrix, matrix, matrix, matrix, matrix)
        + (vector, matrix, matrix, matrix, matrix)
        + (vector, matrix, matrix, matrix),
        out_specs=(tokens, tokens, tokens)
        + (vector, matrix, matrix, matrix, matrix, matrix)
        + (vector, matrix, matrix, matrix, matrix)
        + (vector, matrix, matrix, matrix),
        check_vma=False,
    )
```

```python
import functools
import math

import jax
import jax.numpy as jnp
from jax import lax
from jax.experimental import pallas as pl
from jax.experimental.pallas import tpu as pltpu
from jax.sharding import Mesh
from jax.sharding import PartitionSpec as P

BUCKETS = 32
DISTANCE = 128
PROMPT = 2048
CLEN = 256
BLK = 128
TILE = 256
NEG = -1e30
F32 = jnp.float32
BF = jnp.bfloat16
epsilon = 1e-06
gelu_scale = math.sqrt(2.0 / math.pi)
VMEM_LIMIT = 56 * 1024 * 1024


def bucket_starts():
    half=BUCKETS//2
    edges=[math.ceil(half*(DISTANCE/half)**(e/half)) for e in range(1,half)]
    return list(range(half+1))+edges

def nt(a,b):
    return lax.dot_general(a,b,(((1,),(1,)),((),())),preferred_element_type=F32)
def nn(a,b):
    return lax.dot_general(a,b,(((1,),(0,)),((),())),preferred_element_type=F32)

def head_mask(value,head,heads):
    if heads==1: return value
    size=value.shape[-1]//heads
    lane=lax.broadcasted_iota(jnp.int32,value.shape,1)
    return jnp.where((lane>=head*size)&(lane<(head+1)*size),value,jnp.zeros_like(value))

def build_bias(tab_ref,bias_ref,heads):
    starts=bucket_starts()
    key=lax.broadcasted_iota(jnp.int32,(BLK,BLK),0)
    query=lax.broadcasted_iota(jnp.int32,(BLK,BLK),1)
    for h in range(heads):
        last=tab_ref[(BUCKETS-1)*heads+h]
        for sub in (0,1):
            dist=query-key+BLK*sub
            val=jnp.full((BLK,BLK),tab_ref[h]-last,F32)
            for b in range(1,BUCKETS):
                val=jnp.where(dist>=starts[b],tab_ref[b*heads+h]-last,val)
            if sub==0:
                val=jnp.where(dist>=0,val,NEG)
                bias_ref[h,0:BLK,0:BLK]=val
                bias_ref[h,BLK:,BLK:]=val
            else:
                bias_ref[h,0:BLK,BLK:]=val
        bias_ref[h,BLK:,0:BLK]=jnp.full((BLK,BLK),NEG,F32)

def load_tile(src,slots,tile,lo,hi):
    a=src[slots[2*tile],:,lo:hi]
    b=src[slots[2*tile+1],:,lo:hi]
    return jnp.concatenate([a,b],axis=0)

def fwd_kernel(heads,prompt_tiles,slots,tab,qkv,o_ref,ot_ref,lse_ref,bias,kc,vt,qm,s_scr):
    tiles=kc.shape[0]//TILE
    width=kc.shape[1]
    size=width//heads
    build_bias(tab,bias,heads)
    def arrange(t,_):
        rows=pl.ds(pl.multiple_of(t*TILE,TILE),TILE)
        kc[rows,:]=load_tile(qkv,slots,t,width,2*width)
        vt[t]=jnp.transpose(load_tile(qkv,slots,t,2*width,3*width),(1,0))
        return 0
    lax.fori_loop(0,tiles,arrange,0)

    def scores(t_rows,h,kind,qh):
        s=nt(kc[t_rows,:],qh)
        if kind=="own":
            s=s+bias[h]
        elif kind=="prev":
            top=s[:BLK]
            low=jnp.concatenate([s[BLK:,:BLK]+bias[h,0:BLK,BLK:],s[BLK:,BLK:]],axis=1)
            s=jnp.concatenate([top,low],axis=0)
        return s

    def tile_body(t,n_far,own_static):
        q=load_tile(qkv,slots,t,0,width)
        outs=[]
        for h in range(heads):
            qh=head_mask(q,h,heads)
            m=None
            for j in range(n_far+1):
                if j<n_far:
                    rows=pl.ds(j*TILE,TILE); kind="prev" if j==n_far-1 else "far"
                else:
                    rows=pl.ds(pl.multiple_of(t*TILE,TILE),TILE) if not own_static else pl.ds(t*TILE,TILE); kind="own"
                s=scores(rows,h,kind,qh)
                s_scr[h,j]=s
                part=jnp.max(s.reshape(TILE//8,8,TILE),axis=0)
                m=part if m is None else jnp.maximum(m,part)
            m=jnp.max(m,axis=0,keepdims=True)
            l=None; acc=None
            for j in range(n_far+1):
                p=jnp.exp(s_scr[h,j]-m)
                part=jnp.sum(p.reshape(TILE//8,8,TILE),axis=0)
                l=part if l is None else l+part
                vrow=j if j<n_far else t
                a=nn(vt[vrow,h*size:(h+1)*size,:],p.astype(BF))
                acc=a if acc is None else acc+a
            l=jnp.sum(l,axis=0,keepdims=True)
            o=acc*(1.0/l)
            cols=pl.ds(t*TILE if own_static else pl.multiple_of(t*TILE,TILE),TILE)
            ot_ref[h*size:(h+1)*size,cols]=o
            lse_ref[h:h+1,cols]=m+jnp.log(l)
            outs.append(o)
        o=jnp.concatenate(outs,axis=0) if heads>1 else outs[0]
        o=jnp.transpose(o,(1,0)).astype(BF)
        o_ref[slots[2*t]]=o[:BLK]
        o_ref[slots[2*t+1]]=o[BLK:]
    for t in range(prompt_tiles):
        tile_body(t,t,True)
    def cont(c,_):
        tile_body(c,prompt_tiles,False)
        return 0
    lax.fori_loop(prompt_tiles,tiles,cont,0)

def sa_fwd(slots,tab,qkv,heads,prompt_tiles):
    nb,_,w3=qkv.shape; w=w3//3; n=nb*BLK; tiles=n//TILE
    return pl.pallas_call(
        functools.partial(fwd_kernel,heads,prompt_tiles),
        out_shape=(jax.ShapeDtypeStruct((nb,BLK,w),BF),jax.ShapeDtypeStruct((w,n),F32),jax.ShapeDtypeStruct((heads,n),F32)),
        in_specs=[pl.BlockSpec(memory_space=pltpu.SMEM),pl.BlockSpec(memory_space=pltpu.SMEM),pl.BlockSpec(memory_space=pltpu.VMEM)],
        out_specs=[pl.BlockSpec(memory_space=pltpu.VMEM)]*3,
        scratch_shapes=[pltpu.VMEM((heads,TILE,TILE),F32),pltpu.VMEM((n,w),BF),pltpu.VMEM((tiles,w,TILE),BF),pltpu.VMEM((8,128),F32),pltpu.VMEM((heads,prompt_tiles+1,TILE,TILE),F32)],
        compiler_params=pltpu.CompilerParams(vmem_limit_bytes=VMEM_LIMIT),
        cost_estimate=pl.CostEstimate(flops=32 * 10**9, bytes_accessed=8 * n * w3, transcendentals=0),
        name="self_attention_forward",
    )(slots,tab,qkv)

def bwd_kernel(heads,prompt_tiles,unroll,low,high,slots,tab,qkv,do_ref,ot_ref,lse_ref,*refs):
    if low:
        dq_in,dkv_in,near_in,far_in,dqkv_ref,dtab_ref,bias,kc,vc,kt,dqt,dkv,near,far=refs
    else:
        dq_out,dkv,near,far,bias,kc,vc,kt,dqt=refs
    tiles=kc.shape[0]//TILE
    width=kc.shape[1]
    size=width//heads
    build_bias(tab,bias,heads)
    for mine,start in ((near,near_in if low else None),(far,far_in if low else None),(dkv,dkv_in if low else None)):
        mine[...]=start[...] if low else jnp.zeros_like(mine)
    def arrange(t,_):
        rows=pl.ds(pl.multiple_of(t*TILE,TILE),TILE)
        k=load_tile(qkv,slots,t,width,2*width)
        kc[rows,:]=k
        kt[t]=jnp.transpose(k,(1,0))
        vc[rows,:]=load_tile(qkv,slots,t,2*width,3*width)
        return 0
    lax.fori_loop(0,tiles,arrange,0)

    def query_tile(t,_):
        cols=pl.ds(pl.multiple_of(t*TILE,TILE),TILE)
        q=load_tile(qkv,slots,t,0,width)
        do=load_tile(do_ref,slots,t,0,width)
        dot=jnp.transpose(do.astype(F32),(1,0))*ot_ref[:,cols]
        qh=[head_mask(q,h,heads) for h in range(heads)]
        doh=[head_mask(do,h,heads) for h in range(heads)]
        lse=[lse_ref[h:h+1,cols] for h in range(heads)]
        delta=[jnp.sum(dot[h*size:(h+1)*size],axis=0,keepdims=True) for h in range(heads)]
        dqt[...]=jnp.zeros_like(dqt)

        def piece(j,kind):
            rows=pl.ds(pl.multiple_of(j*TILE,TILE),TILE)
            k=kc[rows,:]; v=vc[rows,:]
            dv=None; dk=None
            for h in range(heads):
                s=nt(k,qh[h])
                if kind=="own":
                    s=s+bias[h]
                elif kind=="prev":
                    low=jnp.concatenate([s[BLK:,:BLK]+bias[h,0:BLK,BLK:],s[BLK:,BLK:]],axis=1)
                    s=jnp.concatenate([s[:BLK],low],axis=0)
                p=jnp.exp(s-lse[h])
                dp=nt(v,doh[h])
                ds=p*(dp-delta[h])
                if kind=="own":
                    near[h,0]+=ds[:BLK,:BLK]+ds[BLK:,BLK:]
                    near[h,1]+=ds[:BLK,BLK:]
                elif kind=="prev":
                    near[h,1]+=ds[BLK:,:BLK]
                    f=jnp.sum(ds[:BLK].reshape(BLK//8,8,TILE),axis=0)
                    f2=jnp.sum(ds[BLK:,BLK:].reshape(BLK//8,8,BLK),axis=0)
                    far[h]+=f
                    far[h,:,BLK:]+=f2
                else:
                    far[h]+=jnp.sum(ds.reshape(TILE//8,8,TILE),axis=0)
                pb=p.astype(BF); db=ds.astype(BF)
                a=nn(pb,doh[h]); dv=a if dv is None else dv+a
                b=nn(db,qh[h]); dk=b if dk is None else dk+b
                dqt[h*size:(h+1)*size,:]+=nn(kt[j,h*size:(h+1)*size,:],db)
            dkv[rows,0:width]+=dk
            dkv[rows,width:2*width]+=dv
        n_far=jnp.maximum(jnp.minimum(t,prompt_tiles)-1,0)
        def far_step(j,_):
            piece(j,"far"); return 0
        def far_many(j,_):
            for u in range(unroll): piece(j*unroll+u,"far")
            return 0
        if unroll>1:
            lax.fori_loop(0,n_far//unroll,far_many,0)
            lax.fori_loop((n_far//unroll)*unroll,n_far,far_step,0)
        else:
            lax.fori_loop(0,n_far,far_step,0)
        @pl.when(t>0)
        def _():
            piece(n_far,"prev")
        piece(t,"own")
        dq=jnp.transpose(dqt[...],(1,0)).astype(BF)
        if low:
            dqkv_ref[slots[2*t],:,0:width]=dq[:BLK]
            dqkv_ref[slots[2*t+1],:,0:width]=dq[BLK:]
        else:
            dq_out[cols,:]=dq
        return 0
    lax.fori_loop(low,high,query_tile,0)
    if not low:
        return
    def bring(t,_):
        dq=dq_in[pl.ds(pl.multiple_of(t*TILE,TILE),TILE),:]
        dqkv_ref[slots[2*t],:,0:width]=dq[:BLK]
        dqkv_ref[slots[2*t+1],:,0:width]=dq[BLK:]
        return 0
    lax.fori_loop(0,low,bring,0)
    def finish(t,_):
        g=dkv[pl.ds(pl.multiple_of(t*TILE,TILE),TILE),:].astype(BF)
        dqkv_ref[slots[2*t],:,width:3*width]=g[:BLK]
        dqkv_ref[slots[2*t+1],:,width:3*width]=g[BLK:]
        return 0
    lax.fori_loop(0,tiles,finish,0)
    starts=bucket_starts()
    key=lax.broadcasted_iota(jnp.int32,(BLK,BLK),0)
    query=lax.broadcasted_iota(jnp.int32,(BLK,BLK),1)
    for h in range(heads):
        for b in range(BUCKETS):
            total=jnp.zeros((8,BLK),F32)
            for sub in (0,1):
                dist=query-key+BLK*sub
                inside=dist>=starts[b]
                if b<BUCKETS-1: inside=inside&(dist<starts[b+1])
                total=total+jnp.sum(jnp.where(inside,near[h,sub],0.0).reshape(BLK//8,8,BLK),axis=0)
            if b==BUCKETS-1:
                total=total+far[h,:,0:BLK]+far[h,:,BLK:]
            row=jnp.sum(total,axis=0,keepdims=True)
            dtab_ref[h,b:b+1,:]=jnp.broadcast_to(jnp.sum(row,axis=1,keepdims=True),(1,BLK))

def sa_bwd(slots,tab,qkv,do,ot,lse,heads,prompt_tiles,low,high,held=(),unroll=2):
    nb,_,w3=qkv.shape; w=w3//3; n=nb*BLK; tiles=n//TILE
    shape=jax.ShapeDtypeStruct
    sums=[shape((n,2*w),F32),shape((heads,2,BLK,BLK),F32),shape((heads,8,TILE),F32)]
    if low:
        out=[shape((nb,BLK,w3),BF),shape((heads,BUCKETS,BLK),F32)]
    else:
        out=[shape((high*TILE,w),BF)]+sums
    scratch=[pltpu.VMEM((heads,TILE,TILE),F32),pltpu.VMEM((n,w),BF),pltpu.VMEM((n,w),BF),pltpu.VMEM((tiles,w,TILE),BF),pltpu.VMEM((w,TILE),F32)]
    if low:
        scratch+=[pltpu.VMEM(v.shape,F32) for v in sums]
    return pl.pallas_call(
        functools.partial(bwd_kernel,heads,prompt_tiles,unroll,low,high),
        out_shape=out,
        in_specs=[pl.BlockSpec(memory_space=pltpu.SMEM)]*2+[pl.BlockSpec(memory_space=pltpu.VMEM)]*(4+len(held)),
        out_specs=[pl.BlockSpec(memory_space=pltpu.VMEM)]*len(out),
        scratch_shapes=scratch,
        compiler_params=pltpu.CompilerParams(vmem_limit_bytes=VMEM_LIMIT),
        cost_estimate=pl.CostEstimate(flops=43 * 10**9, bytes_accessed=12 * n * w3, transcendentals=0),
        name="self_attention_backward",
    )(slots,tab,qkv,do,ot,lse,*held)


def line_tile(step, size=TILE):
    return pl.ds(pl.multiple_of(step * size, size), size)


def whole_weight(ref, scratch):
    parts, shards, _, rows, _ = ref.shape
    for z in range(shards):
        for c in range(parts):
            start = (z * parts + c) * rows
            scratch[start : start + rows, :] = ref[c, z, 0]


def store_rows(ref, layout, which, cols, value):
    parts, shards, matrices, rows = layout
    for z in range(shards):
        for c in range(parts):
            start = (z * parts + c) * rows
            place = (z * matrices + which) * rows
            ref[c, place : place + rows, cols] = value[start : start + rows]


def store_grad(ref, which, cols, value):
    parts, shards, _, rows, _ = ref.shape
    for z in range(shards):
        for c in range(parts):
            start = (z * parts + c) * rows
            ref[c, z, which, :, cols] = value[start : start + rows]


def inverse_rms(v):
    return lax.rsqrt(jnp.mean(v * v, axis=-1, keepdims=True) + epsilon)


def norm_back(v, gain, dn):
    r = inverse_rms(v)
    weighted = dn * gain
    dv = r * weighted - v * (r * r * r) * jnp.mean(weighted * v, axis=-1, keepdims=True)
    return dv, jnp.sum(dn * v * r, axis=0, keepdims=True)


def whole(shape, index=None):
    zeros = (0,) * len(shape)
    return pl.BlockSpec(shape, lambda *_: zeros if index is None else index)


def packed_spec(packed, which):
    parts, shards, _, rows, width = packed.shape
    return pl.BlockSpec((parts, shards, 1, rows, width), lambda *_: (0, 0, which, 0, 0))


def params():
    return pltpu.CompilerParams(vmem_limit_bytes=VMEM_LIMIT)


def cost(flops, size):
    return pl.CostEstimate(flops=flops, bytes_accessed=size, transcendentals=0)


def source_kernel(source_ref, w_ref, out_ref, weight):
    whole_weight(w_ref, weight)
    source = source_ref[...]
    for t in range(out_ref.shape[-1] // TILE):
        cols = slice(t * TILE, (t + 1) * TILE)
        out_ref[0, :, cols] = nn(source, weight[:, cols]).astype(BF)


def source_projection(source, packed):
    rows, width = source.shape
    parts, shards, _, own, _ = packed.shape
    return pl.pallas_call(
        source_kernel,
        grid=(2,),
        out_shape=jax.ShapeDtypeStruct((2, rows, width), BF),
        in_specs=[
            whole((rows, width)),
            pl.BlockSpec((parts, shards, 1, own, width), lambda i: (0, 0, 3 + i, 0, 0)),
        ],
        out_specs=pl.BlockSpec((1, rows, width), lambda i: (i, 0, 0)),
        scratch_shapes=[pltpu.VMEM((width, width), BF)],
        compiler_params=params(),
        cost_estimate=cost(4 * rows * width * width, 8 * width * width),
        name="source_projection",
    )(source, packed)


def middle_kernel(
    head_count, o_ref, states_ref, gain_two, gain_three, wo_ref, wq_ref, wc_ref, ckv_ref,
    ob_ref, x1_ref, cq_ref, cob_ref, cot_ref, lse_ref, x2_ref, n3_ref, weight, cvt,
):
    rows, width = states_ref.shape
    size = width // head_count
    pair = 2 * size
    for s in range(o_ref.shape[0]):
        inner = o_ref.shape[2]
        ob_ref[:, s * inner : (s + 1) * inner] = o_ref[s]
    whole_weight(wo_ref, weight)

    def add_out(t, _):
        cols = line_tile(t)
        x1_ref[:, cols] = states_ref[:, cols].astype(F32) + nn(ob_ref[...], weight[:, cols])
        return 0

    lax.fori_loop(0, width // TILE, add_out, 0)
    x1 = x1_ref[...]
    n3_ref[...] = (x1 * inverse_rms(x1) * gain_two[...]).astype(BF)
    whole_weight(wq_ref, weight)

    def make_query(t, _):
        cols = line_tile(t)
        cq_ref[:, cols] = nn(n3_ref[...], weight[:, cols]).astype(BF)
        return 0

    lax.fori_loop(0, width // TILE, make_query, 0)

    def attend(p, _):
        cols = line_tile(p, pair)
        keys = ckv_ref[0, :, cols]
        cvt[...] = jnp.transpose(ckv_ref[1, :, cols], (1, 0))
        count = keys.shape[0]
        for half in range(rows // TILE):
            span = slice(half * TILE, (half + 1) * TILE)
            q = cq_ref[span, cols]
            outs = []
            for h in range(2):
                s = nt(keys, head_mask(q, h, 2))
                m = jnp.max(jnp.max(s.reshape(count // 8, 8, TILE), axis=0), axis=0, keepdims=True)
                e = jnp.exp(s - m)
                total = jnp.sum(jnp.sum(e.reshape(count // 8, 8, TILE), axis=0), axis=0, keepdims=True)
                out = nn(cvt[h * size : (h + 1) * size, :], e.astype(BF)) * (1.0 / total)
                lse_ref[p, h : h + 1, span] = m + jnp.log(total)
                outs.append(out)
            both = jnp.concatenate(outs, axis=0)
            cot_ref[p, :, span] = both
            cob_ref[span, cols] = jnp.transpose(both, (1, 0)).astype(BF)
        return 0

    lax.fori_loop(0, width // pair, attend, 0)
    whole_weight(wc_ref, weight)

    def add_cross(t, _):
        cols = line_tile(t)
        x2_ref[:, cols] = x1_ref[:, cols] + nn(cob_ref[...], weight[:, cols])
        return 0

    lax.fori_loop(0, width // TILE, add_cross, 0)
    x2 = x2_ref[...]
    n3_ref[...] = (x2 * inverse_rms(x2) * gain_three[...]).astype(BF)


def middle_forward(o, states, gain_two, gain_three, packed, ckv, head_count):
    rows, width = states.shape
    size = width // head_count
    pairs = head_count // 2
    tokens = lambda dtype: jax.ShapeDtypeStruct((rows, width), dtype)
    shapes = [
        tokens(BF), tokens(F32), tokens(BF), tokens(BF),
        jax.ShapeDtypeStruct((pairs, 2 * size, rows), F32), jax.ShapeDtypeStruct((pairs, 8, rows), F32),
        tokens(F32), tokens(BF),
    ]
    return pl.pallas_call(
        functools.partial(middle_kernel, head_count),
        grid=(1,),
        out_shape=shapes,
        in_specs=[
            whole(o.shape), whole((rows, width)), whole((1, width)), whole((1, width)),
            packed_spec(packed, 0), packed_spec(packed, 1), packed_spec(packed, 2), whole(ckv.shape),
        ],
        out_specs=[whole(s.shape) for s in shapes],
        scratch_shapes=[pltpu.VMEM((width, width), BF), pltpu.VMEM((2 * size, ckv.shape[1]), BF)],
        compiler_params=params(),
        cost_estimate=cost(60 * rows * width * width, 24 * rows * width),
        name="middle_forward",
    )(o, states, gain_two, gain_three, packed, packed, packed, ckv)


def feed_kernel(
    n3_ref, cot_ref, x2_ref, gain_ref, w_ref, wd_ref,
    out_ref, dx2_ref, gain_out_ref, gw_ref, gd_ref, n3t, acc, dn, wg, wu,
):
    step = pl.program_id(0)

    @pl.when(step == 0)
    def _():
        n3t[...] = jnp.transpose(n3_ref[...], (1, 0))
        acc[...] = jnp.zeros_like(acc)
        dn[...] = jnp.zeros_like(dn)

    parts, shards, _, rows, _ = w_ref.shape
    for z in range(shards):
        for c in range(parts):
            start = (z * parts + c) * rows
            wg[start : start + rows, :] = w_ref[c, z, 0]
            wu[start : start + rows, :] = w_ref[c, z, 1]
    n3, cot, wd = n3_ref[...], cot_ref[...], wd_ref[...]
    gate, up = nn(n3, wg[...]), nn(n3, wu[...])
    dh = nt(cot, wd)
    t = jnp.tanh(gelu_scale * (gate + 0.044715 * gate * gate * gate))
    gelu = 0.5 * gate * (1.0 + t)
    slope = 0.5 * (1.0 + t) + 0.5 * gate * (1.0 - t * t) * (gelu_scale * (1.0 + 3 * 0.044715 * gate * gate))
    hidden = (gelu * up).astype(BF)
    dgate = (dh * up * slope).astype(BF)
    dup = (dh * gelu).astype(BF)
    acc[...] += nn(hidden, wd)
    gd_ref[...] = nn(jnp.transpose(hidden, (1, 0)), cot).astype(BF)
    everything = slice(None)
    store_grad(gw_ref, 0, everything, nn(n3t[...], dgate).astype(BF))
    store_grad(gw_ref, 1, everything, nn(n3t[...], dup).astype(BF))
    dn[...] += nt(dgate, wg[...]) + nt(dup, wu[...])

    @pl.when(step == pl.num_programs(0) - 1)
    def _():
        x2 = x2_ref[...]
        out_ref[...] = (x2 + acc[...]).astype(BF)
        dv, gain_out_ref[...] = norm_back(x2, gain_ref[...], dn[...])
        dx2_ref[...] = cot_ref[...].astype(F32) + dv


def feed_forward(n3, cot, x2, gain, wide, down):
    rows, width = n3.shape
    parts, shards, _, own, hidden = wide.shape
    tokens = lambda dtype: jax.ShapeDtypeStruct((rows, width), dtype)
    piece = pl.BlockSpec((parts, shards, 2, own, TILE), lambda i: (0, 0, 0, 0, i))
    return pl.pallas_call(
        feed_kernel,
        grid=(hidden // TILE,),
        out_shape=[
            tokens(BF), tokens(F32), jax.ShapeDtypeStruct((1, width), F32),
            jax.ShapeDtypeStruct(wide.shape, BF), jax.ShapeDtypeStruct(down.shape, BF),
        ],
        in_specs=[
            whole((rows, width)), whole((rows, width)), whole((rows, width)), whole((1, width)),
            piece, pl.BlockSpec((TILE, width), lambda i: (i, 0)),
        ],
        out_specs=[
            whole((rows, width)), whole((rows, width)), whole((1, width)),
            piece, pl.BlockSpec((TILE, width), lambda i: (i, 0)),
        ],
        scratch_shapes=[
            pltpu.VMEM((width, rows), BF), pltpu.VMEM((rows, width), F32), pltpu.VMEM((rows, width), F32),
            pltpu.VMEM((width, TILE), BF), pltpu.VMEM((width, TILE), BF),
        ],
        compiler_params=params(),
        cost_estimate=cost(28 * rows * width * hidden, 12 * width * hidden),
        name="feed_forward",
    )(n3, cot, x2, gain, wide, down)


def middle_back_kernel(
    head_count, dx2_ref, x1_ref, gain_ref, wo_ref, wq_ref, wc_ref, cq_ref, ckv_ref, cot_ref, lse_ref,
    dx1_ref, gain_out_ref, dcq_ref, dckv_ref, dso_ref, weight, dco, ckt, dn,
):
    rows, width = dx2_ref.shape
    size = width // head_count
    pair = 2 * size
    count = ckv_ref.shape[1]
    whole_weight(wc_ref, weight)

    def back_out(t, _):
        dco[:, line_tile(t)] = nt(dx2_ref[...].astype(BF), weight[line_tile(t), :]).astype(BF)
        return 0

    lax.fori_loop(0, width // TILE, back_out, 0)

    def attend(p, _):
        cols = line_tile(p, pair)
        q, do = cq_ref[:, cols], dco[:, cols]
        terms = jnp.transpose(do.astype(F32), (1, 0)) * cot_ref[p]
        ckt[...] = jnp.transpose(ckv_ref[0, :, cols], (1, 0))
        qh = [head_mask(q, h, 2) for h in range(2)]
        doh = [head_mask(do, h, 2) for h in range(2)]
        lse = [lse_ref[p, h : h + 1, :] for h in range(2)]
        delta = [jnp.sum(terms[h * size : (h + 1) * size], axis=0, keepdims=True) for h in range(2)]
        dqt = [None, None]
        for t in range(count // TILE):
            span = slice(t * TILE, (t + 1) * TILE)
            k, v = ckv_ref[0, span, cols], ckv_ref[1, span, cols]
            dk = dv = None
            for h in range(2):
                weights = jnp.exp(nt(k, qh[h]) - lse[h])
                ds = (weights * (nt(v, doh[h]) - delta[h])).astype(BF)
                a, b = nn(weights.astype(BF), doh[h]), nn(ds, qh[h])
                dv = a if dv is None else dv + a
                dk = b if dk is None else dk + b
                c = nn(ckt[h * size : (h + 1) * size, span], ds)
                dqt[h] = c if dqt[h] is None else dqt[h] + c
            dckv_ref[0, span, cols] = dk.astype(BF)
            dckv_ref[1, span, cols] = dv.astype(BF)
        dcq_ref[:, cols] = jnp.transpose(jnp.concatenate(dqt, axis=0), (1, 0)).astype(BF)
        return 0

    lax.fori_loop(0, width // pair, attend, 0)
    whole_weight(wq_ref, weight)

    def back_query(t, _):
        dn[:, line_tile(t)] = nt(dcq_ref[...], weight[line_tile(t), :])
        return 0

    lax.fori_loop(0, width // TILE, back_query, 0)
    dv, gain_out_ref[...] = norm_back(x1_ref[...], gain_ref[...], dn[...])
    dx1_ref[...] = dx2_ref[...] + dv
    whole_weight(wo_ref, weight)
    inner = dso_ref.shape[2]
    per = TILE // inner if inner < TILE else 1
    da = dx1_ref[...].astype(BF)
    for t in range(width // TILE):
        tile = nt(da, weight[t * TILE : (t + 1) * TILE, :]).astype(BF)
        for u in range(per):
            dso_ref[t * per + u] = tile[:, u * inner : (u + 1) * inner]


def middle_back(dx2, x1, gain, packed, cq, ckv, cot, lse, head_count, parts):
    rows, width = dx2.shape
    size = width // head_count
    count = ckv.shape[1]
    shapes = [
        jax.ShapeDtypeStruct((rows, width), F32), jax.ShapeDtypeStruct((1, width), F32),
        jax.ShapeDtypeStruct((rows, width), BF), jax.ShapeDtypeStruct(ckv.shape, BF),
        jax.ShapeDtypeStruct((parts, rows, width // parts), BF),
    ]
    return pl.pallas_call(
        functools.partial(middle_back_kernel, head_count),
        grid=(1,),
        out_shape=shapes,
        in_specs=[
            whole((rows, width)), whole((rows, width)), whole((1, width)),
            packed_spec(packed, 0), packed_spec(packed, 1), packed_spec(packed, 2),
            whole((rows, width)), whole(ckv.shape), whole(cot.shape), whole(lse.shape),
        ],
        out_specs=[whole(s.shape) for s in shapes],
        scratch_shapes=[
            pltpu.VMEM((width, width), BF), pltpu.VMEM((rows, width), BF),
            pltpu.VMEM((2 * size, count), BF), pltpu.VMEM((rows, width), F32),
        ],
        compiler_params=params(),
        cost_estimate=cost(60 * rows * width * width, 24 * rows * width),
        name="middle_back",
    )(dx2, x1, gain, packed, packed, packed, cq, ckv, cot, lse)


def middle_grad_kernel(
    dx2_ref, x1_ref, gain_ref, cob_ref, dcq_ref, dckv_ref, source_ref, ob_ref, dx1_ref, wk_ref, wv_ref,
    g_ref, wk, wv, left, left_source,
):
    width = x1_ref.shape[1]
    parts, shards, _, own, _ = wk_ref.shape
    layout = (parts, shards, 5, own)
    tail = shards * 5 * own
    piece = source_ref.shape[0] // parts
    whole_weight(wk_ref, wk)
    whole_weight(wv_ref, wv)
    for t in range(width // TILE):
        span = slice(t * TILE, (t + 1) * TILE)
        value = (nt(dckv_ref[0], wk[span, :]) + nt(dckv_ref[1], wv[span, :])).astype(BF)
        for c in range(parts):
            g_ref[c, tail : tail + piece, span] = value[c * piece : (c + 1) * piece]

    def product(which, lhs, right):
        def tile(t, _):
            cols = line_tile(t)
            store_rows(g_ref, layout, which, cols, nn(lhs[...], right(cols)).astype(BF))
            return 0

        lax.fori_loop(0, width // TILE, tile, 0)

    left[...] = jnp.transpose(ob_ref[...], (1, 0))
    product(0, left, lambda cols: dx1_ref[:, cols].astype(BF))
    x1 = x1_ref[...]
    left[...] = jnp.transpose((x1 * inverse_rms(x1) * gain_ref[...]).astype(BF), (1, 0))
    product(1, left, lambda cols: dcq_ref[:, cols])
    left[...] = jnp.transpose(cob_ref[...], (1, 0))
    product(2, left, lambda cols: dx2_ref[:, cols].astype(BF))
    left_source[...] = jnp.transpose(source_ref[...], (1, 0))
    product(3, left_source, lambda cols: dckv_ref[0, :, cols])
    product(4, left_source, lambda cols: dckv_ref[1, :, cols])


def middle_grads(dx2, x1, gain, cob, dcq, dckv, source, ob, dx1, packed):
    rows, width = dx2.shape
    count = source.shape[0]
    parts, shards, _, own, _ = packed.shape
    tokens = whole((rows, width))
    shape = (parts, shards * 5 * own + count // parts, width)
    return pl.pallas_call(
        middle_grad_kernel,
        grid=(1,),
        out_shape=jax.ShapeDtypeStruct(shape, BF),
        in_specs=[
            tokens, tokens, whole((1, width)), tokens, tokens, whole(dckv.shape), whole((count, width)), tokens, tokens,
            packed_spec(packed, 3), packed_spec(packed, 4),
        ],
        out_specs=whole(shape),
        scratch_shapes=[
            pltpu.VMEM((width, width), BF), pltpu.VMEM((width, width), BF),
            pltpu.VMEM((width, rows), BF), pltpu.VMEM((width, count), BF),
        ],
        compiler_params=params(),
        cost_estimate=cost(46 * rows * width * width, 24 * rows * width),
        name="middle_grads",
    )(dx2, x1, gain, cob, dcq, dckv, source, ob, dx1, packed, packed)


def final_kernel(d_ref, w_ref, states_ref, gain_ref, dx1_ref, out_ref):
    dn = None
    for s in range(d_ref.shape[0]):
        part = nt(d_ref[s], w_ref[s])
        dn = part if dn is None else dn + part
    dv, _ = norm_back(states_ref[...].astype(F32), gain_ref[...], dn)
    out_ref[...] = dx1_ref[...] + dv


def final_back(dqkv, weights, states, gain, dx1, tile=128):
    parts, rows, inner = dqkv.shape
    width = states.shape[1]
    return pl.pallas_call(
        final_kernel,
        grid=(rows // tile,),
        out_shape=jax.ShapeDtypeStruct((rows, width), F32),
        in_specs=[
            pl.BlockSpec((parts, tile, inner), lambda i: (0, i, 0)),
            whole(weights.shape),
            pl.BlockSpec((tile, width), lambda i: (i, 0)),
            whole((1, width)),
            pl.BlockSpec((tile, width), lambda i: (i, 0)),
        ],
        out_specs=pl.BlockSpec((tile, width), lambda i: (i, 0)),
        compiler_params=params(),
        cost_estimate=cost(6 * rows * width * width, 12 * rows * width),
        name="final_back",
    )(dqkv, weights, states, gain, dx1)


def first_kernel(states_ref, gain_ref, w_ref, out_ref):
    x = states_ref[0].astype(F32)
    n = (x * inverse_rms(x) * gain_ref[...]).astype(BF)
    out_ref[...] = nn(n, w_ref[...]).astype(BF)


def first_projection(gathered, gain, weight, rows):
    parts, _, width = gathered.shape
    cols = weight.shape[1]
    return pl.pallas_call(
        first_kernel,
        grid=(parts,),
        out_shape=jax.ShapeDtypeStruct((parts * rows, cols), BF),
        in_specs=[
            pl.BlockSpec((1, rows, width), lambda i: (i, 0, 0)), whole((1, width)), whole((width, cols)),
        ],
        out_specs=pl.BlockSpec((rows, cols), lambda i: (i, 0)),
        compiler_params=params(),
        cost_estimate=cost(2 * parts * rows * width * cols, 2 * parts * rows * (width + cols)),
        name="first_projection",
    )(gathered, gain, weight)


def last_kernel(states_ref, gain_ref, w_ref, d_ref, gw_ref, gain_out_ref, acc_ref):
    step = pl.program_id(0)
    x = states_ref[0].astype(F32)
    n = (x * inverse_rms(x) * gain_ref[...]).astype(BF)
    g = lax.dot_general(n, d_ref[...], (((0,), (0,)), ((), ())), preferred_element_type=F32)

    @pl.when(step == 0)
    def _():
        acc_ref[...] = g

    @pl.when(step > 0)
    def _():
        acc_ref[...] += g

    @pl.when(step == pl.num_programs(0) - 1)
    def _():
        total = acc_ref[...]
        gw_ref[...] = total.astype(BF)
        gain_out_ref[...] = jnp.sum(total * w_ref[...].astype(F32), axis=1, keepdims=True)


def last_projection(gathered, gain, weight, grads, rows):
    parts, _, width = gathered.shape
    cols = weight.shape[1]
    return pl.pallas_call(
        last_kernel,
        grid=(parts,),
        out_shape=(jax.ShapeDtypeStruct((width, cols), BF), jax.ShapeDtypeStruct((width, 1), F32)),
        in_specs=[
            pl.BlockSpec((1, rows, width), lambda i: (i, 0, 0)), whole((1, width)), whole((width, cols)),
            pl.BlockSpec((rows, cols), lambda i: (i, 0)),
        ],
        out_specs=[whole((width, cols)), whole((width, 1))],
        scratch_shapes=[pltpu.VMEM((width, cols), F32)],
        compiler_params=params(),
        cost_estimate=cost(2 * parts * rows * width * cols, 2 * parts * rows * (width + cols)),
        name="last_projection",
    )(gathered, gain, weight, grads)


CTX = ("plane", "core")


def spread(piece):
    count = lax.axis_size("fsdp")
    return lax.all_to_all(jnp.broadcast_to(piece[None], (count,) + piece.shape), "fsdp", 0, 0, tiled=True)


def collect(parts):
    return jnp.sum(lax.all_to_all(parts, "fsdp", 0, 0, tiled=True).astype(F32), axis=0)


def collect_far(parts):
    count, mine = lax.axis_size("fsdp"), lax.axis_index("fsdp")
    if count > 4:
        return collect(parts)
    total = take(parts, mine, 0).astype(F32)
    for step in range(1, count):
        for sign in (1, -1):
            message = take(parts, jnp.clip(mine + sign * step, 0, count - 1), 0)
            pairs = [(i, i + sign * step) for i in range(count) if 0 <= i + sign * step < count]
            total = total + lax.ppermute(message, "fsdp", pairs).astype(F32)
    return total


def after(value, earlier):
    return lax.optimization_barrier((value, earlier))[0]


def own_rows(shard):
    rows = shard.shape[0] // lax.axis_size(CTX)
    return lax.dynamic_slice_in_dim(shard, lax.axis_index(CTX) * rows, rows, 0)


def swap(value, axis):
    return lax.ppermute(value, axis, [(0, 1), (1, 0)])


def take(value, index, axis):
    return lax.dynamic_index_in_dim(value, index, axis, keepdims=False)


def gather_down(shard):
    core = lax.axis_index("core")
    rows, width = shard.shape
    mine = spread(lax.dynamic_slice_in_dim(shard, core * (rows // 2), rows // 2, 0))
    other = swap(mine, "core")
    first = jnp.where(core == 0, mine, other)
    second = jnp.where(core == 0, other, mine)
    return jnp.stack([first, second], axis=1).reshape(-1, width)


def share_down(grad):
    shards, core = lax.axis_size("fsdp"), lax.axis_index("core")
    halves = grad.reshape(shards, 2, -1, grad.shape[1])
    other = swap(take(halves, 1 - core, 1), "core")
    return (take(halves, core, 1).astype(F32) + other.astype(F32)).astype(BF)


def reduce_planes(half):
    planes, width = lax.axis_size("plane"), half.shape[1]
    if planes != 4:
        return lax.psum_scatter(half, "plane", scatter_dimension=0, tiled=True)
    plane = lax.axis_index("plane")
    for bit, size in ((1, 2), (2, 1)):
        side = (plane // bit) % 2
        split = half.reshape(size, 2, -1, width)
        got = lax.ppermute(take(split, 1 - side, 1), "plane", [(i, i ^ bit) for i in range(4)])
        half = (take(split, side, 1).astype(F32) + got.astype(F32)).astype(BF)
    return half.reshape(-1, width)


def on_device(
    states, positions, segments, encoded, cotangent,
    self_gain, self_query, self_key, self_value, self_output, bias_table,
    cross_gain, cross_query, cross_key, cross_value, cross_output,
    feed_gain, gate_weight, up_weight, down_weight,
):
    parts, shards = lax.axis_size(CTX), lax.axis_size("fsdp")
    place = lax.axis_index(CTX)
    local, width = states.shape[1:]
    head_count = bias_table.shape[1]
    size = width // head_count
    heads = head_count // parts
    inner = heads * size
    blocks = local // BLK
    shard_width = self_gain.shape[0]
    hidden_width = gate_weight.shape[1]
    own = shard_width // parts
    aligned = own % 16 == 0

    def arranged(pieces):
        if aligned:
            return pieces
        matrices, columns = pieces.shape[2], pieces.shape[4]
        return pieces.transpose(2, 1, 0, 3, 4).reshape(1, 1, matrices, width, columns)

    def scattered(grads):
        if aligned:
            return grads
        matrices, columns = grads.shape[2], grads.shape[4]
        return grads.reshape(matrices, shards, parts, own, columns).transpose(2, 1, 0, 3, 4)

    gathered = lax.all_gather(jnp.concatenate([states[0], encoded[0]], axis=0), CTX, axis=0, tiled=False)
    encoded_all = gathered[:, local:].reshape(-1, width)
    columns = lax.dynamic_slice_in_dim(
        jnp.stack([self_query, self_key, self_value], axis=1), place * inner, inner, 2
    ).reshape(shard_width, 3 * inner)
    small = jnp.concatenate([self_gain, cross_gain, feed_gain, bias_table.reshape(-1)])
    small_width = small.shape[0]
    small = jnp.pad(small, (0, 16 * 3 * inner - small_width)).reshape(16, 3 * inner)
    line = spread(jnp.concatenate([columns, small], axis=0))
    qkv_weight = line[:, :shard_width].reshape(width, 3 * inner)
    small = line[:, shard_width:].reshape(shards, -1)[:, :small_width].astype(F32)
    gains = [small[:, i * shard_width : (i + 1) * shard_width].reshape(1, width) for i in range(3)]
    table = small[:, 3 * shard_width :].reshape(BUCKETS, head_count)
    own_table = lax.dynamic_slice_in_dim(table, place * heads, heads, 1).reshape(-1)
    first_pos, first_seg = positions[0, ::BLK], segments[0, ::BLK]
    canon = jnp.where(
        first_seg == 0,
        first_pos // BLK,
        PROMPT // BLK + (first_seg - 1) * (CLEN // BLK) + (first_pos - PROMPT) // BLK,
    )
    canon_all = lax.all_gather(canon, CTX, axis=0, tiled=True)
    slots = jnp.argmax(canon_all[None, :] == jnp.arange(blocks * parts)[:, None], axis=1).astype(jnp.int32)

    squares = jnp.stack([own_rows(w) for w in (self_output, cross_query, cross_output, cross_key, cross_value)], axis=0)
    squares = spread(after(squares, line))
    wide = spread(after(jnp.stack([own_rows(gate_weight), own_rows(up_weight)], axis=0), squares))
    squares = lax.all_gather(after(squares, gathered), CTX, axis=0, tiled=False)

    prompt_tiles = PROMPT // TILE
    qkv = first_projection(gathered, gains[0], qkv_weight, local).reshape(parts * blocks, BLK, 3 * inner)
    o, ot, lse = sa_fwd(slots, own_table, qkv, heads, prompt_tiles)
    o = lax.all_to_all(o.reshape(parts, local, inner), CTX, 0, 0, tiled=True)

    wide = lax.all_gather(after(wide, (squares, lse)), CTX, axis=0, tiled=False)
    qkv_all = lax.all_gather(after(qkv_weight, wide), CTX, axis=0, tiled=False)
    squares, wide = arranged(squares), arranged(wide)
    down = gather_down(after(down_weight, o))
    ckv = source_projection(encoded_all, squares)
    ob, x1, cq, cob, cot, cross_lse, x2, n3 = middle_forward(
        o, states[0], gains[1], gains[2], squares, ckv, head_count
    )
    layer_out, dx2, feed_gain_part, g_wide, g_down = feed_forward(n3, cotangent[0], x2, gains[2], wide, down)
    g_wide = lax.psum_scatter(scattered(g_wide), CTX, scatter_dimension=0, tiled=False)
    g_down = share_down(g_down)
    dx1, cross_gain_part, dcq, dckv, dso = middle_back(
        after(dx2, qkv_all), x1, gains[1], squares, cq, ckv, cot, cross_lse, head_count, parts
    )
    dso = lax.all_to_all(dso, CTX, 0, 0, tiled=True).reshape(parts * blocks, BLK, inner)
    g_squares = middle_grads(dx2, x1, gains[1], cob, dcq, dckv, encoded_all, ob, dx1, squares)
    if not aligned:
        encoded_part = g_squares[0, 5 * width :].reshape(parts, -1, width)
        g_squares = scattered(g_squares[0, : 5 * width].reshape(1, 1, 5, width, width)).reshape(parts, -1, width)
        g_squares = jnp.concatenate([g_squares, encoded_part], axis=1)
    g_squares = lax.psum_scatter(g_squares, CTX, scatter_dimension=0, tiled=False)
    encoded_grad = g_squares[shards * 5 * own :].astype(F32)
    g_squares = collect(g_squares[: shards * 5 * own].reshape(shards, 5 * own, width)).astype(BF)

    middle = prompt_tiles + (blocks * parts * BLK // TILE - prompt_tiles) // 4
    g_down = collect(after(g_down, dso)).astype(BF)
    held = sa_bwd(slots, own_table, qkv, dso, ot, lse, heads, prompt_tiles, 0, middle)
    second = after(dso, g_wide)
    g_wide = collect_far(g_wide).astype(BF)
    dqkv, dtable = sa_bwd(
        slots, own_table, qkv, second, ot, lse, heads, prompt_tiles, middle, blocks * parts * BLK // TILE, held
    )
    grads = after(dqkv, (g_down, g_wide)).reshape(parts * local, 3 * inner)
    g_qkv, self_gain_part = last_projection(gathered, gains[0], qkv_weight, grads, local)
    g_down = reduce_planes(g_down)
    dqkv = lax.all_to_all(dqkv.reshape(parts, local, 3 * inner), CTX, 0, 0, tiled=True)
    states_grad = final_back(dqkv, qkv_all, states[0], gains[0], dx1)

    table_part = jnp.zeros((BUCKETS, head_count), F32)
    table_part = lax.dynamic_update_slice_in_dim(table_part, dtable[:, :, 0].T, place * heads, 1)
    sums = [self_gain_part[:, 0] / gains[0][0], cross_gain_part[0], feed_gain_part[0]]
    sums = jnp.concatenate([v.reshape(shards, shard_width) for v in sums] + [table_part.reshape(shards, -1)], axis=1)
    sums = jnp.pad(sums, ((0, 0), (0, 16 * 3 * inner - small_width))).reshape(shards, 16, 3 * inner).astype(BF)
    last = jnp.concatenate([g_qkv.reshape(shards, shard_width, 3 * inner), sums], axis=1)
    last = lax.all_gather(collect(last).astype(BF), CTX, axis=0, tiled=False)
    sums = jnp.sum(last[:, shard_width:].reshape(parts, -1)[:, :small_width].astype(F32), axis=0)
    g_qkv = last[:, :shard_width].astype(F32).reshape(parts, shard_width, 3, inner).transpose(2, 1, 0, 3)
    g_qkv = g_qkv.reshape(3, shard_width, width)
    gain_grads = [sums[i * shard_width : (i + 1) * shard_width] for i in range(3)]
    table_grad = sums[3 * shard_width :].reshape(-1, head_count)
    g_wide = lax.all_gather(g_wide, CTX, axis=0, tiled=False).astype(F32)
    g_wide = g_wide.transpose(1, 0, 2, 3).reshape(2, shard_width, hidden_width)
    rest = lax.all_gather(jnp.concatenate([g_squares, g_down], axis=0), CTX, axis=0, tiled=False).astype(F32)
    g_squares = rest[:, : 5 * own].reshape(parts, 5, own, width).transpose(1, 0, 2, 3).reshape(5, shard_width, width)
    g_down = rest[:, 5 * own :].reshape(parts // 2, 2, -1, width).transpose(1, 0, 2, 3).reshape(-1, width)
    return (
        layer_out[None], states_grad[None], encoded_grad[None],
        gain_grads[0], g_qkv[0], g_qkv[1], g_qkv[2], g_squares[0], table_grad,
        gain_grads[1], g_squares[1], g_squares[3], g_squares[4], g_squares[2],
        gain_grads[2], g_wide[0], g_wide[1], g_down,
    )


def solution(mesh):
    ctx, fsdp = mesh.devices.shape
    split = Mesh(mesh.devices.reshape(ctx // 2, 2, fsdp), ("plane", "core", "fsdp"))
    tokens, matrix, vector = P("fsdp", CTX, None), P("fsdp", None), P("fsdp")
    place = P("fsdp", CTX)
    return jax.shard_map(
        on_device,
        mesh=split,
        in_specs=(tokens, place, place, tokens, tokens)
        + (vector, matrix, matrix, matrix, matrix, matrix)
        + (vector, matrix, matrix, matrix, matrix)
        + (vector, matrix, matrix, matrix),
        out_specs=(tokens, tokens, tokens)
        + (vector, matrix, matrix, matrix, matrix, matrix)
        + (vector, matrix, matrix, matrix, matrix)
        + (vector, matrix, matrix, matrix),
        check_vma=False,
    )
```

```python
import functools
import math

import jax
import jax.numpy as jnp
from jax import lax
from jax.experimental import pallas as pl
from jax.experimental.pallas import tpu as pltpu
from jax.sharding import Mesh
from jax.sharding import PartitionSpec as P

BUCKETS = 32
DISTANCE = 128
PROMPT = 2048
CLEN = 256
BLK = 128
TILE = 256
NEG = -1e30
F32 = jnp.float32
BF = jnp.bfloat16
epsilon = 1e-06
gelu_scale = math.sqrt(2.0 / math.pi)
VMEM_LIMIT = 56 * 1024 * 1024


def bucket_starts():
    half=BUCKETS//2
    edges=[math.ceil(half*(DISTANCE/half)**(e/half)) for e in range(1,half)]
    return list(range(half+1))+edges

def nt(a,b):
    return lax.dot_general(a,b,(((1,),(1,)),((),())),preferred_element_type=F32)
def nn(a,b):
    return lax.dot_general(a,b,(((1,),(0,)),((),())),preferred_element_type=F32)

def head_mask(value,head,heads):
    if heads==1: return value
    size=value.shape[-1]//heads
    lane=lax.broadcasted_iota(jnp.int32,value.shape,1)
    return jnp.where((lane>=head*size)&(lane<(head+1)*size),value,jnp.zeros_like(value))

def build_bias(tab_ref,bias_ref,heads):
    starts=bucket_starts()
    key=lax.broadcasted_iota(jnp.int32,(BLK,BLK),0)
    query=lax.broadcasted_iota(jnp.int32,(BLK,BLK),1)
    for h in range(heads):
        last=tab_ref[(BUCKETS-1)*heads+h]
        for sub in (0,1):
            dist=query-key+BLK*sub
            val=jnp.full((BLK,BLK),tab_ref[h]-last,F32)
            for b in range(1,BUCKETS):
                val=jnp.where(dist>=starts[b],tab_ref[b*heads+h]-last,val)
            if sub==0:
                val=jnp.where(dist>=0,val,NEG)
                bias_ref[h,0:BLK,0:BLK]=val
                bias_ref[h,BLK:,BLK:]=val
            else:
                bias_ref[h,0:BLK,BLK:]=val
        bias_ref[h,BLK:,0:BLK]=jnp.full((BLK,BLK),NEG,F32)

def load_tile(src,slots,tile,lo,hi):
    a=src[slots[2*tile],:,lo:hi]
    b=src[slots[2*tile+1],:,lo:hi]
    return jnp.concatenate([a,b],axis=0)

def fwd_kernel(heads,prompt_tiles,slots,tab,qkv,o_ref,ot_ref,lse_ref,bias,kc,vt,qm,s_scr):
    tiles=kc.shape[0]//TILE
    width=kc.shape[1]
    size=width//heads
    build_bias(tab,bias,heads)
    def arrange(t,_):
        rows=pl.ds(pl.multiple_of(t*TILE,TILE),TILE)
        kc[rows,:]=load_tile(qkv,slots,t,width,2*width)
        vt[t]=jnp.transpose(load_tile(qkv,slots,t,2*width,3*width),(1,0))
        return 0
    lax.fori_loop(0,tiles,arrange,0)

    def scores(t_rows,h,kind,qh):
        s=nt(kc[t_rows,:],qh)
        if kind=="own":
            s=s+bias[h]
        elif kind=="prev":
            top=s[:BLK]
            low=jnp.concatenate([s[BLK:,:BLK]+bias[h,0:BLK,BLK:],s[BLK:,BLK:]],axis=1)
            s=jnp.concatenate([top,low],axis=0)
        return s

    def tile_body(t,n_far,own_static):
        q=load_tile(qkv,slots,t,0,width)
        outs=[]
        for h in range(heads):
            qh=head_mask(q,h,heads)
            m=None
            for j in range(n_far+1):
                if j<n_far:
                    rows=pl.ds(j*TILE,TILE); kind="prev" if j==n_far-1 else "far"
                else:
                    rows=pl.ds(pl.multiple_of(t*TILE,TILE),TILE) if not own_static else pl.ds(t*TILE,TILE); kind="own"
                s=scores(rows,h,kind,qh)
                s_scr[h,j]=s
                part=jnp.max(s.reshape(TILE//8,8,TILE),axis=0)
                m=part if m is None else jnp.maximum(m,part)
            m=jnp.max(m,axis=0,keepdims=True)
            l=None; acc=None
            for j in range(n_far+1):
                p=jnp.exp(s_scr[h,j]-m)
                part=jnp.sum(p.reshape(TILE//8,8,TILE),axis=0)
                l=part if l is None else l+part
                vrow=j if j<n_far else t
                a=nn(vt[vrow,h*size:(h+1)*size,:],p.astype(BF))
                acc=a if acc is None else acc+a
            l=jnp.sum(l,axis=0,keepdims=True)
            o=acc*(1.0/l)
            cols=pl.ds(t*TILE if own_static else pl.multiple_of(t*TILE,TILE),TILE)
            ot_ref[h*size:(h+1)*size,cols]=o
            lse_ref[h:h+1,cols]=m+jnp.log(l)
            outs.append(o)
        o=jnp.concatenate(outs,axis=0) if heads>1 else outs[0]
        o=jnp.transpose(o,(1,0)).astype(BF)
        o_ref[slots[2*t]]=o[:BLK]
        o_ref[slots[2*t+1]]=o[BLK:]
    for t in range(prompt_tiles):
        tile_body(t,t,True)
    def cont(c,_):
        tile_body(c,prompt_tiles,False)
        return 0
    lax.fori_loop(prompt_tiles,tiles,cont,0)

def sa_fwd(slots,tab,qkv,heads,prompt_tiles):
    nb,_,w3=qkv.shape; w=w3//3; n=nb*BLK; tiles=n//TILE
    return pl.pallas_call(
        functools.partial(fwd_kernel,heads,prompt_tiles),
        out_shape=(jax.ShapeDtypeStruct((nb,BLK,w),BF),jax.ShapeDtypeStruct((w,n),F32),jax.ShapeDtypeStruct((heads,n),F32)),
        in_specs=[pl.BlockSpec(memory_space=pltpu.SMEM),pl.BlockSpec(memory_space=pltpu.SMEM),pl.BlockSpec(memory_space=pltpu.VMEM)],
        out_specs=[pl.BlockSpec(memory_space=pltpu.VMEM)]*3,
        scratch_shapes=[pltpu.VMEM((heads,TILE,TILE),F32),pltpu.VMEM((n,w),BF),pltpu.VMEM((tiles,w,TILE),BF),pltpu.VMEM((8,128),F32),pltpu.VMEM((heads,prompt_tiles+1,TILE,TILE),F32)],
        compiler_params=pltpu.CompilerParams(vmem_limit_bytes=VMEM_LIMIT),
        cost_estimate=pl.CostEstimate(flops=32 * 10**9, bytes_accessed=8 * n * w3, transcendentals=0),
        name="self_attention_forward",
    )(slots,tab,qkv)

def bwd_kernel(heads,prompt_tiles,unroll,low,high,slots,tab,qkv,do_ref,ot_ref,lse_ref,*refs):
    if low:
        dq_in,dkv_in,near_in,far_in,dqkv_ref,dtab_ref,bias,kc,vc,kt,dqt,dkv,near,far=refs
    else:
        dq_out,dkv,near,far,bias,kc,vc,kt,dqt=refs
    tiles=kc.shape[0]//TILE
    width=kc.shape[1]
    size=width//heads
    build_bias(tab,bias,heads)
    for mine,start in ((near,near_in if low else None),(far,far_in if low else None),(dkv,dkv_in if low else None)):
        mine[...]=start[...] if low else jnp.zeros_like(mine)
    def arrange(t,_):
        rows=pl.ds(pl.multiple_of(t*TILE,TILE),TILE)
        k=load_tile(qkv,slots,t,width,2*width)
        kc[rows,:]=k
        kt[t]=jnp.transpose(k,(1,0))
        vc[rows,:]=load_tile(qkv,slots,t,2*width,3*width)
        return 0
    lax.fori_loop(0,tiles,arrange,0)

    def query_tile(t,_):
        cols=pl.ds(pl.multiple_of(t*TILE,TILE),TILE)
        q=load_tile(qkv,slots,t,0,width)
        do=load_tile(do_ref,slots,t,0,width)
        dot=jnp.transpose(do.astype(F32),(1,0))*ot_ref[:,cols]
        qh=[head_mask(q,h,heads) for h in range(heads)]
        doh=[head_mask(do,h,heads) for h in range(heads)]
        lse=[lse_ref[h:h+1,cols] for h in range(heads)]
        delta=[jnp.sum(dot[h*size:(h+1)*size],axis=0,keepdims=True) for h in range(heads)]
        dqt[...]=jnp.zeros_like(dqt)

        def piece(j,kind):
            rows=pl.ds(pl.multiple_of(j*TILE,TILE),TILE)
            k=kc[rows,:]; v=vc[rows,:]
            dv=None; dk=None
            for h in range(heads):
                s=nt(k,qh[h])
                if kind=="own":
                    s=s+bias[h]
                elif kind=="prev":
                    low=jnp.concatenate([s[BLK:,:BLK]+bias[h,0:BLK,BLK:],s[BLK:,BLK:]],axis=1)
                    s=jnp.concatenate([s[:BLK],low],axis=0)
                p=jnp.exp(s-lse[h])
                dp=nt(v,doh[h])
                ds=p*(dp-delta[h])
                if kind=="own":
                    near[h,0]+=ds[:BLK,:BLK]+ds[BLK:,BLK:]
                    near[h,1]+=ds[:BLK,BLK:]
                elif kind=="prev":
                    near[h,1]+=ds[BLK:,:BLK]
                    f=jnp.sum(ds[:BLK].reshape(BLK//8,8,TILE),axis=0)
                    f2=jnp.sum(ds[BLK:,BLK:].reshape(BLK//8,8,BLK),axis=0)
                    far[h]+=f
                    far[h,:,BLK:]+=f2
                else:
                    far[h]+=jnp.sum(ds.reshape(TILE//8,8,TILE),axis=0)
                pb=p.astype(BF); db=ds.astype(BF)
                a=nn(pb,doh[h]); dv=a if dv is None else dv+a
                b=nn(db,qh[h]); dk=b if dk is None else dk+b
                dqt[h*size:(h+1)*size,:]+=nn(kt[j,h*size:(h+1)*size,:],db)
            dkv[rows,0:width]+=dk
            dkv[rows,width:2*width]+=dv
        n_far=jnp.maximum(jnp.minimum(t,prompt_tiles)-1,0)
        def far_step(j,_):
            piece(j,"far"); return 0
        def far_many(j,_):
            for u in range(unroll): piece(j*unroll+u,"far")
            return 0
        if unroll>1:
            lax.fori_loop(0,n_far//unroll,far_many,0)
            lax.fori_loop((n_far//unroll)*unroll,n_far,far_step,0)
        else:
            lax.fori_loop(0,n_far,far_step,0)
        @pl.when(t>0)
        def _():
            piece(n_far,"prev")
        piece(t,"own")
        dq=jnp.transpose(dqt[...],(1,0)).astype(BF)
        if low:
            dqkv_ref[slots[2*t],:,0:width]=dq[:BLK]
            dqkv_ref[slots[2*t+1],:,0:width]=dq[BLK:]
        else:
            dq_out[cols,:]=dq
        return 0
    lax.fori_loop(low,high,query_tile,0)
    if not low:
        return
    def bring(t,_):
        dq=dq_in[pl.ds(pl.multiple_of(t*TILE,TILE),TILE),:]
        dqkv_ref[slots[2*t],:,0:width]=dq[:BLK]
        dqkv_ref[slots[2*t+1],:,0:width]=dq[BLK:]
        return 0
    lax.fori_loop(0,low,bring,0)
    def finish(t,_):
        g=dkv[pl.ds(pl.multiple_of(t*TILE,TILE),TILE),:].astype(BF)
        dqkv_ref[slots[2*t],:,width:3*width]=g[:BLK]
        dqkv_ref[slots[2*t+1],:,width:3*width]=g[BLK:]
        return 0
    lax.fori_loop(0,tiles,finish,0)
    starts=bucket_starts()
    key=lax.broadcasted_iota(jnp.int32,(BLK,BLK),0)
    query=lax.broadcasted_iota(jnp.int32,(BLK,BLK),1)
    for h in range(heads):
        for b in range(BUCKETS):
            total=jnp.zeros((8,BLK),F32)
            for sub in (0,1):
                dist=query-key+BLK*sub
                inside=dist>=starts[b]
                if b<BUCKETS-1: inside=inside&(dist<starts[b+1])
                total=total+jnp.sum(jnp.where(inside,near[h,sub],0.0).reshape(BLK//8,8,BLK),axis=0)
            if b==BUCKETS-1:
                total=total+far[h,:,0:BLK]+far[h,:,BLK:]
            row=jnp.sum(total,axis=0,keepdims=True)
            dtab_ref[h,b:b+1,:]=jnp.broadcast_to(jnp.sum(row,axis=1,keepdims=True),(1,BLK))

def sa_bwd(slots,tab,qkv,do,ot,lse,heads,prompt_tiles,low,high,held=(),unroll=2):
    nb,_,w3=qkv.shape; w=w3//3; n=nb*BLK; tiles=n//TILE
    shape=jax.ShapeDtypeStruct
    sums=[shape((n,2*w),F32),shape((heads,2,BLK,BLK),F32),shape((heads,8,TILE),F32)]
    if low:
        out=[shape((nb,BLK,w3),BF),shape((heads,BUCKETS,BLK),F32)]
    else:
        out=[shape((high*TILE,w),BF)]+sums
    scratch=[pltpu.VMEM((heads,TILE,TILE),F32),pltpu.VMEM((n,w),BF),pltpu.VMEM((n,w),BF),pltpu.VMEM((tiles,w,TILE),BF),pltpu.VMEM((w,TILE),F32)]
    if low:
        scratch+=[pltpu.VMEM(v.shape,F32) for v in sums]
    return pl.pallas_call(
        functools.partial(bwd_kernel,heads,prompt_tiles,unroll,low,high),
        out_shape=out,
        in_specs=[pl.BlockSpec(memory_space=pltpu.SMEM)]*2+[pl.BlockSpec(memory_space=pltpu.VMEM)]*(4+len(held)),
        out_specs=[pl.BlockSpec(memory_space=pltpu.VMEM)]*len(out),
        scratch_shapes=scratch,
        compiler_params=pltpu.CompilerParams(vmem_limit_bytes=VMEM_LIMIT),
        cost_estimate=pl.CostEstimate(flops=43 * 10**9, bytes_accessed=12 * n * w3, transcendentals=0),
        name="self_attention_backward",
    )(slots,tab,qkv,do,ot,lse,*held)


def line_tile(step, size=TILE):
    return pl.ds(pl.multiple_of(step * size, size), size)


def whole_weight(ref, scratch):
    parts, shards, _, rows, _ = ref.shape
    for z in range(shards):
        for c in range(parts):
            start = (z * parts + c) * rows
            scratch[start : start + rows, :] = ref[c, z, 0]


def store_rows(ref, layout, which, cols, value):
    parts, shards, matrices, rows = layout
    for z in range(shards):
        for c in range(parts):
            start = (z * parts + c) * rows
            place = (z * matrices + which) * rows
            ref[c, place : place + rows, cols] = value[start : start + rows]


def store_grad(ref, which, cols, value):
    parts, shards, _, rows, _ = ref.shape
    for z in range(shards):
        for c in range(parts):
            start = (z * parts + c) * rows
            ref[c, z, which, :, cols] = value[start : start + rows]


def inverse_rms(v):
    return lax.rsqrt(jnp.mean(v * v, axis=-1, keepdims=True) + epsilon)


def norm_back(v, gain, dn):
    r = inverse_rms(v)
    weighted = dn * gain
    dv = r * weighted - v * (r * r * r) * jnp.mean(weighted * v, axis=-1, keepdims=True)
    return dv, jnp.sum(dn * v * r, axis=0, keepdims=True)


def whole(shape, index=None):
    zeros = (0,) * len(shape)
    return pl.BlockSpec(shape, lambda *_: zeros if index is None else index)


def packed_spec(packed, which):
    parts, shards, _, rows, width = packed.shape
    return pl.BlockSpec((parts, shards, 1, rows, width), lambda *_: (0, 0, which, 0, 0))


def params():
    return pltpu.CompilerParams(vmem_limit_bytes=VMEM_LIMIT)


def cost(flops, size):
    return pl.CostEstimate(flops=flops, bytes_accessed=size, transcendentals=0)


def source_kernel(source_ref, w_ref, out_ref, weight):
    whole_weight(w_ref, weight)
    source = source_ref[...]
    for t in range(out_ref.shape[-1] // TILE):
        cols = slice(t * TILE, (t + 1) * TILE)
        out_ref[0, :, cols] = nn(source, weight[:, cols]).astype(BF)


def source_projection(source, packed):
    rows, width = source.shape
    parts, shards, _, own, _ = packed.shape
    return pl.pallas_call(
        source_kernel,
        grid=(2,),
        out_shape=jax.ShapeDtypeStruct((2, rows, width), BF),
        in_specs=[
            whole((rows, width)),
            pl.BlockSpec((parts, shards, 1, own, width), lambda i: (0, 0, 3 + i, 0, 0)),
        ],
        out_specs=pl.BlockSpec((1, rows, width), lambda i: (i, 0, 0)),
        scratch_shapes=[pltpu.VMEM((width, width), BF)],
        compiler_params=params(),
        cost_estimate=cost(4 * rows * width * width, 8 * width * width),
        name="source_projection",
    )(source, packed)


def middle_kernel(
    head_count, o_ref, states_ref, gain_two, gain_three, wo_ref, wq_ref, wc_ref, ckv_ref,
    ob_ref, x1_ref, cq_ref, cob_ref, cot_ref, lse_ref, x2_ref, n3_ref, weight, cvt,
):
    rows, width = states_ref.shape
    size = width // head_count
    pair = 2 * size
    for s in range(o_ref.shape[0]):
        inner = o_ref.shape[2]
        ob_ref[:, s * inner : (s + 1) * inner] = o_ref[s]
    whole_weight(wo_ref, weight)

    def add_out(t, _):
        cols = line_tile(t)
        x1_ref[:, cols] = states_ref[:, cols].astype(F32) + nn(ob_ref[...], weight[:, cols])
        return 0

    lax.fori_loop(0, width // TILE, add_out, 0)
    x1 = x1_ref[...]
    n3_ref[...] = (x1 * inverse_rms(x1) * gain_two[...]).astype(BF)
    whole_weight(wq_ref, weight)

    def make_query(t, _):
        cols = line_tile(t)
        cq_ref[:, cols] = nn(n3_ref[...], weight[:, cols]).astype(BF)
        return 0

    lax.fori_loop(0, width // TILE, make_query, 0)

    def attend(p, _):
        cols = line_tile(p, pair)
        keys = ckv_ref[0, :, cols]
        cvt[...] = jnp.transpose(ckv_ref[1, :, cols], (1, 0))
        count = keys.shape[0]
        for half in range(rows // TILE):
            span = slice(half * TILE, (half + 1) * TILE)
            q = cq_ref[span, cols]
            outs = []
            for h in range(2):
                s = nt(keys, head_mask(q, h, 2))
                m = jnp.max(jnp.max(s.reshape(count // 8, 8, TILE), axis=0), axis=0, keepdims=True)
                e = jnp.exp(s - m)
                total = jnp.sum(jnp.sum(e.reshape(count // 8, 8, TILE), axis=0), axis=0, keepdims=True)
                out = nn(cvt[h * size : (h + 1) * size, :], e.astype(BF)) * (1.0 / total)
                lse_ref[p, h : h + 1, span] = m + jnp.log(total)
                outs.append(out)
            both = jnp.concatenate(outs, axis=0)
            cot_ref[p, :, span] = both
            cob_ref[span, cols] = jnp.transpose(both, (1, 0)).astype(BF)
        return 0

    lax.fori_loop(0, width // pair, attend, 0)
    whole_weight(wc_ref, weight)

    def add_cross(t, _):
        cols = line_tile(t)
        x2_ref[:, cols] = x1_ref[:, cols] + nn(cob_ref[...], weight[:, cols])
        return 0

    lax.fori_loop(0, width // TILE, add_cross, 0)
    x2 = x2_ref[...]
    n3_ref[...] = (x2 * inverse_rms(x2) * gain_three[...]).astype(BF)


def middle_forward(o, states, gain_two, gain_three, packed, ckv, head_count):
    rows, width = states.shape
    size = width // head_count
    pairs = head_count // 2
    tokens = lambda dtype: jax.ShapeDtypeStruct((rows, width), dtype)
    shapes = [
        tokens(BF), tokens(F32), tokens(BF), tokens(BF),
        jax.ShapeDtypeStruct((pairs, 2 * size, rows), F32), jax.ShapeDtypeStruct((pairs, 8, rows), F32),
        tokens(F32), tokens(BF),
    ]
    return pl.pallas_call(
        functools.partial(middle_kernel, head_count),
        grid=(1,),
        out_shape=shapes,
        in_specs=[
            whole(o.shape), whole((rows, width)), whole((1, width)), whole((1, width)),
            packed_spec(packed, 0), packed_spec(packed, 1), packed_spec(packed, 2), whole(ckv.shape),
        ],
        out_specs=[whole(s.shape) for s in shapes],
        scratch_shapes=[pltpu.VMEM((width, width), BF), pltpu.VMEM((2 * size, ckv.shape[1]), BF)],
        compiler_params=params(),
        cost_estimate=cost(60 * rows * width * width, 24 * rows * width),
        name="middle_forward",
    )(o, states, gain_two, gain_three, packed, packed, packed, ckv)


def feed_kernel(
    core_ref, n3_ref, cot_ref, x2_ref, gain_ref, w_ref, mine_ref, other_ref,
    out_ref, dx2_ref, gain_out_ref, gw_ref, keep_ref, give_ref, n3t, acc, dn, wg, wu, down,
):
    half = mine_ref.shape[1]
    own_half = pl.ds(pl.multiple_of(core_ref[0] * half, half), half)
    other_half = pl.ds(pl.multiple_of((1 - core_ref[0]) * half, half), half)
    down[:, own_half] = mine_ref[...]
    down[:, other_half] = other_ref[...]
    step = pl.program_id(0)

    @pl.when(step == 0)
    def _():
        n3t[...] = jnp.transpose(n3_ref[...], (1, 0))
        acc[...] = jnp.zeros_like(acc)
        dn[...] = jnp.zeros_like(dn)

    parts, shards, _, rows, _ = w_ref.shape
    for z in range(shards):
        for c in range(parts):
            start = (z * parts + c) * rows
            wg[start : start + rows, :] = w_ref[c, z, 0]
            wu[start : start + rows, :] = w_ref[c, z, 1]
    n3, cot, wd = n3_ref[...], cot_ref[...], down[...]
    gate, up = nn(n3, wg[...]), nn(n3, wu[...])
    dh = nt(cot, wd)
    t = jnp.tanh(gelu_scale * (gate + 0.044715 * gate * gate * gate))
    gelu = 0.5 * gate * (1.0 + t)
    slope = 0.5 * (1.0 + t) + 0.5 * gate * (1.0 - t * t) * (gelu_scale * (1.0 + 3 * 0.044715 * gate * gate))
    hidden = (gelu * up).astype(BF)
    dgate = (dh * up * slope).astype(BF)
    dup = (dh * gelu).astype(BF)
    acc[...] += nn(hidden, wd)
    down[...] = nn(jnp.transpose(hidden, (1, 0)), cot).astype(BF)
    keep_ref[...] = down[:, own_half]
    give_ref[...] = down[:, other_half]
    everything = slice(None)
    store_grad(gw_ref, 0, everything, nn(n3t[...], dgate).astype(BF))
    store_grad(gw_ref, 1, everything, nn(n3t[...], dup).astype(BF))
    dn[...] += nt(dgate, wg[...]) + nt(dup, wu[...])

    @pl.when(step == pl.num_programs(0) - 1)
    def _():
        x2 = x2_ref[...]
        out_ref[...] = (x2 + acc[...]).astype(BF)
        dv, gain_out_ref[...] = norm_back(x2, gain_ref[...], dn[...])
        dx2_ref[...] = cot_ref[...].astype(F32) + dv


def feed_forward(core, n3, cot, x2, gain, wide, mine, other):
    rows, width = n3.shape
    parts, shards, _, own, hidden = wide.shape
    tokens = lambda dtype: jax.ShapeDtypeStruct((rows, width), dtype)
    part = pl.BlockSpec((TILE, width // 2), lambda i: (i, 0))
    piece = pl.BlockSpec((parts, shards, 2, own, TILE), lambda i: (0, 0, 0, 0, i))
    return pl.pallas_call(
        feed_kernel,
        grid=(hidden // TILE,),
        out_shape=[
            tokens(BF), tokens(F32), jax.ShapeDtypeStruct((1, width), F32),
            jax.ShapeDtypeStruct(wide.shape, BF), jax.ShapeDtypeStruct(mine.shape, BF), jax.ShapeDtypeStruct(mine.shape, BF),
        ],
        in_specs=[
            pl.BlockSpec(memory_space=pltpu.SMEM),
            whole((rows, width)), whole((rows, width)), whole((rows, width)), whole((1, width)), piece, part, part,
        ],
        out_specs=[
            whole((rows, width)), whole((rows, width)), whole((1, width)),
            piece, part, part,
        ],
        scratch_shapes=[
            pltpu.VMEM((width, rows), BF), pltpu.VMEM((rows, width), F32), pltpu.VMEM((rows, width), F32),
            pltpu.VMEM((width, TILE), BF), pltpu.VMEM((width, TILE), BF), pltpu.VMEM((TILE, width), BF),
        ],
        compiler_params=params(),
        cost_estimate=cost(28 * rows * width * hidden, 12 * width * hidden),
        name="feed_forward",
    )(core, n3, cot, x2, gain, wide, mine, other)


def middle_back_kernel(
    head_count, dx2_ref, x1_ref, gain_ref, wo_ref, wq_ref, wc_ref, cq_ref, ckv_ref, cot_ref, lse_ref,
    dx1_ref, gain_out_ref, dcq_ref, dckv_ref, dso_ref, weight, dco, ckt, dn,
):
    rows, width = dx2_ref.shape
    size = width // head_count
    pair = 2 * size
    count = ckv_ref.shape[1]
    whole_weight(wc_ref, weight)

    def back_out(t, _):
        dco[:, line_tile(t)] = nt(dx2_ref[...].astype(BF), weight[line_tile(t), :]).astype(BF)
        return 0

    lax.fori_loop(0, width // TILE, back_out, 0)

    def attend(p, _):
        cols = line_tile(p, pair)
        q, do = cq_ref[:, cols], dco[:, cols]
        terms = jnp.transpose(do.astype(F32), (1, 0)) * cot_ref[p]
        ckt[...] = jnp.transpose(ckv_ref[0, :, cols], (1, 0))
        qh = [head_mask(q, h, 2) for h in range(2)]
        doh = [head_mask(do, h, 2) for h in range(2)]
        lse = [lse_ref[p, h : h + 1, :] for h in range(2)]
        delta = [jnp.sum(terms[h * size : (h + 1) * size], axis=0, keepdims=True) for h in range(2)]
        dqt = [None, None]
        for t in range(count // TILE):
            span = slice(t * TILE, (t + 1) * TILE)
            k, v = ckv_ref[0, span, cols], ckv_ref[1, span, cols]
            dk = dv = None
            for h in range(2):
                weights = jnp.exp(nt(k, qh[h]) - lse[h])
                ds = (weights * (nt(v, doh[h]) - delta[h])).astype(BF)
                a, b = nn(weights.astype(BF), doh[h]), nn(ds, qh[h])
                dv = a if dv is None else dv + a
                dk = b if dk is None else dk + b
                c = nn(ckt[h * size : (h + 1) * size, span], ds)
                dqt[h] = c if dqt[h] is None else dqt[h] + c
            dckv_ref[0, span, cols] = dk.astype(BF)
            dckv_ref[1, span, cols] = dv.astype(BF)
        dcq_ref[:, cols] = jnp.transpose(jnp.concatenate(dqt, axis=0), (1, 0)).astype(BF)
        return 0

    lax.fori_loop(0, width // pair, attend, 0)
    whole_weight(wq_ref, weight)

    def back_query(t, _):
        dn[:, line_tile(t)] = nt(dcq_ref[...], weight[line_tile(t), :])
        return 0

    lax.fori_loop(0, width // TILE, back_query, 0)
    dv, gain_out_ref[...] = norm_back(x1_ref[...], gain_ref[...], dn[...])
    dx1_ref[...] = dx2_ref[...] + dv
    whole_weight(wo_ref, weight)
    inner = dso_ref.shape[2]
    per = TILE // inner if inner < TILE else 1
    da = dx1_ref[...].astype(BF)
    for t in range(width // TILE):
        tile = nt(da, weight[t * TILE : (t + 1) * TILE, :]).astype(BF)
        for u in range(per):
            dso_ref[t * per + u] = tile[:, u * inner : (u + 1) * inner]


def middle_back(dx2, x1, gain, packed, cq, ckv, cot, lse, head_count, parts):
    rows, width = dx2.shape
    size = width // head_count
    count = ckv.shape[1]
    shapes = [
        jax.ShapeDtypeStruct((rows, width), F32), jax.ShapeDtypeStruct((1, width), F32),
        jax.ShapeDtypeStruct((rows, width), BF), jax.ShapeDtypeStruct(ckv.shape, BF),
        jax.ShapeDtypeStruct((parts, rows, width // parts), BF),
    ]
    return pl.pallas_call(
        functools.partial(middle_back_kernel, head_count),
        grid=(1,),
        out_shape=shapes,
        in_specs=[
            whole((rows, width)), whole((rows, width)), whole((1, width)),
            packed_spec(packed, 0), packed_spec(packed, 1), packed_spec(packed, 2),
            whole((rows, width)), whole(ckv.shape), whole(cot.shape), whole(lse.shape),
        ],
        out_specs=[whole(s.shape) for s in shapes],
        scratch_shapes=[
            pltpu.VMEM((width, width), BF), pltpu.VMEM((rows, width), BF),
            pltpu.VMEM((2 * size, count), BF), pltpu.VMEM((rows, width), F32),
        ],
        compiler_params=params(),
        cost_estimate=cost(60 * rows * width * width, 24 * rows * width),
        name="middle_back",
    )(dx2, x1, gain, packed, packed, packed, cq, ckv, cot, lse)


def middle_grad_kernel(
    dx2_ref, x1_ref, gain_ref, cob_ref, dcq_ref, dckv_ref, source_ref, ob_ref, dx1_ref, wk_ref, wv_ref,
    g_ref, wk, wv, left, left_source,
):
    width = x1_ref.shape[1]
    parts, shards, _, own, _ = wk_ref.shape
    layout = (parts, shards, 5, own)
    tail = shards * 5 * own
    piece = source_ref.shape[0] // parts
    whole_weight(wk_ref, wk)
    whole_weight(wv_ref, wv)
    for t in range(width // TILE):
        span = slice(t * TILE, (t + 1) * TILE)
        value = (nt(dckv_ref[0], wk[span, :]) + nt(dckv_ref[1], wv[span, :])).astype(BF)
        for c in range(parts):
            g_ref[c, tail : tail + piece, span] = value[c * piece : (c + 1) * piece]

    def product(which, lhs, right):
        def tile(t, _):
            cols = line_tile(t)
            store_rows(g_ref, layout, which, cols, nn(lhs[...], right(cols)).astype(BF))
            return 0

        lax.fori_loop(0, width // TILE, tile, 0)

    left[...] = jnp.transpose(ob_ref[...], (1, 0))
    product(0, left, lambda cols: dx1_ref[:, cols].astype(BF))
    x1 = x1_ref[...]
    left[...] = jnp.transpose((x1 * inverse_rms(x1) * gain_ref[...]).astype(BF), (1, 0))
    product(1, left, lambda cols: dcq_ref[:, cols])
    left[...] = jnp.transpose(cob_ref[...], (1, 0))
    product(2, left, lambda cols: dx2_ref[:, cols].astype(BF))
    left_source[...] = jnp.transpose(source_ref[...], (1, 0))
    product(3, left_source, lambda cols: dckv_ref[0, :, cols])
    product(4, left_source, lambda cols: dckv_ref[1, :, cols])


def middle_grads(dx2, x1, gain, cob, dcq, dckv, source, ob, dx1, packed):
    rows, width = dx2.shape
    count = source.shape[0]
    parts, shards, _, own, _ = packed.shape
    tokens = whole((rows, width))
    shape = (parts, shards * 5 * own + count // parts, width)
    return pl.pallas_call(
        middle_grad_kernel,
        grid=(1,),
        out_shape=jax.ShapeDtypeStruct(shape, BF),
        in_specs=[
            tokens, tokens, whole((1, width)), tokens, tokens, whole(dckv.shape), whole((count, width)), tokens, tokens,
            packed_spec(packed, 3), packed_spec(packed, 4),
        ],
        out_specs=whole(shape),
        scratch_shapes=[
            pltpu.VMEM((width, width), BF), pltpu.VMEM((width, width), BF),
            pltpu.VMEM((width, rows), BF), pltpu.VMEM((width, count), BF),
        ],
        compiler_params=params(),
        cost_estimate=cost(46 * rows * width * width, 24 * rows * width),
        name="middle_grads",
    )(dx2, x1, gain, cob, dcq, dckv, source, ob, dx1, packed, packed)


def final_kernel(d_ref, w_ref, states_ref, gain_ref, dx1_ref, out_ref):
    dn = None
    for s in range(d_ref.shape[0]):
        part = nt(d_ref[s], w_ref[s])
        dn = part if dn is None else dn + part
    dv, _ = norm_back(states_ref[...].astype(F32), gain_ref[...], dn)
    out_ref[...] = dx1_ref[...] + dv


def final_back(dqkv, weights, states, gain, dx1, tile=128):
    parts, rows, inner = dqkv.shape
    width = states.shape[1]
    return pl.pallas_call(
        final_kernel,
        grid=(rows // tile,),
        out_shape=jax.ShapeDtypeStruct((rows, width), F32),
        in_specs=[
            pl.BlockSpec((parts, tile, inner), lambda i: (0, i, 0)),
            whole(weights.shape),
            pl.BlockSpec((tile, width), lambda i: (i, 0)),
            whole((1, width)),
            pl.BlockSpec((tile, width), lambda i: (i, 0)),
        ],
        out_specs=pl.BlockSpec((tile, width), lambda i: (i, 0)),
        compiler_params=params(),
        cost_estimate=cost(6 * rows * width * width, 12 * rows * width),
        name="final_back",
    )(dqkv, weights, states, gain, dx1)


def first_kernel(states_ref, gain_ref, w_ref, out_ref):
    x = states_ref[0].astype(F32)
    n = (x * inverse_rms(x) * gain_ref[...]).astype(BF)
    out_ref[...] = nn(n, w_ref[...]).astype(BF)


def first_projection(gathered, gain, weight, rows):
    parts, _, width = gathered.shape
    cols = weight.shape[1]
    return pl.pallas_call(
        first_kernel,
        grid=(parts,),
        out_shape=jax.ShapeDtypeStruct((parts * rows, cols), BF),
        in_specs=[
            pl.BlockSpec((1, rows, width), lambda i: (i, 0, 0)), whole((1, width)), whole((width, cols)),
        ],
        out_specs=pl.BlockSpec((rows, cols), lambda i: (i, 0)),
        compiler_params=params(),
        cost_estimate=cost(2 * parts * rows * width * cols, 2 * parts * rows * (width + cols)),
        name="first_projection",
    )(gathered, gain, weight)


def last_kernel(states_ref, gain_ref, w_ref, d_ref, gw_ref, gain_out_ref, acc_ref):
    step = pl.program_id(0)
    x = states_ref[0].astype(F32)
    n = (x * inverse_rms(x) * gain_ref[...]).astype(BF)
    g = lax.dot_general(n, d_ref[...], (((0,), (0,)), ((), ())), preferred_element_type=F32)

    @pl.when(step == 0)
    def _():
        acc_ref[...] = g

    @pl.when(step > 0)
    def _():
        acc_ref[...] += g

    @pl.when(step == pl.num_programs(0) - 1)
    def _():
        total = acc_ref[...]
        gw_ref[...] = total.astype(BF)
        gain_out_ref[...] = jnp.sum(total * w_ref[...].astype(F32), axis=1, keepdims=True)


def last_projection(gathered, gain, weight, grads, rows):
    parts, _, width = gathered.shape
    cols = weight.shape[1]
    return pl.pallas_call(
        last_kernel,
        grid=(parts,),
        out_shape=(jax.ShapeDtypeStruct((width, cols), BF), jax.ShapeDtypeStruct((width, 1), F32)),
        in_specs=[
            pl.BlockSpec((1, rows, width), lambda i: (i, 0, 0)), whole((1, width)), whole((width, cols)),
            pl.BlockSpec((rows, cols), lambda i: (i, 0)),
        ],
        out_specs=[whole((width, cols)), whole((width, 1))],
        scratch_shapes=[pltpu.VMEM((width, cols), F32)],
        compiler_params=params(),
        cost_estimate=cost(2 * parts * rows * width * cols, 2 * parts * rows * (width + cols)),
        name="last_projection",
    )(gathered, gain, weight, grads)


def unpack_kernel(own, rest_ref, last_ref, *outs):
    parts = rest_ref.shape[0]
    down = outs[5].shape[0] // parts
    rows, inner = outs[0].shape[0], last_ref.shape[2] // 3
    for c in range(parts):
        for i in range(5):
            outs[i][c * own : (c + 1) * own, :] = rest_ref[c, i * own : (i + 1) * own, :].astype(F32)
        half = rest_ref.shape[2] // 2
        for i in range(2):
            start = ((c // 2) * 2 + i) * down
            value = rest_ref[c, 5 * own : 5 * own + down, i * half : (i + 1) * half]
            outs[5][start : start + down, (c % 2) * half : (c % 2 + 1) * half] = value.astype(F32)
        for i in range(3):
            outs[6 + i][:, c * inner : (c + 1) * inner] = last_ref[c, 0:rows, i * inner : (i + 1) * inner].astype(F32)


def unpack(rest, last, own, down_rows):
    parts, _, width = rest.shape
    square = jax.ShapeDtypeStruct((own * parts, width), F32)
    shapes = [square] * 5 + [jax.ShapeDtypeStruct((down_rows, width), F32)] + [square] * 3
    return pl.pallas_call(
        functools.partial(unpack_kernel, own),
        grid=(1,),
        out_shape=shapes,
        in_specs=[whole(rest.shape), whole(last.shape)],
        out_specs=[whole(v.shape) for v in shapes],
        compiler_params=params(),
        cost_estimate=cost(0, 6 * rest.size),
        name="unpack",
    )(rest, last)


CTX = ("plane", "core")


def spread(piece):
    count = lax.axis_size("fsdp")
    return lax.all_to_all(jnp.broadcast_to(piece[None], (count,) + piece.shape), "fsdp", 0, 0, tiled=True)


def collect(parts, *earlier):
    parts = lax.all_to_all(parts, "fsdp", 0, 0, tiled=True)
    if earlier:
        parts = after(parts, *earlier)
    return jnp.sum(parts.astype(F32), axis=0).astype(BF)


def collect_far(parts):
    count, mine = lax.axis_size("fsdp"), lax.axis_index("fsdp")
    if count > 4:
        return collect(parts).astype(F32)
    total = take(parts, mine, 0).astype(F32)
    for step in range(1, count):
        for sign in (1, -1):
            message = take(parts, jnp.clip(mine + sign * step, 0, count - 1), 0)
            pairs = [(i, i + sign * step) for i in range(count) if 0 <= i + sign * step < count]
            total = total + lax.ppermute(message, "fsdp", pairs).astype(F32)
    return total


def nothing(*refs):
    pass


def after(value, *earlier):
    return pl.pallas_call(
        nothing,
        out_shape=jax.ShapeDtypeStruct(value.shape, value.dtype),
        in_specs=[pl.BlockSpec(memory_space=pl.ANY)] * (1 + len(earlier)),
        out_specs=pl.BlockSpec(memory_space=pl.ANY),
        input_output_aliases={0: 0},
        name="after",
    )(value, *earlier)


def own_rows(shard):
    rows = shard.shape[0] // lax.axis_size(CTX)
    return lax.dynamic_slice_in_dim(shard, lax.axis_index(CTX) * rows, rows, 0)


def swap(value, axis):
    return lax.ppermute(value, axis, [(0, 1), (1, 0)])


def take(value, index, axis):
    return lax.dynamic_index_in_dim(value, index, axis, keepdims=False)


def gather_down(shard):
    rows, width = shard.shape
    start = lax.axis_index("core") * (width // 2)
    mine = spread(lax.dynamic_slice_in_dim(shard, start, width // 2, 1)).reshape(-1, width // 2)
    return mine, swap(mine, "core")


def reduce_planes(half):
    planes, width = lax.axis_size("plane"), half.shape[1]
    if planes != 4:
        return lax.psum_scatter(half, "plane", scatter_dimension=0, tiled=True)
    plane = lax.axis_index("plane")
    for bit, size in ((1, 2), (2, 1)):
        side = (plane // bit) % 2
        split = half.reshape(size, 2, -1, width)
        got = lax.ppermute(take(split, 1 - side, 1), "plane", [(i, i ^ bit) for i in range(4)])
        half = (take(split, side, 1).astype(F32) + got.astype(F32)).astype(BF)
    return half.reshape(-1, width)


def on_device(
    states, positions, segments, encoded, cotangent,
    self_gain, self_query, self_key, self_value, self_output, bias_table,
    cross_gain, cross_query, cross_key, cross_value, cross_output,
    feed_gain, gate_weight, up_weight, down_weight,
):
    parts, shards = lax.axis_size(CTX), lax.axis_size("fsdp")
    place = lax.axis_index(CTX)
    local, width = states.shape[1:]
    head_count = bias_table.shape[1]
    size = width // head_count
    heads = head_count // parts
    inner = heads * size
    blocks = local // BLK
    shard_width = self_gain.shape[0]
    hidden_width = gate_weight.shape[1]
    own = shard_width // parts
    aligned = own % 16 == 0

    def arranged(pieces):
        if aligned:
            return pieces
        matrices, columns = pieces.shape[2], pieces.shape[4]
        return pieces.transpose(2, 1, 0, 3, 4).reshape(1, 1, matrices, width, columns)

    def scattered(grads):
        if aligned:
            return grads
        matrices, columns = grads.shape[2], grads.shape[4]
        return grads.reshape(matrices, shards, parts, own, columns).transpose(2, 1, 0, 3, 4)

    gathered = lax.all_gather(jnp.concatenate([states[0], encoded[0]], axis=0), CTX, axis=0, tiled=False)
    encoded_all = gathered[:, local:].reshape(-1, width)
    columns = lax.dynamic_slice_in_dim(
        jnp.stack([self_query, self_key, self_value], axis=1), place * inner, inner, 2
    ).reshape(shard_width, 3 * inner)
    small = jnp.concatenate([self_gain, cross_gain, feed_gain, bias_table.reshape(-1)])
    small_width = small.shape[0]
    small = jnp.pad(small, (0, 16 * 3 * inner - small_width)).reshape(16, 3 * inner)
    line = spread(jnp.concatenate([columns, small], axis=0))
    qkv_weight = line[:, :shard_width].reshape(width, 3 * inner)
    small = line[:, shard_width:].reshape(shards, -1)[:, :small_width].astype(F32)
    gains = [small[:, i * shard_width : (i + 1) * shard_width].reshape(1, width) for i in range(3)]
    table = small[:, 3 * shard_width :].reshape(BUCKETS, head_count)
    own_table = lax.dynamic_slice_in_dim(table, place * heads, heads, 1).reshape(-1)
    first_pos, first_seg = positions[0, ::BLK], segments[0, ::BLK]
    canon = jnp.where(
        first_seg == 0,
        first_pos // BLK,
        PROMPT // BLK + (first_seg - 1) * (CLEN // BLK) + (first_pos - PROMPT) // BLK,
    )
    canon_all = lax.all_gather(canon, CTX, axis=0, tiled=True)
    slots = jnp.argmax(canon_all[None, :] == jnp.arange(blocks * parts)[:, None], axis=1).astype(jnp.int32)

    squares = jnp.stack([own_rows(w) for w in (self_output, cross_query, cross_output, cross_key, cross_value)], axis=0)
    squares = spread(after(squares, line, slots))
    wide = spread(after(jnp.stack([own_rows(gate_weight), own_rows(up_weight)], axis=0), squares))
    squares = lax.all_gather(squares, CTX, axis=0, tiled=False)

    prompt_tiles = PROMPT // TILE
    qkv = first_projection(gathered, gains[0], qkv_weight, local).reshape(parts * blocks, BLK, 3 * inner)
    o, ot, lse = sa_fwd(slots, own_table, qkv, heads, prompt_tiles)
    o = lax.all_to_all(o.reshape(parts, local, inner), CTX, 0, 0, tiled=True)

    wide = lax.all_gather(after(wide, o), CTX, axis=0, tiled=False)
    squares, wide = arranged(squares), arranged(wide)
    down, other_down = gather_down(after(down_weight, o))
    ckv = source_projection(encoded_all, squares)
    ob, x1, cq, cob, cot, cross_lse, x2, n3 = middle_forward(
        o, states[0], gains[1], gains[2], squares, ckv, head_count
    )
    qkv_all = lax.all_gather(after(qkv_weight, x2), CTX, axis=0, tiled=False)
    layer_out, dx2, feed_gain_part, g_wide, g_down, g_other = feed_forward(
        lax.axis_index("core").astype(jnp.int32).reshape(1), n3, cotangent[0], x2, gains[2], wide, down, other_down
    )
    g_wide = lax.psum_scatter(scattered(g_wide), CTX, scatter_dimension=0, tiled=False)
    g_down = (g_down.astype(F32) + swap(g_other, "core").astype(F32)).astype(BF).reshape(shards, -1, width // 2)
    dx1, cross_gain_part, dcq, dckv, dso = middle_back(
        after(dx2, qkv_all), x1, gains[1], squares, cq, ckv, cot, cross_lse, head_count, parts
    )
    dso = lax.all_to_all(dso, CTX, 0, 0, tiled=True).reshape(parts * blocks, BLK, inner)
    g_squares = middle_grads(dx2, x1, gains[1], cob, dcq, dckv, encoded_all, ob, dx1, squares)
    if not aligned:
        encoded_part = g_squares[0, 5 * width :].reshape(parts, -1, width)
        g_squares = scattered(g_squares[0, : 5 * width].reshape(1, 1, 5, width, width)).reshape(parts, -1, width)
        g_squares = jnp.concatenate([g_squares, encoded_part], axis=1)
    middle = prompt_tiles + (blocks * parts * BLK // TILE - prompt_tiles) // 4
    held = sa_bwd(slots, own_table, qkv, after(dso, g_down, g_squares), ot, lse, heads, prompt_tiles, 0, middle)
    g_squares = lax.psum_scatter(g_squares, CTX, scatter_dimension=0, tiled=False)
    g_down = collect(after(g_down, dso), held[0])
    dqkv, dtable = sa_bwd(
        slots, own_table, qkv, after(dso, g_wide), ot, lse, heads, prompt_tiles, middle,
        blocks * parts * BLK // TILE, held,
    )
    g_wide = collect(after(g_wide, g_down), dqkv)
    g_squares = after(g_squares, g_wide)
    g_squares_sum = collect(g_squares[: shards * 5 * own].reshape(shards, 5 * own, width))
    dqkv_local = lax.all_to_all(after(dqkv, g_squares_sum).reshape(parts, local, 3 * inner), CTX, 0, 0, tiled=True)
    states_grad = final_back(dqkv_local, qkv_all, states[0], gains[0], dx1)
    g_wide = lax.all_gather(g_wide, CTX, axis=0, tiled=False)
    grads = dqkv.reshape(parts * local, 3 * inner)
    g_qkv, self_gain_part = last_projection(gathered, gains[0], qkv_weight, grads, local)
    g_down = reduce_planes(g_down)
    encoded_grad = g_squares[shards * 5 * own :].astype(F32)
    table_part = jnp.zeros((BUCKETS, head_count), F32)
    table_part = lax.dynamic_update_slice_in_dim(table_part, dtable[:, :, 0].T, place * heads, 1)
    sums = [self_gain_part[:, 0] / gains[0][0], cross_gain_part[0], feed_gain_part[0]]
    sums = jnp.concatenate([v.reshape(shards, shard_width) for v in sums] + [table_part.reshape(shards, -1)], axis=1)
    sums = jnp.pad(sums, ((0, 0), (0, 16 * 3 * inner - small_width))).reshape(shards, 16, 3 * inner).astype(BF)
    last = jnp.concatenate([g_qkv.reshape(shards, shard_width, 3 * inner), sums], axis=1)
    last = collect_far(last).astype(BF)
    g_down = jnp.concatenate([g_down[: g_down.shape[0] // 2], g_down[g_down.shape[0] // 2 :]], axis=1)
    rest = jnp.concatenate([g_squares_sum, g_down], axis=0)
    rest = lax.all_gather(after(rest, g_wide), CTX, axis=0, tiled=False)
    last = lax.all_gather(after(last, rest, dqkv_local), CTX, axis=0, tiled=False)
    sums = jnp.sum(last[:, shard_width:].reshape(parts, -1)[:, :small_width].astype(F32), axis=0)
    gain_grads = [sums[i * shard_width : (i + 1) * shard_width] for i in range(3)]
    table_grad = sums[3 * shard_width :].reshape(-1, head_count)
    g_wide = g_wide.astype(F32).transpose(1, 0, 2, 3).reshape(2, shard_width, hidden_width)
    if aligned:
        *g_squares, g_down, g_query, g_key, g_value = unpack(rest, last, own, down_weight.shape[0])
    else:
        rest = rest.astype(F32)
        g_squares = rest[:, : 5 * own].reshape(parts, 5, own, width).transpose(1, 0, 2, 3).reshape(5, shard_width, width)
        g_down = rest[:, 5 * own :].reshape(parts // 2, 2, -1, 2, width // 2).transpose(0, 3, 2, 1, 4).reshape(-1, width)
        g_qkv = last[:, :shard_width].astype(F32).reshape(parts, shard_width, 3, inner).transpose(2, 1, 0, 3)
        g_query, g_key, g_value = g_qkv.reshape(3, shard_width, width)
    return (
        layer_out[None], states_grad[None], encoded_grad[None],
        gain_grads[0], g_query, g_key, g_value, g_squares[0], table_grad,
        gain_grads[1], g_squares[1], g_squares[3], g_squares[4], g_squares[2],
        gain_grads[2], g_wide[0], g_wide[1], g_down,
    )


def solution(mesh):
    ctx, fsdp = mesh.devices.shape
    split = Mesh(mesh.devices.reshape(ctx // 2, 2, fsdp), ("plane", "core", "fsdp"))
    tokens, matrix, vector = P("fsdp", CTX, None), P("fsdp", None), P("fsdp")
    place = P("fsdp", CTX)
    return jax.shard_map(
        on_device,
        mesh=split,
        in_specs=(tokens, place, place, tokens, tokens)
        + (vector, matrix, matrix, matrix, matrix, matrix)
        + (vector, matrix, matrix, matrix, matrix)
        + (vector, matrix, matrix, matrix),
        out_specs=(tokens, tokens, tokens)
        + (vector, matrix, matrix, matrix, matrix, matrix)
        + (vector, matrix, matrix, matrix, matrix)
        + (vector, matrix, matrix, matrix),
        check_vma=False,
    )
```

```python
import functools
import math

import jax
import jax.numpy as jnp
from jax import lax
from jax.experimental import pallas as pl
from jax.experimental.pallas import tpu as pltpu
from jax.sharding import Mesh
from jax.sharding import PartitionSpec as P

BUCKETS = 32
DISTANCE = 128
PROMPT = 2048
CLEN = 256
BLK = 128
TILE = 256
NEG = -1e30
F32 = jnp.float32
BF = jnp.bfloat16
epsilon = 1e-06
gelu_scale = math.sqrt(2.0 / math.pi)
VMEM_LIMIT = 56 * 1024 * 1024


def bucket_starts():
    half=BUCKETS//2
    edges=[math.ceil(half*(DISTANCE/half)**(e/half)) for e in range(1,half)]
    return list(range(half+1))+edges

def nt(a,b):
    return lax.dot_general(a,b,(((1,),(1,)),((),())),preferred_element_type=F32)
def nn(a,b):
    return lax.dot_general(a,b,(((1,),(0,)),((),())),preferred_element_type=F32)

def leaving_out(kernel,count):
    return lambda *refs: kernel(*refs[count:])

def unread(operands):
    return [pl.BlockSpec(memory_space=pl.ANY)]*len(operands)

def head_mask(value,head,heads):
    if heads==1: return value
    size=value.shape[-1]//heads
    lane=lax.broadcasted_iota(jnp.int32,value.shape,1)
    return jnp.where((lane>=head*size)&(lane<(head+1)*size),value,jnp.zeros_like(value))

def build_bias(tab_ref,bias_ref,heads):
    starts=bucket_starts()
    key=lax.broadcasted_iota(jnp.int32,(BLK,BLK),0)
    query=lax.broadcasted_iota(jnp.int32,(BLK,BLK),1)
    for h in range(heads):
        last=tab_ref[(BUCKETS-1)*heads+h]
        for sub in (0,1):
            dist=query-key+BLK*sub
            val=jnp.full((BLK,BLK),tab_ref[h]-last,F32)
            for b in range(1,BUCKETS):
                val=jnp.where(dist>=starts[b],tab_ref[b*heads+h]-last,val)
            if sub==0:
                val=jnp.where(dist>=0,val,NEG)
                bias_ref[h,0:BLK,0:BLK]=val
                bias_ref[h,BLK:,BLK:]=val
            else:
                bias_ref[h,0:BLK,BLK:]=val
        bias_ref[h,BLK:,0:BLK]=jnp.full((BLK,BLK),NEG,F32)

def load_tile(src,slots,tile,lo,hi):
    a=src[slots[2*tile],:,lo:hi]
    b=src[slots[2*tile+1],:,lo:hi]
    return jnp.concatenate([a,b],axis=0)

def fwd_kernel(heads,prompt_tiles,slots,tab,qkv,o_ref,ot_ref,lse_ref,bias,kc,vt,qm,s_scr):
    tiles=kc.shape[0]//TILE
    width=kc.shape[1]
    size=width//heads
    build_bias(tab,bias,heads)
    def arrange(t,_):
        rows=pl.ds(pl.multiple_of(t*TILE,TILE),TILE)
        kc[rows,:]=load_tile(qkv,slots,t,width,2*width)
        vt[t]=jnp.transpose(load_tile(qkv,slots,t,2*width,3*width),(1,0))
        return 0
    lax.fori_loop(0,tiles,arrange,0)

    def scores(t_rows,h,kind,qh):
        s=nt(kc[t_rows,:],qh)
        if kind=="own":
            s=s+bias[h]
        elif kind=="prev":
            top=s[:BLK]
            low=jnp.concatenate([s[BLK:,:BLK]+bias[h,0:BLK,BLK:],s[BLK:,BLK:]],axis=1)
            s=jnp.concatenate([top,low],axis=0)
        return s

    def tile_body(t,n_far,own_static):
        q=load_tile(qkv,slots,t,0,width)
        outs=[]
        for h in range(heads):
            qh=head_mask(q,h,heads)
            m=None
            for j in range(n_far+1):
                if j<n_far:
                    rows=pl.ds(j*TILE,TILE); kind="prev" if j==n_far-1 else "far"
                else:
                    rows=pl.ds(pl.multiple_of(t*TILE,TILE),TILE) if not own_static else pl.ds(t*TILE,TILE); kind="own"
                s=scores(rows,h,kind,qh)
                s_scr[h,j]=s
                part=jnp.max(s.reshape(TILE//8,8,TILE),axis=0)
                m=part if m is None else jnp.maximum(m,part)
            m=jnp.max(m,axis=0,keepdims=True)
            l=None; acc=None
            for j in range(n_far+1):
                p=jnp.exp(s_scr[h,j]-m)
                part=jnp.sum(p.reshape(TILE//8,8,TILE),axis=0)
                l=part if l is None else l+part
                vrow=j if j<n_far else t
                a=nn(vt[vrow,h*size:(h+1)*size,:],p.astype(BF))
                acc=a if acc is None else acc+a
            l=jnp.sum(l,axis=0,keepdims=True)
            o=acc*(1.0/l)
            cols=pl.ds(t*TILE if own_static else pl.multiple_of(t*TILE,TILE),TILE)
            ot_ref[h*size:(h+1)*size,cols]=o
            lse_ref[h:h+1,cols]=m+jnp.log(l)
            outs.append(o)
        o=jnp.concatenate(outs,axis=0) if heads>1 else outs[0]
        o=jnp.transpose(o,(1,0)).astype(BF)
        o_ref[slots[2*t]]=o[:BLK]
        o_ref[slots[2*t+1]]=o[BLK:]
    for t in range(prompt_tiles):
        tile_body(t,t,True)
    def cont(c,_):
        tile_body(c,prompt_tiles,False)
        return 0
    lax.fori_loop(prompt_tiles,tiles,cont,0)

def sa_fwd(slots,tab,qkv,heads,prompt_tiles):
    nb,_,w3=qkv.shape; w=w3//3; n=nb*BLK; tiles=n//TILE
    return pl.pallas_call(
        functools.partial(fwd_kernel,heads,prompt_tiles),
        out_shape=(jax.ShapeDtypeStruct((nb,BLK,w),BF),jax.ShapeDtypeStruct((w,n),F32),jax.ShapeDtypeStruct((heads,n),F32)),
        in_specs=[pl.BlockSpec(memory_space=pltpu.SMEM),pl.BlockSpec(memory_space=pltpu.SMEM),pl.BlockSpec(memory_space=pltpu.VMEM)],
        out_specs=[pl.BlockSpec(memory_space=pltpu.VMEM)]*3,
        scratch_shapes=[pltpu.VMEM((heads,TILE,TILE),F32),pltpu.VMEM((n,w),BF),pltpu.VMEM((tiles,w,TILE),BF),pltpu.VMEM((8,128),F32),pltpu.VMEM((heads,prompt_tiles+1,TILE,TILE),F32)],
        compiler_params=pltpu.CompilerParams(vmem_limit_bytes=VMEM_LIMIT),
        cost_estimate=cost(32 * 10**9, 8 * n * w3),
        name="self_attention_forward",
    )(slots,tab,qkv)

def bwd_kernel(heads,prompt_tiles,low,high,slots,tab,qkv,do_ref,ot_ref,lse_ref,*refs):
    if low:
        dq_in,dkv_in,near_in,far_in,dqkv_ref,dtab_ref,bias,kc,vc,kt,dqt,dkv,near,far=refs
    else:
        dq_out,dkv,near,far,bias,kc,vc,kt,dqt=refs
    tiles=kc.shape[0]//TILE
    width=kc.shape[1]
    size=width//heads
    build_bias(tab,bias,heads)
    for mine,start in ((near,near_in if low else None),(far,far_in if low else None),(dkv,dkv_in if low else None)):
        mine[...]=start[...] if low else jnp.zeros_like(mine)
    def arrange(t,_):
        rows=pl.ds(pl.multiple_of(t*TILE,TILE),TILE)
        k=load_tile(qkv,slots,t,width,2*width)
        kc[rows,:]=k
        kt[t]=jnp.transpose(k,(1,0))
        vc[rows,:]=load_tile(qkv,slots,t,2*width,3*width)
        return 0
    lax.fori_loop(0,tiles,arrange,0)

    def query_tile(t,_):
        cols=pl.ds(pl.multiple_of(t*TILE,TILE),TILE)
        q=load_tile(qkv,slots,t,0,width)
        do=load_tile(do_ref,slots,t,0,width)
        dot=jnp.transpose(do.astype(F32),(1,0))*ot_ref[:,cols]
        qh=[head_mask(q,h,heads) for h in range(heads)]
        doh=[head_mask(do,h,heads) for h in range(heads)]
        lse=[lse_ref[h:h+1,cols] for h in range(heads)]
        delta=[jnp.sum(dot[h*size:(h+1)*size],axis=0,keepdims=True) for h in range(heads)]
        dqt[...]=jnp.zeros_like(dqt)

        def group(*pieces):
            spans=[pl.ds(pl.multiple_of(j*TILE,TILE),TILE) for j,_ in pieces]
            keys=[kc[rows,:] for rows in spans]
            values=[vc[rows,:] for rows in spans]
            turned=[kt[j] for j,_ in pieces]
            dk=[None]*len(pieces); dv=[None]*len(pieces)
            dq_parts=[]; far_parts=[]
            for h in range(heads):
                dq=None; sums=None
                for i,(j,kind) in enumerate(pieces):
                    s=nt(keys[i],qh[h])
                    if kind=="own":
                        s=s+bias[h]
                    elif kind=="prev":
                        lower=jnp.concatenate([s[BLK:,:BLK]+bias[h,0:BLK,BLK:],s[BLK:,BLK:]],axis=1)
                        s=jnp.concatenate([s[:BLK],lower],axis=0)
                    p=jnp.exp(s-lse[h])
                    ds=p*(nt(values[i],doh[h])-delta[h])
                    if kind=="own":
                        near[h,0]+=ds[:BLK,:BLK]+ds[BLK:,BLK:]
                        near[h,1]+=ds[:BLK,BLK:]
                    else:
                        if kind=="prev":
                            near[h,1]+=ds[BLK:,:BLK]
                            rest=jnp.concatenate([jnp.zeros((BLK,BLK),F32),ds[BLK:,BLK:]],axis=1)
                            part=jnp.sum((ds[:BLK]+rest).reshape(BLK//8,8,TILE),axis=0)
                        else:
                            part=jnp.sum(ds.reshape(TILE//8,8,TILE),axis=0)
                        sums=part if sums is None else sums+part
                    pb=p.astype(BF); db=ds.astype(BF)
                    a=nn(pb,doh[h]); dv[i]=a if dv[i] is None else dv[i]+a
                    b=nn(db,qh[h]); dk[i]=b if dk[i] is None else dk[i]+b
                    c=nn(turned[i][h*size:(h+1)*size,:],db); dq=c if dq is None else dq+c
                dq_parts.append(dq); far_parts.append(sums)
            for h in range(heads):
                dqt[h*size:(h+1)*size,:]+=dq_parts[h]
                if far_parts[h] is not None:
                    far[h]+=far_parts[h]
            for i,rows in enumerate(spans):
                dkv[rows,0:width]+=dk[i]
                dkv[rows,width:2*width]+=dv[i]
        count=jnp.minimum(t,prompt_tiles)
        pairs=jnp.maximum(count-1,0)//2
        def far_pair(i,_):
            group((2*i,"far"),(2*i+1,"far"))
            return 0
        lax.fori_loop(0,pairs,far_pair,0)
        left=count-2*pairs
        @pl.when(left==0)
        def _():
            group((t,"own"))
        @pl.when(left==1)
        def _():
            group((count-1,"prev"),(t,"own"))
        @pl.when(left==2)
        def _():
            group((count-2,"far"),(count-1,"prev"),(t,"own"))
        dq=jnp.transpose(dqt[...],(1,0)).astype(BF)
        if low:
            dqkv_ref[slots[2*t],:,0:width]=dq[:BLK]
            dqkv_ref[slots[2*t+1],:,0:width]=dq[BLK:]
        else:
            dq_out[cols,:]=dq
        return 0
    lax.fori_loop(low,high,query_tile,0)
    if not low:
        return
    def bring(t,_):
        dq=dq_in[pl.ds(pl.multiple_of(t*TILE,TILE),TILE),:]
        dqkv_ref[slots[2*t],:,0:width]=dq[:BLK]
        dqkv_ref[slots[2*t+1],:,0:width]=dq[BLK:]
        return 0
    lax.fori_loop(0,low,bring,0)
    def finish(t,_):
        g=dkv[pl.ds(pl.multiple_of(t*TILE,TILE),TILE),:].astype(BF)
        dqkv_ref[slots[2*t],:,width:3*width]=g[:BLK]
        dqkv_ref[slots[2*t+1],:,width:3*width]=g[BLK:]
        return 0
    lax.fori_loop(0,tiles,finish,0)
    starts=bucket_starts()
    key=lax.broadcasted_iota(jnp.int32,(BLK,BLK),0)
    query=lax.broadcasted_iota(jnp.int32,(BLK,BLK),1)
    for h in range(heads):
        for b in range(BUCKETS):
            total=jnp.zeros((8,BLK),F32)
            for sub in (0,1):
                dist=query-key+BLK*sub
                inside=dist>=starts[b]
                if b<BUCKETS-1: inside=inside&(dist<starts[b+1])
                total=total+jnp.sum(jnp.where(inside,near[h,sub],0.0).reshape(BLK//8,8,BLK),axis=0)
            if b==BUCKETS-1:
                total=total+far[h,:,0:BLK]+far[h,:,BLK:]
            row=jnp.sum(total,axis=0,keepdims=True)
            dtab_ref[h,b:b+1,:]=jnp.broadcast_to(jnp.sum(row,axis=1,keepdims=True),(1,BLK))

def sa_bwd(earlier,slots,tab,qkv,do,ot,lse,heads,prompt_tiles,low,high,held=()):
    nb,_,w3=qkv.shape; w=w3//3; n=nb*BLK; tiles=n//TILE
    shape=jax.ShapeDtypeStruct
    sums=[shape((n,2*w),F32),shape((heads,2,BLK,BLK),F32),shape((heads,8,TILE),F32)]
    if low:
        out=[shape((nb,BLK,w3),BF),shape((heads,BUCKETS,BLK),F32)]
    else:
        out=[shape((high*TILE,w),BF)]+sums
    scratch=[pltpu.VMEM((heads,TILE,TILE),F32),pltpu.VMEM((n,w),BF),pltpu.VMEM((n,w),BF),pltpu.VMEM((tiles,w,TILE),BF),pltpu.VMEM((w,TILE),F32)]
    if low:
        scratch+=[pltpu.VMEM(v.shape,F32) for v in sums]
    return pl.pallas_call(
        leaving_out(functools.partial(bwd_kernel,heads,prompt_tiles,low,high),len(earlier)),
        out_shape=out,
        in_specs=unread(earlier)+[pl.BlockSpec(memory_space=pltpu.SMEM)]*2+[pl.BlockSpec(memory_space=pltpu.VMEM)]*(4+len(held)),
        out_specs=[pl.BlockSpec(memory_space=pltpu.VMEM)]*len(out),
        scratch_shapes=scratch,
        compiler_params=pltpu.CompilerParams(vmem_limit_bytes=VMEM_LIMIT),
        cost_estimate=cost((250 if low else 43) * 10**9, 12 * n * w3),
        name="self_attention_backward",
    )(*earlier,slots,tab,qkv,do,ot,lse,*held)


def line_tile(step, size=TILE):
    return pl.ds(pl.multiple_of(step * size, size), size)


def whole_weight(ref, scratch):
    parts, shards, _, rows, _ = ref.shape
    for z in range(shards):
        for c in range(parts):
            start = (z * parts + c) * rows
            scratch[start : start + rows, :] = ref[c, z, 0]


def store_rows(ref, layout, which, cols, value):
    parts, shards, matrices, rows = layout
    for z in range(shards):
        place = (z * matrices + which) * rows
        for c in range(parts):
            start = (z * parts + c) * rows
            ref[c, place : place + rows, cols] = value[start : start + rows]


def store_grad(ref, which, cols, value):
    parts, shards, _, rows, _ = ref.shape
    for z in range(shards):
        for c in range(parts):
            start = (z * parts + c) * rows
            ref[c, z, which, :, cols] = value[start : start + rows]


def inverse_rms(v):
    return lax.rsqrt(jnp.mean(v * v, axis=-1, keepdims=True) + epsilon)


def norm_back(v, gain, dn):
    r = inverse_rms(v)
    weighted = dn * gain
    dv = r * weighted - v * (r * r * r) * jnp.mean(weighted * v, axis=-1, keepdims=True)
    return dv, jnp.sum(dn * v * r, axis=0, keepdims=True)


def whole(shape, index=None):
    zeros = (0,) * len(shape)
    return pl.BlockSpec(shape, lambda *_: zeros if index is None else index)


def packed_spec(packed, which):
    parts, shards, _, rows, width = packed.shape
    return pl.BlockSpec((parts, shards, 1, rows, width), lambda *_: (0, 0, which, 0, 0))


def params():
    return pltpu.CompilerParams(vmem_limit_bytes=VMEM_LIMIT)


def cost(flops, size):
    return pl.CostEstimate(flops=flops, bytes_accessed=size, transcendentals=0)


def source_kernel(source_ref, w_ref, out_ref, weight):
    whole_weight(w_ref, weight)
    source = source_ref[...]
    for t in range(out_ref.shape[-1] // TILE):
        cols = slice(t * TILE, (t + 1) * TILE)
        out_ref[0, :, cols] = nn(source, weight[:, cols]).astype(BF)


def source_projection(source, packed):
    rows, width = source.shape
    parts, shards, _, own, _ = packed.shape
    return pl.pallas_call(
        source_kernel,
        grid=(2,),
        out_shape=jax.ShapeDtypeStruct((2, rows, width), BF),
        in_specs=[
            whole((rows, width)),
            pl.BlockSpec((parts, shards, 1, own, width), lambda i: (0, 0, 3 + i, 0, 0)),
        ],
        out_specs=pl.BlockSpec((1, rows, width), lambda i: (i, 0, 0)),
        scratch_shapes=[pltpu.VMEM((width, width), BF)],
        compiler_params=params(),
        cost_estimate=cost(4 * rows * width * width, 8 * width * width),
        name="source_projection",
    )(source, packed)


def middle_kernel(
    head_count, o_ref, states_ref, gain_two, gain_three, wo_ref, wq_ref, wc_ref, ckv_ref,
    ob_ref, x1_ref, cq_ref, cob_ref, cot_ref, lse_ref, x2_ref, n3_ref, weight, cvt,
):
    rows, width = states_ref.shape
    size = width // head_count
    pair = 2 * size
    for s in range(o_ref.shape[0]):
        inner = o_ref.shape[2]
        ob_ref[:, s * inner : (s + 1) * inner] = o_ref[s]
    whole_weight(wo_ref, weight)

    def add_out(t, _):
        cols = line_tile(t)
        x1_ref[:, cols] = states_ref[:, cols].astype(F32) + nn(ob_ref[...], weight[:, cols])
        return 0

    lax.fori_loop(0, width // TILE, add_out, 0)
    x1 = x1_ref[...]
    n3_ref[...] = (x1 * inverse_rms(x1) * gain_two[...]).astype(BF)
    whole_weight(wq_ref, weight)

    def make_query(t, _):
        cols = line_tile(t)
        cq_ref[:, cols] = nn(n3_ref[...], weight[:, cols]).astype(BF)
        return 0

    lax.fori_loop(0, width // TILE, make_query, 0)

    def attend(p, _):
        cols = line_tile(p, pair)
        keys = ckv_ref[0, :, cols]
        cvt[...] = jnp.transpose(ckv_ref[1, :, cols], (1, 0))
        count = keys.shape[0]
        for half in range(rows // TILE):
            span = slice(half * TILE, (half + 1) * TILE)
            q = cq_ref[span, cols]
            outs = []
            for h in range(2):
                s = nt(keys, head_mask(q, h, 2))
                m = jnp.max(jnp.max(s.reshape(count // 8, 8, TILE), axis=0), axis=0, keepdims=True)
                e = jnp.exp(s - m)
                total = jnp.sum(jnp.sum(e.reshape(count // 8, 8, TILE), axis=0), axis=0, keepdims=True)
                out = nn(cvt[h * size : (h + 1) * size, :], e.astype(BF)) * (1.0 / total)
                lse_ref[p, h : h + 1, span] = m + jnp.log(total)
                outs.append(out)
            both = jnp.concatenate(outs, axis=0)
            cot_ref[p, :, span] = both
            cob_ref[span, cols] = jnp.transpose(both, (1, 0)).astype(BF)
        return 0

    lax.fori_loop(0, width // pair, attend, 0)
    whole_weight(wc_ref, weight)

    def add_cross(t, _):
        cols = line_tile(t)
        x2_ref[:, cols] = x1_ref[:, cols] + nn(cob_ref[...], weight[:, cols])
        return 0

    lax.fori_loop(0, width // TILE, add_cross, 0)
    x2 = x2_ref[...]
    n3_ref[...] = (x2 * inverse_rms(x2) * gain_three[...]).astype(BF)


def middle_forward(o, states, gain_two, gain_three, packed, ckv, head_count):
    rows, width = states.shape
    size = width // head_count
    pairs = head_count // 2
    tokens = lambda dtype: jax.ShapeDtypeStruct((rows, width), dtype)
    shapes = [
        tokens(BF), tokens(F32), tokens(BF), tokens(BF),
        jax.ShapeDtypeStruct((pairs, 2 * size, rows), F32), jax.ShapeDtypeStruct((pairs, 8, rows), F32),
        tokens(F32), tokens(BF),
    ]
    return pl.pallas_call(
        functools.partial(middle_kernel, head_count),
        grid=(1,),
        out_shape=shapes,
        in_specs=[
            whole(o.shape), whole((rows, width)), whole((1, width)), whole((1, width)),
            packed_spec(packed, 0), packed_spec(packed, 1), packed_spec(packed, 2), whole(ckv.shape),
        ],
        out_specs=[whole(s.shape) for s in shapes],
        scratch_shapes=[pltpu.VMEM((width, width), BF), pltpu.VMEM((2 * size, ckv.shape[1]), BF)],
        compiler_params=params(),
        cost_estimate=cost(60 * rows * width * width, 24 * rows * width),
        name="middle_forward",
    )(o, states, gain_two, gain_three, packed, packed, packed, ckv)


def feed_kernel(
    core_ref, n3_ref, cot_ref, x2_ref, gain_ref, w_ref, mine_ref, other_ref,
    hidden_ref, dx2_ref, gain_out_ref, gw_ref, keep_ref, give_ref, n3t, wg, wu, dgate, dup, down,
):
    step = pl.program_id(0)
    half = mine_ref.shape[1]
    own_half = pl.ds(pl.multiple_of(core_ref[0] * half, half), half)
    other_half = pl.ds(pl.multiple_of((1 - core_ref[0]) * half, half), half)
    down[:, own_half] = mine_ref[...]
    down[:, other_half] = other_ref[...]

    @pl.when(step == 0)
    def _():
        n3t[...] = jnp.transpose(n3_ref[...], (1, 0))

    parts, shards, _, rows, _ = w_ref.shape
    for z in range(shards):
        for c in range(parts):
            start = (z * parts + c) * rows
            wg[step, start : start + rows, :] = w_ref[c, z, 0]
            wu[step, start : start + rows, :] = w_ref[c, z, 1]
    n3, cot, wd = n3_ref[...], cot_ref[...], down[...]
    gate, up = nn(n3, wg[step]), nn(n3, wu[step])
    dh = nt(cot, wd)
    t = jnp.tanh(gelu_scale * (gate + 0.044715 * gate * gate * gate))
    gelu = 0.5 * gate * (1.0 + t)
    slope = 0.5 * (1.0 + t) + 0.5 * gate * (1.0 - t * t) * (gelu_scale * (1.0 + 3 * 0.044715 * gate * gate))
    hidden = (gelu * up).astype(BF)
    hidden_ref[...] = hidden
    dgate_low = (dh * up * slope).astype(BF)
    dup_low = (dh * gelu).astype(BF)
    dgate[step] = dgate_low
    dup[step] = dup_low
    down[...] = nn(jnp.transpose(hidden, (1, 0)), cot).astype(BF)
    keep_ref[...] = down[:, own_half]
    give_ref[...] = down[:, other_half]
    everything = slice(None)
    store_grad(gw_ref, 0, everything, nn(n3t[...], dgate_low).astype(BF))
    store_grad(gw_ref, 1, everything, nn(n3t[...], dup_low).astype(BF))

    @pl.when(step == pl.num_programs(0) - 1)
    def _():
        def tile(i, _):
            span = line_tile(i)
            total = None
            for s in range(dgate.shape[0]):
                term = nt(dgate[s], wg[s, span, :]) + nt(dup[s], wu[s, span, :])
                total = term if total is None else total + term
            dx2_ref[:, span] = total
            return 0

        lax.fori_loop(0, dx2_ref.shape[1] // TILE, tile, 0)
        dv, gain_out_ref[...] = norm_back(x2_ref[...], gain_ref[...], dx2_ref[...])
        dx2_ref[...] = cot_ref[...].astype(F32) + dv


def feed_forward(core, n3, cot, x2, gain, wide, mine, other):
    rows, width = n3.shape
    parts, shards, _, own, hidden = wide.shape
    steps = hidden // TILE
    tokens = lambda dtype: jax.ShapeDtypeStruct((rows, width), dtype)
    part = pl.BlockSpec((TILE, width // 2), lambda i: (i, 0))
    piece = pl.BlockSpec((parts, shards, 2, own, TILE), lambda i: (0, 0, 0, 0, i))
    return pl.pallas_call(
        feed_kernel,
        grid=(steps,),
        out_shape=[
            jax.ShapeDtypeStruct((rows, hidden), BF), tokens(F32), jax.ShapeDtypeStruct((1, width), F32),
            jax.ShapeDtypeStruct(wide.shape, BF), jax.ShapeDtypeStruct(mine.shape, BF), jax.ShapeDtypeStruct(mine.shape, BF),
        ],
        in_specs=[
            pl.BlockSpec(memory_space=pltpu.SMEM),
            whole((rows, width)), whole((rows, width)), whole((rows, width)), whole((1, width)), piece, part, part,
        ],
        out_specs=[
            pl.BlockSpec((rows, TILE), lambda i: (0, i)), whole((rows, width)), whole((1, width)),
            piece, part, part,
        ],
        scratch_shapes=[
            pltpu.VMEM((width, rows), BF), pltpu.VMEM((steps, width, TILE), BF), pltpu.VMEM((steps, width, TILE), BF),
            pltpu.VMEM((steps, rows, TILE), BF), pltpu.VMEM((steps, rows, TILE), BF), pltpu.VMEM((TILE, width), BF),
        ],
        compiler_params=params(),
        cost_estimate=cost(28 * rows * width * hidden, 12 * width * hidden),
        name="feed_forward",
    )(core, n3, cot, x2, gain, wide, mine, other)


def output_kernel(core_ref, hidden_ref, x2_ref, mine_ref, other_ref, out_ref):
    half = mine_ref.shape[1]
    own_half = pl.ds(pl.multiple_of(core_ref[0] * half, half), half)
    other_half = pl.ds(pl.multiple_of((1 - core_ref[0]) * half, half), half)
    hidden = hidden_ref[...]
    out_ref[:, own_half] = (x2_ref[:, own_half] + nn(hidden, mine_ref[...])).astype(BF)
    out_ref[:, other_half] = (x2_ref[:, other_half] + nn(hidden, other_ref[...])).astype(BF)


def layer_output(earlier, core, hidden, x2, mine, other, tile=128):
    rows, width = x2.shape
    units = hidden.shape[1]
    return pl.pallas_call(
        leaving_out(output_kernel, len(earlier)),
        grid=(rows // tile,),
        out_shape=jax.ShapeDtypeStruct((rows, width), BF),
        in_specs=unread(earlier) + [
            pl.BlockSpec(memory_space=pltpu.SMEM),
            pl.BlockSpec((tile, units), lambda i: (i, 0)), pl.BlockSpec((tile, width), lambda i: (i, 0)),
            whole(mine.shape), whole(mine.shape),
        ],
        out_specs=pl.BlockSpec((tile, width), lambda i: (i, 0)),
        compiler_params=params(),
        cost_estimate=cost(4 * rows * width * units, 4 * width * units),
        name="layer_output",
    )(*earlier, core, hidden, x2, mine, other)


def middle_back_kernel(
    head_count, dx2_ref, x1_ref, gain_ref, wo_ref, wq_ref, wc_ref, cq_ref, ckv_ref, cot_ref, lse_ref,
    dx1_ref, gain_out_ref, dcq_ref, dckv_ref, dso_ref, weight, dco, ckt, dn,
):
    rows, width = dx2_ref.shape
    size = width // head_count
    pair = 2 * size
    count = ckv_ref.shape[1]
    whole_weight(wc_ref, weight)

    def back_out(t, _):
        dco[:, line_tile(t)] = nt(dx2_ref[...].astype(BF), weight[line_tile(t), :]).astype(BF)
        return 0

    lax.fori_loop(0, width // TILE, back_out, 0)

    def attend(p, _):
        cols = line_tile(p, pair)
        q, do = cq_ref[:, cols], dco[:, cols]
        terms = jnp.transpose(do.astype(F32), (1, 0)) * cot_ref[p]
        ckt[...] = jnp.transpose(ckv_ref[0, :, cols], (1, 0))
        qh = [head_mask(q, h, 2) for h in range(2)]
        doh = [head_mask(do, h, 2) for h in range(2)]
        lse = [lse_ref[p, h : h + 1, :] for h in range(2)]
        delta = [jnp.sum(terms[h * size : (h + 1) * size], axis=0, keepdims=True) for h in range(2)]
        dqt = [None, None]
        for t in range(count // TILE):
            span = slice(t * TILE, (t + 1) * TILE)
            k, v = ckv_ref[0, span, cols], ckv_ref[1, span, cols]
            dk = dv = None
            for h in range(2):
                weights = jnp.exp(nt(k, qh[h]) - lse[h])
                ds = (weights * (nt(v, doh[h]) - delta[h])).astype(BF)
                a, b = nn(weights.astype(BF), doh[h]), nn(ds, qh[h])
                dv = a if dv is None else dv + a
                dk = b if dk is None else dk + b
                c = nn(ckt[h * size : (h + 1) * size, span], ds)
                dqt[h] = c if dqt[h] is None else dqt[h] + c
            dckv_ref[0, span, cols] = dk.astype(BF)
            dckv_ref[1, span, cols] = dv.astype(BF)
        dcq_ref[:, cols] = jnp.transpose(jnp.concatenate(dqt, axis=0), (1, 0)).astype(BF)
        return 0

    lax.fori_loop(0, width // pair, attend, 0)
    whole_weight(wq_ref, weight)

    def back_query(t, _):
        dn[:, line_tile(t)] = nt(dcq_ref[...], weight[line_tile(t), :])
        return 0

    lax.fori_loop(0, width // TILE, back_query, 0)
    dv, gain_out_ref[...] = norm_back(x1_ref[...], gain_ref[...], dn[...])
    dx1_ref[...] = dx2_ref[...] + dv
    whole_weight(wo_ref, weight)
    inner = dso_ref.shape[2]
    per = TILE // inner if inner < TILE else 1
    da = dx1_ref[...].astype(BF)
    for t in range(width // TILE):
        tile = nt(da, weight[t * TILE : (t + 1) * TILE, :]).astype(BF)
        for u in range(per):
            dso_ref[t * per + u] = tile[:, u * inner : (u + 1) * inner]


def middle_back(earlier, dx2, x1, gain, packed, cq, ckv, cot, lse, head_count, parts):
    rows, width = dx2.shape
    size = width // head_count
    count = ckv.shape[1]
    shapes = [
        jax.ShapeDtypeStruct((rows, width), F32), jax.ShapeDtypeStruct((1, width), F32),
        jax.ShapeDtypeStruct((rows, width), BF), jax.ShapeDtypeStruct(ckv.shape, BF),
        jax.ShapeDtypeStruct((parts, rows, width // parts), BF),
    ]
    return pl.pallas_call(
        leaving_out(functools.partial(middle_back_kernel, head_count), len(earlier)),
        grid=(1,),
        out_shape=shapes,
        in_specs=unread(earlier) + [
            whole((rows, width)), whole((rows, width)), whole((1, width)),
            packed_spec(packed, 0), packed_spec(packed, 1), packed_spec(packed, 2),
            whole((rows, width)), whole(ckv.shape), whole(cot.shape), whole(lse.shape),
        ],
        out_specs=[whole(s.shape) for s in shapes],
        scratch_shapes=[
            pltpu.VMEM((width, width), BF), pltpu.VMEM((rows, width), BF),
            pltpu.VMEM((2 * size, count), BF), pltpu.VMEM((rows, width), F32),
        ],
        compiler_params=params(),
        cost_estimate=cost(60 * rows * width * width, 24 * rows * width),
        name="middle_back",
    )(*earlier, dx2, x1, gain, packed, packed, packed, cq, ckv, cot, lse)


def middle_grad_kernel(
    dx2_ref, x1_ref, gain_ref, cob_ref, dcq_ref, dckv_ref, source_ref, ob_ref, dx1_ref, wk_ref, wv_ref,
    g_ref, wk, wv, left, left_source,
):
    width = x1_ref.shape[1]
    parts, shards, _, own, _ = wk_ref.shape
    layout = (parts, shards, 5, own)
    tail = shards * 5 * own
    piece = source_ref.shape[0] // parts
    whole_weight(wk_ref, wk)
    whole_weight(wv_ref, wv)
    for t in range(width // TILE):
        span = slice(t * TILE, (t + 1) * TILE)
        value = (nt(dckv_ref[0], wk[span, :]) + nt(dckv_ref[1], wv[span, :])).astype(BF)
        for c in range(parts):
            g_ref[c, tail : tail + piece, span] = value[c * piece : (c + 1) * piece]

    def product(which, lhs, right):
        def tile(t, _):
            cols = line_tile(t)
            store_rows(g_ref, layout, which, cols, nn(lhs[...], right(cols)).astype(BF))
            return 0

        lax.fori_loop(0, width // TILE, tile, 0)

    left[...] = jnp.transpose(ob_ref[...], (1, 0))
    product(0, left, lambda cols: dx1_ref[:, cols].astype(BF))
    x1 = x1_ref[...]
    left[...] = jnp.transpose((x1 * inverse_rms(x1) * gain_ref[...]).astype(BF), (1, 0))
    product(1, left, lambda cols: dcq_ref[:, cols])
    left[...] = jnp.transpose(cob_ref[...], (1, 0))
    product(2, left, lambda cols: dx2_ref[:, cols].astype(BF))
    left_source[...] = jnp.transpose(source_ref[...], (1, 0))
    product(3, left_source, lambda cols: dckv_ref[0, :, cols])
    product(4, left_source, lambda cols: dckv_ref[1, :, cols])


def middle_grads(dx2, x1, gain, cob, dcq, dckv, source, ob, dx1, packed):
    rows, width = dx2.shape
    count = source.shape[0]
    parts, shards, _, own, _ = packed.shape
    tokens = whole((rows, width))
    shape = (parts, shards * 5 * own + count // parts, width)
    return pl.pallas_call(
        middle_grad_kernel,
        grid=(1,),
        out_shape=jax.ShapeDtypeStruct(shape, BF),
        in_specs=[
            tokens, tokens, whole((1, width)), tokens, tokens, whole(dckv.shape), whole((count, width)), tokens, tokens,
            packed_spec(packed, 3), packed_spec(packed, 4),
        ],
        out_specs=whole(shape),
        scratch_shapes=[
            pltpu.VMEM((width, width), BF), pltpu.VMEM((width, width), BF),
            pltpu.VMEM((width, rows), BF), pltpu.VMEM((width, count), BF),
        ],
        compiler_params=params(),
        cost_estimate=cost(46 * rows * width * width, 24 * rows * width),
        name="middle_grads",
    )(dx2, x1, gain, cob, dcq, dckv, source, ob, dx1, packed, packed)


def final_kernel(d_ref, w_ref, states_ref, gain_ref, dx1_ref, out_ref):
    dn = None
    for s in range(d_ref.shape[0]):
        part = nt(d_ref[s], w_ref[s])
        dn = part if dn is None else dn + part
    dv, _ = norm_back(states_ref[...].astype(F32), gain_ref[...], dn)
    out_ref[...] = dx1_ref[...] + dv


def final_back(dqkv, weights, states, gain, dx1, tile=128):
    parts, rows, inner = dqkv.shape
    width = states.shape[1]
    return pl.pallas_call(
        final_kernel,
        grid=(rows // tile,),
        out_shape=jax.ShapeDtypeStruct((rows, width), F32),
        in_specs=[
            pl.BlockSpec((parts, tile, inner), lambda i: (0, i, 0)),
            whole(weights.shape),
            pl.BlockSpec((tile, width), lambda i: (i, 0)),
            whole((1, width)),
            pl.BlockSpec((tile, width), lambda i: (i, 0)),
        ],
        out_specs=pl.BlockSpec((tile, width), lambda i: (i, 0)),
        compiler_params=params(),
        cost_estimate=cost(6 * rows * width * width, 12 * rows * width),
        name="final_back",
    )(dqkv, weights, states, gain, dx1)


def first_kernel(states_ref, gain_ref, w_ref, out_ref):
    x = states_ref[0].astype(F32)
    n = (x * inverse_rms(x) * gain_ref[...]).astype(BF)
    out_ref[...] = nn(n, w_ref[...]).astype(BF)


def first_projection(gathered, gain, weight, rows):
    parts, _, width = gathered.shape
    cols = weight.shape[1]
    return pl.pallas_call(
        first_kernel,
        grid=(parts,),
        out_shape=jax.ShapeDtypeStruct((parts * rows, cols), BF),
        in_specs=[
            pl.BlockSpec((1, rows, width), lambda i: (i, 0, 0)), whole((1, width)), whole((width, cols)),
        ],
        out_specs=pl.BlockSpec((rows, cols), lambda i: (i, 0)),
        compiler_params=params(),
        cost_estimate=cost(4 * parts * rows * width * cols, 2 * parts * rows * (width + cols)),
        name="first_projection",
    )(gathered, gain, weight)


def last_kernel(states_ref, gain_ref, w_ref, d_ref, gw_ref, gain_out_ref, acc_ref):
    step = pl.program_id(0)
    x = states_ref[0].astype(F32)
    n = (x * inverse_rms(x) * gain_ref[...]).astype(BF)
    g = lax.dot_general(n, d_ref[...], (((0,), (0,)), ((), ())), preferred_element_type=F32)

    @pl.when(step == 0)
    def _():
        acc_ref[...] = g

    @pl.when(step > 0)
    def _():
        acc_ref[...] += g

    @pl.when(step == pl.num_programs(0) - 1)
    def _():
        total = acc_ref[...]
        if len(gw_ref.shape) == 2:
            gw_ref[...] = total.astype(BF)
        else:
            shards, piece, wide = gw_ref.shape
            rows = total.shape[0] // shards
            for z in range(shards):
                block = total[z * rows : (z + 1) * rows].astype(BF)
                stacked = jnp.concatenate([block[:, i * 128 : (i + 1) * 128] for i in range(3)], axis=0)
                for b in range(wide // 128):
                    gw_ref[z, :, b * 128 : (b + 1) * 128] = stacked[b * piece : (b + 1) * piece]
        gain_out_ref[...] = jnp.sum(total * w_ref[...].astype(F32), axis=1, keepdims=True)


def last_projection(gathered, gain, weight, grads, rows, shards):
    parts, _, width = gathered.shape
    cols = weight.shape[1]
    shape = (shards, cols // shards, width) if shards else (width, cols)
    return pl.pallas_call(
        last_kernel,
        grid=(parts,),
        out_shape=(jax.ShapeDtypeStruct(shape, BF), jax.ShapeDtypeStruct((width, 1), F32)),
        in_specs=[
            pl.BlockSpec((1, rows, width), lambda i: (i, 0, 0)), whole((1, width)), whole((width, cols)),
            pl.BlockSpec((rows, cols), lambda i: (i, 0)),
        ],
        out_specs=[whole(shape), whole((width, 1))],
        scratch_shapes=[pltpu.VMEM((width, cols), F32)],
        compiler_params=params(),
        cost_estimate=cost(4 * parts * rows * width * cols, 2 * parts * rows * (width + cols)),
        name="last_projection",
    )(gathered, gain, weight, grads)


def unpack_kernel(own, piece, rest_ref, *outs):
    parts, total, width = rest_ref.shape
    first = 5 * own
    rows, inner = outs[6].shape[0], width // parts
    down_at = first + piece + 16
    down, half = total - down_at, width // 2
    for c in range(parts):
        for i in range(5):
            outs[i][c * own : (c + 1) * own, :] = rest_ref[c, i * own : (i + 1) * own, :].astype(F32)
        for i in range(2):
            start = ((c // 2) * 2 + i) * down
            value = rest_ref[c, down_at:total, i * half : (i + 1) * half]
            outs[5][start : start + down, (c % 2) * half : (c % 2 + 1) * half] = value.astype(F32)
        for b in range(width // 128):
            low, end = b * piece, (b + 1) * piece
            while low < end:
                which, row = low // rows, low % rows
                count = min(end - low, rows - row)
                at = first + low - b * piece
                value = rest_ref[c, at : at + count, b * 128 : (b + 1) * 128]
                outs[6 + which][row : row + count, c * inner : (c + 1) * inner] = value.astype(F32)
                low += count


def unpack(rest, own, piece, rows, inner):
    parts, total, width = rest.shape
    down_rows = (total - 5 * own - piece - 16) * parts
    square = jax.ShapeDtypeStruct((rows, width), F32)
    shapes = [square] * 5 + [jax.ShapeDtypeStruct((down_rows, width), F32)] + [square] * 3
    return pl.pallas_call(
        functools.partial(unpack_kernel, own, piece),
        grid=(1,),
        out_shape=shapes,
        in_specs=[whole(rest.shape)],
        out_specs=[whole(v.shape) for v in shapes],
        compiler_params=params(),
        cost_estimate=cost(0, 6 * rest.size),
        name="unpack",
    )(rest)


CTX = ("plane", "core")


def copies(piece):
    return jnp.broadcast_to(piece[None], (lax.axis_size("fsdp"),) + piece.shape)


def spread(piece):
    return lax.all_to_all(copies(piece), "fsdp", 0, 0, tiled=True)


def collect(parts, *earlier):
    parts = lax.all_to_all(parts, "fsdp", 0, 0, tiled=True)
    if earlier:
        parts = after(parts, *earlier)
    return jnp.sum(parts.astype(F32), axis=0).astype(BF)


def collect_far(parts):
    count, mine = lax.axis_size("fsdp"), lax.axis_index("fsdp")
    if count > 4:
        return collect(parts).astype(F32)
    total = take(parts, mine, 0).astype(F32)
    for step in range(1, count):
        for sign in (1, -1):
            message = take(parts, jnp.clip(mine + sign * step, 0, count - 1), 0)
            pairs = [(i, i + sign * step) for i in range(count) if 0 <= i + sign * step < count]
            total = total + lax.ppermute(message, "fsdp", pairs).astype(F32)
    return total


def nothing(*refs):
    pass


def after(value, *earlier):
    return pl.pallas_call(
        nothing,
        out_shape=jax.ShapeDtypeStruct(value.shape, value.dtype),
        in_specs=[pl.BlockSpec(memory_space=pl.ANY)] * (1 + len(earlier)),
        out_specs=pl.BlockSpec(memory_space=pl.ANY),
        input_output_aliases={0: 0},
        name="after",
    )(value, *earlier)


def own_rows(shard):
    rows = shard.shape[0] // lax.axis_size(CTX)
    return lax.dynamic_slice_in_dim(shard, lax.axis_index(CTX) * rows, rows, 0)


def swap(value, axis):
    return lax.ppermute(value, axis, [(0, 1), (1, 0)])


def take(value, index, axis):
    return lax.dynamic_index_in_dim(value, index, axis, keepdims=False)


def gather_down(shard, earlier):
    rows, width = shard.shape
    start = lax.axis_index("core") * (width // 2)
    mine = spread(after(lax.dynamic_slice_in_dim(shard, start, width // 2, 1), earlier)).reshape(-1, width // 2)
    return mine, swap(mine, "core")


def reduce_planes(half, later):
    planes, width = lax.axis_size("plane"), half.shape[1]
    if planes != 4:
        return lax.psum_scatter(half, "plane", scatter_dimension=0, tiled=True)
    plane = lax.axis_index("plane")
    quarters = half.reshape(planes, -1, width)
    total = take(quarters, plane, 0).astype(F32)
    for step in range(1, planes):
        message = take(quarters, plane ^ step, 0)
        got = lax.ppermute(message, "plane", [(i, i ^ step) for i in range(planes)])
        total = total + after(got, later).astype(F32)
    return total.astype(BF)


def on_device(
    states, positions, segments, encoded, cotangent,
    self_gain, self_query, self_key, self_value, self_output, bias_table,
    cross_gain, cross_query, cross_key, cross_value, cross_output,
    feed_gain, gate_weight, up_weight, down_weight,
):
    parts, shards = lax.axis_size(CTX), lax.axis_size("fsdp")
    place = lax.axis_index(CTX)
    core = lax.axis_index("core").astype(jnp.int32).reshape(1)
    local, width = states.shape[1:]
    head_count = bias_table.shape[1]
    size = width // head_count
    heads = head_count // parts
    inner = heads * size
    blocks = local // BLK
    shard_width = self_gain.shape[0]
    hidden_width = gate_weight.shape[1]
    own = shard_width // parts
    aligned = own % 16 == 0

    def arranged(pieces):
        if aligned:
            return pieces
        matrices, columns = pieces.shape[2], pieces.shape[4]
        return pieces.transpose(2, 1, 0, 3, 4).reshape(1, 1, matrices, width, columns)

    def scattered(grads):
        if aligned:
            return grads
        matrices, columns = grads.shape[2], grads.shape[4]
        return grads.reshape(matrices, shards, parts, own, columns).transpose(2, 1, 0, 3, 4)

    gathered = lax.all_gather(jnp.concatenate([states[0], encoded[0]], axis=0), CTX, axis=0, tiled=False)
    encoded_all = gathered[:, local:].reshape(-1, width)
    columns = lax.dynamic_slice_in_dim(
        jnp.stack([self_query, self_key, self_value], axis=1), place * inner, inner, 2
    ).reshape(shard_width, 3 * inner)
    small = jnp.concatenate([self_gain, cross_gain, feed_gain, bias_table.reshape(-1)])
    small_width = small.shape[0]
    small = jnp.pad(small, (0, 16 * 3 * inner - small_width)).reshape(16, 3 * inner)
    first_pos, first_seg = positions[0, ::BLK], segments[0, ::BLK]
    canon = jnp.where(
        first_seg == 0,
        first_pos // BLK,
        PROMPT // BLK + (first_seg - 1) * (CLEN // BLK) + (first_pos - PROMPT) // BLK,
    )
    canon_all = lax.all_gather(canon, CTX, axis=0, tiled=True)
    slots = jnp.argmax(canon_all[None, :] == jnp.arange(blocks * parts)[:, None], axis=1).astype(jnp.int32)
    line = jnp.concatenate([columns, small], axis=0)
    squares = [own_rows(w) for w in (self_output, cross_query, cross_output, cross_key, cross_value)]
    wide = copies(jnp.stack([own_rows(gate_weight), own_rows(up_weight)], axis=0))
    squares = spread(jnp.concatenate(squares + [line.reshape(-1, width)], axis=0))
    squares = after(squares, slots, wide)
    line = squares[:, 5 * own :].reshape((shards,) + line.shape)
    squares = squares[:, : 5 * own].reshape(shards, 5, own, width)
    qkv_weight = line[:, :shard_width].reshape(width, 3 * inner)
    small = line[:, shard_width:].reshape(shards, -1)[:, :small_width].astype(F32)
    gains = [small[:, i * shard_width : (i + 1) * shard_width].reshape(1, width) for i in range(3)]
    table = small[:, 3 * shard_width :].reshape(BUCKETS, head_count)
    own_table = lax.dynamic_slice_in_dim(table, place * heads, heads, 1).reshape(-1)

    wide = lax.all_to_all(after(wide, squares), "fsdp", 0, 0, tiled=True)
    squares = lax.all_gather(squares, CTX, axis=0, tiled=False)

    prompt_tiles = PROMPT // TILE
    qkv = first_projection(gathered, gains[0], qkv_weight, local).reshape(parts * blocks, BLK, 3 * inner)
    o, ot, lse = sa_fwd(slots, own_table, qkv, heads, prompt_tiles)
    o = lax.all_to_all(o.reshape(parts, local, inner), CTX, 0, 0, tiled=True)

    wide = lax.all_gather(after(wide, o), CTX, axis=0, tiled=False)
    squares, wide = arranged(squares), arranged(wide)
    down, other_down = gather_down(down_weight, o)
    ckv = source_projection(encoded_all, squares)
    ob, x1, cq, cob, cot, cross_lse, x2, n3 = middle_forward(
        o, states[0], gains[1], gains[2], squares, ckv, head_count
    )
    qkv_all = lax.all_gather(after(qkv_weight, x2), CTX, axis=0, tiled=False)
    hidden, dx2, feed_gain_part, g_wide, g_down, g_other = feed_forward(
        core, n3, cotangent[0], x2, gains[2], wide, down, other_down
    )
    g_wide = lax.psum_scatter(scattered(g_wide), CTX, scatter_dimension=0, tiled=False)
    g_down = (g_down.astype(F32) + swap(g_other, "core").astype(F32)).astype(BF).reshape(shards, -1, width // 2)
    dx1, cross_gain_part, dcq, dckv, dso = middle_back(
        (qkv_all,), dx2, x1, gains[1], squares, cq, ckv, cot, cross_lse, head_count, parts
    )
    dso = lax.all_to_all(dso, CTX, 0, 0, tiled=True).reshape(parts * blocks, BLK, inner)
    g_squares = middle_grads(dx2, x1, gains[1], cob, after(dcq, g_down), dckv, encoded_all, ob, dx1, squares)
    if not aligned:
        encoded_part = g_squares[0, 5 * width :].reshape(parts, -1, width)
        g_squares = scattered(g_squares[0, : 5 * width].reshape(1, 1, 5, width, width)).reshape(parts, -1, width)
        g_squares = jnp.concatenate([g_squares, encoded_part], axis=1)
    middle = prompt_tiles + (blocks * parts * BLK // TILE - prompt_tiles) // 4
    g_squares = after(g_squares, dso)
    held = sa_bwd((g_squares,), slots, own_table, qkv, dso, ot, lse, heads, prompt_tiles, 0, middle)
    g_squares = lax.psum_scatter(g_squares, CTX, scatter_dimension=0, tiled=False)
    g_down = collect(after(g_down, dso), held[0])
    dqkv, dtable = sa_bwd(
        (g_wide,), slots, own_table, qkv, dso, ot, lse, heads, prompt_tiles, middle,
        blocks * parts * BLK // TILE, held,
    )
    g_wide = collect(after(g_wide, g_down), dqkv)
    g_down = reduce_planes(g_down, dqkv)
    dqkv_local = lax.all_to_all(after(dqkv, g_wide, g_down).reshape(parts, local, 3 * inner), CTX, 0, 0, tiled=True)
    g_down = jnp.concatenate([g_down[: g_down.shape[0] // 2], g_down[g_down.shape[0] // 2 :]], axis=1)
    grads = dqkv.reshape(parts * local, 3 * inner)
    compact = aligned and inner == 128 and (3 * inner // shards) % 16 == 0
    g_qkv, self_gain_part = last_projection(gathered, gains[0], qkv_weight, grads, local, shards if compact else 0)
    table_part = jnp.zeros((BUCKETS, head_count), F32)
    table_part = lax.dynamic_update_slice_in_dim(table_part, dtable[:, :, 0].T, place * heads, 1)
    sums = [self_gain_part[:, 0] / gains[0][0], cross_gain_part[0], feed_gain_part[0]]
    sums = jnp.concatenate([v.reshape(shards, shard_width) for v in sums] + [table_part.reshape(shards, -1)], axis=1)
    if compact:
        sums = jnp.pad(sums, ((0, 0), (0, 16 * width - small_width))).reshape(shards, 16, width).astype(BF)
        last = jnp.concatenate([g_qkv, sums], axis=1)
    else:
        sums = jnp.pad(sums, ((0, 0), (0, 16 * 3 * inner - small_width))).reshape(shards, 16, 3 * inner).astype(BF)
        last = jnp.concatenate([g_qkv.reshape(shards, shard_width, 3 * inner), sums], axis=1).reshape(shards, -1, width)
    g_squares = after(g_squares, g_wide, g_qkv)
    encoded_grad = g_squares[shards * 5 * own :].astype(F32)
    last_rows = last.shape[1]
    rest = jnp.concatenate([g_squares[: shards * 5 * own].reshape(shards, 5 * own, width), last], axis=1)
    rest = collect_far(rest).astype(BF)
    layer_out = layer_output((dqkv,), core, hidden, x2, down, other_down)
    states_grad = final_back(dqkv_local, qkv_all, states[0], gains[0], dx1)
    g_wide = lax.all_gather(g_wide, CTX, axis=0, tiled=False)
    rest = jnp.concatenate([rest, g_down], axis=0)
    rest = lax.all_gather(after(rest, g_wide, dqkv_local), CTX, axis=0, tiled=False)
    if compact:
        sums_at = 5 * own + g_qkv.shape[1]
        *g_squares, g_down, g_query, g_key, g_value = unpack(rest, own, g_qkv.shape[1], shard_width, inner)
        sums = jnp.sum(rest[:, sums_at].astype(F32), axis=0)
    else:
        last = rest[:, 5 * own : 5 * own + last_rows].reshape(parts, -1, 3 * inner)
        sums = jnp.sum(last[:, shard_width:].reshape(parts, -1).astype(F32), axis=0)
        rest = rest.astype(F32)
        g_squares = rest[:, : 5 * own].reshape(parts, 5, own, width).transpose(1, 0, 2, 3).reshape(5, shard_width, width)
        g_down = rest[:, 5 * own + last_rows :].reshape(parts // 2, 2, -1, 2, width // 2).transpose(0, 3, 2, 1, 4)
        g_down = g_down.reshape(-1, width)
        g_qkv = last[:, :shard_width].astype(F32).reshape(parts, shard_width, 3, inner).transpose(2, 1, 0, 3)
        g_query, g_key, g_value = g_qkv.reshape(3, shard_width, width)
    gain_grads = [sums[i * shard_width : (i + 1) * shard_width] for i in range(3)]
    table_grad = sums[3 * shard_width : small_width].reshape(-1, head_count)
    g_wide = g_wide.astype(F32).transpose(1, 0, 2, 3).reshape(2, shard_width, hidden_width)
    return (
        layer_out[None], states_grad[None], encoded_grad[None],
        gain_grads[0], g_query, g_key, g_value, g_squares[0], table_grad,
        gain_grads[1], g_squares[1], g_squares[3], g_squares[4], g_squares[2],
        gain_grads[2], g_wide[0], g_wide[1], g_down,
    )


def solution(mesh):
    ctx, fsdp = mesh.devices.shape
    split = Mesh(mesh.devices.reshape(ctx // 2, 2, fsdp), ("plane", "core", "fsdp"))
    tokens, matrix, vector = P("fsdp", CTX, None), P("fsdp", None), P("fsdp")
    place = P("fsdp", CTX)
    return jax.shard_map(
        on_device,
        mesh=split,
        in_specs=(tokens, place, place, tokens, tokens)
        + (vector, matrix, matrix, matrix, matrix, matrix)
        + (vector, matrix, matrix, matrix, matrix)
        + (vector, matrix, matrix, matrix),
        out_specs=(tokens, tokens, tokens)
        + (vector, matrix, matrix, matrix, matrix, matrix)
        + (vector, matrix, matrix, matrix, matrix)
        + (vector, matrix, matrix, matrix),
        check_vma=False,
    )
```

```python
import functools
import math

import jax
import jax.numpy as jnp
from jax import lax
from jax.experimental import pallas as pl
from jax.experimental.pallas import tpu as pltpu
from jax.sharding import Mesh
from jax.sharding import PartitionSpec as P

BUCKETS = 32
DISTANCE = 128
PROMPT = 2048
CLEN = 256
BLK = 128
TILE = 256
NEG = -1e30
F32 = jnp.float32
BF = jnp.bfloat16
epsilon = 1e-06
gelu_scale = math.sqrt(2.0 / math.pi)
VMEM_LIMIT = 56 * 1024 * 1024


def bucket_starts():
    half=BUCKETS//2
    edges=[math.ceil(half*(DISTANCE/half)**(e/half)) for e in range(1,half)]
    return list(range(half+1))+edges

def nt(a,b):
    return lax.dot_general(a,b,(((1,),(1,)),((),())),preferred_element_type=F32)
def nn(a,b):
    return lax.dot_general(a,b,(((1,),(0,)),((),())),preferred_element_type=F32)

def leaving_out(kernel,count):
    return lambda *refs: kernel(*refs[count:])

def unread(operands):
    return [pl.BlockSpec(memory_space=pl.ANY)]*len(operands)

def head_mask(value,head,heads):
    if heads==1: return value
    size=value.shape[-1]//heads
    lane=lax.broadcasted_iota(jnp.int32,value.shape,1)
    return jnp.where((lane>=head*size)&(lane<(head+1)*size),value,jnp.zeros_like(value))

def build_bias(tab_ref,bias_ref,heads):
    starts=bucket_starts()
    key=lax.broadcasted_iota(jnp.int32,(BLK,BLK),0)
    query=lax.broadcasted_iota(jnp.int32,(BLK,BLK),1)
    for h in range(heads):
        last=tab_ref[(BUCKETS-1)*heads+h]
        for sub in (0,1):
            dist=query-key+BLK*sub
            val=jnp.full((BLK,BLK),tab_ref[h]-last,F32)
            for b in range(1,BUCKETS):
                val=jnp.where(dist>=starts[b],tab_ref[b*heads+h]-last,val)
            if sub==0:
                val=jnp.where(dist>=0,val,NEG)
                bias_ref[h,0:BLK,0:BLK]=val
                bias_ref[h,BLK:,BLK:]=val
            else:
                bias_ref[h,0:BLK,BLK:]=val
        bias_ref[h,BLK:,0:BLK]=jnp.full((BLK,BLK),NEG,F32)

def load_tile(src,slots,tile,lo,hi):
    a=src[slots[2*tile],:,lo:hi]
    b=src[slots[2*tile+1],:,lo:hi]
    return jnp.concatenate([a,b],axis=0)

def fwd_kernel(heads,prompt_tiles,slots,tab,qkv,o_ref,ot_ref,lse_ref,bias,kc,vt,qm,s_scr):
    tiles=kc.shape[0]//TILE
    width=kc.shape[1]
    size=width//heads
    build_bias(tab,bias,heads)
    def arrange(t,_):
        rows=pl.ds(pl.multiple_of(t*TILE,TILE),TILE)
        kc[rows,:]=load_tile(qkv,slots,t,width,2*width)
        vt[t]=jnp.transpose(load_tile(qkv,slots,t,2*width,3*width),(1,0))
        return 0
    lax.fori_loop(0,tiles,arrange,0)

    def scores(t_rows,h,kind,qh):
        s=nt(kc[t_rows,:],qh)
        if kind=="own":
            s=s+bias[h]
        elif kind=="prev":
            top=s[:BLK]
            low=jnp.concatenate([s[BLK:,:BLK]+bias[h,0:BLK,BLK:],s[BLK:,BLK:]],axis=1)
            s=jnp.concatenate([top,low],axis=0)
        return s

    def tile_body(t,n_far,own_static):
        q=load_tile(qkv,slots,t,0,width)
        qh=[head_mask(q,h,heads) for h in range(heads)]
        own_rows_at=pl.ds(t*TILE if own_static else pl.multiple_of(t*TILE,TILE),TILE)
        def make(h,j):
            rows=pl.ds(j*TILE,TILE) if j<n_far else own_rows_at
            s=scores(rows,h,"own" if j==n_far else "prev" if j==n_far-1 else "far",qh[h])
            s_scr[h,j]=s
            return jnp.max(s.reshape(TILE//8,8,TILE),axis=0)
        outs=[]
        peak=None
        for j in range(n_far+1):
            part=make(0,j)
            peak=part if peak is None else jnp.maximum(peak,part)
        for h in range(heads):
            m=jnp.max(peak,axis=0,keepdims=True)
            l=None; acc=None; peak=None
            for j in range(n_far+1):
                if h+1<heads:
                    part=make(h+1,j)
                    peak=part if peak is None else jnp.maximum(peak,part)
                p=jnp.exp(s_scr[h,j]-m)
                part=jnp.sum(p.reshape(TILE//8,8,TILE),axis=0)
                l=part if l is None else l+part
                a=nn(vt[j if j<n_far else t,h*size:(h+1)*size,:],p.astype(BF))
                acc=a if acc is None else acc+a
            l=jnp.sum(l,axis=0,keepdims=True)
            o=acc*(1.0/l)
            ot_ref[h*size:(h+1)*size,own_rows_at]=o
            lse_ref[h:h+1,own_rows_at]=m+jnp.log(l)
            outs.append(o)
        o=jnp.concatenate(outs,axis=0) if heads>1 else outs[0]
        o=jnp.transpose(o,(1,0)).astype(BF)
        o_ref[slots[2*t]]=o[:BLK]
        o_ref[slots[2*t+1]]=o[BLK:]
    for t in range(prompt_tiles):
        tile_body(t,t,True)
    def cont(c,_):
        tile_body(c,prompt_tiles,False)
        return 0
    lax.fori_loop(prompt_tiles,tiles,cont,0)

def sa_fwd(slots,tab,qkv,heads,prompt_tiles):
    nb,_,w3=qkv.shape; w=w3//3; n=nb*BLK; tiles=n//TILE
    return pl.pallas_call(
        functools.partial(fwd_kernel,heads,prompt_tiles),
        out_shape=(jax.ShapeDtypeStruct((nb,BLK,w),BF),jax.ShapeDtypeStruct((w,n),F32),jax.ShapeDtypeStruct((heads,n),F32)),
        in_specs=[pl.BlockSpec(memory_space=pltpu.SMEM),pl.BlockSpec(memory_space=pltpu.SMEM),pl.BlockSpec(memory_space=pltpu.VMEM)],
        out_specs=[pl.BlockSpec(memory_space=pltpu.VMEM)]*3,
        scratch_shapes=[pltpu.VMEM((heads,TILE,TILE),F32),pltpu.VMEM((n,w),BF),pltpu.VMEM((tiles,w,TILE),BF),pltpu.VMEM((8,128),F32),pltpu.VMEM((heads,prompt_tiles+1,TILE,TILE),F32)],
        compiler_params=pltpu.CompilerParams(vmem_limit_bytes=VMEM_LIMIT),
        cost_estimate=cost(32 * 10**9, 8 * n * w3),
        name="self_attention_forward",
    )(slots,tab,qkv)

def bwd_kernel(heads,prompt_tiles,low,high,slots,tab,qkv,do_ref,ot_ref,lse_ref,*refs):
    if low:
        dq_in,dkv_in,near_in,far_in,dqkv_ref,dtab_ref,bias,kc,vc,kt,dqt,dkv,near,far=refs
    else:
        dq_out,dkv,near,far,bias,kc,vc,kt,dqt=refs
    tiles=kc.shape[0]//TILE
    width=kc.shape[1]
    size=width//heads
    build_bias(tab,bias,heads)
    for mine,start in ((near,near_in if low else None),(far,far_in if low else None),(dkv,dkv_in if low else None)):
        mine[...]=start[...] if low else jnp.zeros_like(mine)
    def arrange(t,_):
        rows=pl.ds(pl.multiple_of(t*TILE,TILE),TILE)
        k=load_tile(qkv,slots,t,width,2*width)
        kc[rows,:]=k
        kt[t]=jnp.transpose(k,(1,0))
        vc[rows,:]=load_tile(qkv,slots,t,2*width,3*width)
        return 0
    lax.fori_loop(0,tiles,arrange,0)

    def query_tile(t,_):
        cols=pl.ds(pl.multiple_of(t*TILE,TILE),TILE)
        q=load_tile(qkv,slots,t,0,width)
        do=load_tile(do_ref,slots,t,0,width)
        dot=jnp.transpose(do.astype(F32),(1,0))*ot_ref[:,cols]
        qh=[head_mask(q,h,heads) for h in range(heads)]
        doh=[head_mask(do,h,heads) for h in range(heads)]
        lse=[lse_ref[h:h+1,cols] for h in range(heads)]
        delta=[jnp.sum(dot[h*size:(h+1)*size],axis=0,keepdims=True) for h in range(heads)]
        dqt[...]=jnp.zeros_like(dqt)

        def group(*pieces):
            spans=[pl.ds(pl.multiple_of(j*TILE,TILE),TILE) for j,_ in pieces]
            keys=[kc[rows,:] for rows in spans]
            values=[vc[rows,:] for rows in spans]
            turned=[kt[j] for j,_ in pieces]
            dk=[None]*len(pieces); dv=[None]*len(pieces)
            dq_parts=[]; far_parts=[]
            for h in range(heads):
                dq=None; sums=None
                for i,(j,kind) in enumerate(pieces):
                    s=nt(keys[i],qh[h])
                    if kind=="own":
                        s=s+bias[h]
                    elif kind=="prev":
                        lower=jnp.concatenate([s[BLK:,:BLK]+bias[h,0:BLK,BLK:],s[BLK:,BLK:]],axis=1)
                        s=jnp.concatenate([s[:BLK],lower],axis=0)
                    p=jnp.exp(s-lse[h])
                    ds=p*(nt(values[i],doh[h])-delta[h])
                    if kind=="own":
                        near[h,0]+=ds[:BLK,:BLK]+ds[BLK:,BLK:]
                        near[h,1]+=ds[:BLK,BLK:]
                    else:
                        if kind=="prev":
                            near[h,1]+=ds[BLK:,:BLK]
                            rest=jnp.concatenate([jnp.zeros((BLK,BLK),F32),ds[BLK:,BLK:]],axis=1)
                            part=jnp.sum((ds[:BLK]+rest).reshape(BLK//8,8,TILE),axis=0)
                        else:
                            part=jnp.sum(ds.reshape(TILE//8,8,TILE),axis=0)
                        sums=part if sums is None else sums+part
                    pb=p.astype(BF); db=ds.astype(BF)
                    a=nn(pb,doh[h]); dv[i]=a if dv[i] is None else dv[i]+a
                    b=nn(db,qh[h]); dk[i]=b if dk[i] is None else dk[i]+b
                    c=nn(turned[i][h*size:(h+1)*size,:],db); dq=c if dq is None else dq+c
                dq_parts.append(dq); far_parts.append(sums)
            for h in range(heads):
                dqt[h*size:(h+1)*size,:]+=dq_parts[h]
                if far_parts[h] is not None:
                    far[h]+=far_parts[h]
            for i,rows in enumerate(spans):
                dkv[rows,0:width]+=dk[i]
                dkv[rows,width:2*width]+=dv[i]
        count=jnp.minimum(t,prompt_tiles)
        pairs=jnp.maximum(count-1,0)//2
        def far_pair(i,_):
            group((2*i,"far"),(2*i+1,"far"))
            return 0
        lax.fori_loop(0,pairs,far_pair,0)
        left=count-2*pairs
        @pl.when(left==0)
        def _():
            group((t,"own"))
        @pl.when(left==1)
        def _():
            group((count-1,"prev"),(t,"own"))
        @pl.when(left==2)
        def _():
            group((count-2,"far"),(count-1,"prev"),(t,"own"))
        dq=jnp.transpose(dqt[...],(1,0)).astype(BF)
        if low:
            dqkv_ref[slots[2*t],:,0:width]=dq[:BLK]
            dqkv_ref[slots[2*t+1],:,0:width]=dq[BLK:]
        else:
            dq_out[cols,:]=dq
        return 0
    lax.fori_loop(low,high,query_tile,0)
    if not low:
        return
    def bring(t,_):
        dq=dq_in[pl.ds(pl.multiple_of(t*TILE,TILE),TILE),:]
        dqkv_ref[slots[2*t],:,0:width]=dq[:BLK]
        dqkv_ref[slots[2*t+1],:,0:width]=dq[BLK:]
        return 0
    lax.fori_loop(0,low,bring,0)
    def finish(t,_):
        g=dkv[pl.ds(pl.multiple_of(t*TILE,TILE),TILE),:].astype(BF)
        dqkv_ref[slots[2*t],:,width:3*width]=g[:BLK]
        dqkv_ref[slots[2*t+1],:,width:3*width]=g[BLK:]
        return 0
    lax.fori_loop(0,tiles,finish,0)
    starts=bucket_starts()
    key=lax.broadcasted_iota(jnp.int32,(BLK,BLK),0)
    query=lax.broadcasted_iota(jnp.int32,(BLK,BLK),1)
    for h in range(heads):
        for b in range(BUCKETS):
            total=jnp.zeros((8,BLK),F32)
            for sub in (0,1):
                dist=query-key+BLK*sub
                inside=dist>=starts[b]
                if b<BUCKETS-1: inside=inside&(dist<starts[b+1])
                total=total+jnp.sum(jnp.where(inside,near[h,sub],0.0).reshape(BLK//8,8,BLK),axis=0)
            if b==BUCKETS-1:
                total=total+far[h,:,0:BLK]+far[h,:,BLK:]
            row=jnp.sum(total,axis=0,keepdims=True)
            dtab_ref[h,b:b+1,:]=jnp.broadcast_to(jnp.sum(row,axis=1,keepdims=True),(1,BLK))

def sa_bwd(earlier,slots,tab,qkv,do,ot,lse,heads,prompt_tiles,low,high,held=()):
    nb,_,w3=qkv.shape; w=w3//3; n=nb*BLK; tiles=n//TILE
    shape=jax.ShapeDtypeStruct
    sums=[shape((n,2*w),F32),shape((heads,2,BLK,BLK),F32),shape((heads,8,TILE),F32)]
    if low:
        out=[shape((nb,BLK,w3),BF),shape((heads,BUCKETS,BLK),F32)]
    else:
        out=[shape((high*TILE,w),BF)]+sums
    scratch=[pltpu.VMEM((heads,TILE,TILE),F32),pltpu.VMEM((n,w),BF),pltpu.VMEM((n,w),BF),pltpu.VMEM((tiles,w,TILE),BF),pltpu.VMEM((w,TILE),F32)]
    if low:
        scratch+=[pltpu.VMEM(v.shape,F32) for v in sums]
    return pl.pallas_call(
        leaving_out(functools.partial(bwd_kernel,heads,prompt_tiles,low,high),len(earlier)),
        out_shape=out,
        in_specs=unread(earlier)+[pl.BlockSpec(memory_space=pltpu.SMEM)]*2+[pl.BlockSpec(memory_space=pltpu.VMEM)]*(4+len(held)),
        out_specs=[pl.BlockSpec(memory_space=pltpu.VMEM)]*len(out),
        scratch_shapes=scratch,
        compiler_params=pltpu.CompilerParams(vmem_limit_bytes=VMEM_LIMIT),
        cost_estimate=cost((250 if low else 43) * 10**9, 12 * n * w3),
        name="self_attention_backward",
    )(*earlier,slots,tab,qkv,do,ot,lse,*held)


def line_tile(step, size=TILE):
    return pl.ds(pl.multiple_of(step * size, size), size)


def whole_weight(ref, scratch):
    parts, shards, _, rows, _ = ref.shape
    for z in range(shards):
        for c in range(parts):
            start = (z * parts + c) * rows
            scratch[start : start + rows, :] = ref[c, z, 0]


def store_rows(ref, layout, which, cols, value):
    parts, shards, matrices, rows = layout
    for z in range(shards):
        place = (z * matrices + which) * rows
        for c in range(parts):
            start = (z * parts + c) * rows
            ref[c, place : place + rows, cols] = value[start : start + rows]


def store_grad(ref, which, cols, value):
    parts, shards, _, rows, _ = ref.shape
    for z in range(shards):
        for c in range(parts):
            start = (z * parts + c) * rows
            ref[c, z, which, :, cols] = value[start : start + rows]


def inverse_rms(v):
    return lax.rsqrt(jnp.mean(v * v, axis=-1, keepdims=True) + epsilon)


def norm_back(v, gain, dn):
    r = inverse_rms(v)
    weighted = dn * gain
    dv = r * weighted - v * (r * r * r) * jnp.mean(weighted * v, axis=-1, keepdims=True)
    return dv, jnp.sum(dn * v * r, axis=0, keepdims=True)


def whole(shape, index=None):
    zeros = (0,) * len(shape)
    return pl.BlockSpec(shape, lambda *_: zeros if index is None else index)


def packed_spec(packed, which):
    parts, shards, _, rows, width = packed.shape
    return pl.BlockSpec((parts, shards, 1, rows, width), lambda *_: (0, 0, which, 0, 0))


def params():
    return pltpu.CompilerParams(vmem_limit_bytes=VMEM_LIMIT)


def cost(flops, size):
    return pl.CostEstimate(flops=flops, bytes_accessed=size, transcendentals=0)


def encoder_rows(gathered, rows):
    parts, total, width = gathered.shape
    return pl.BlockSpec((parts, total - rows, width), lambda *_: (0, rows // (total - rows), 0))


def source_kernel(source_ref, w_ref, out_ref, weight):
    whole_weight(w_ref, weight)
    source = source_ref[...].reshape(-1, source_ref.shape[-1])
    for t in range(out_ref.shape[-1] // TILE):
        cols = slice(t * TILE, (t + 1) * TILE)
        out_ref[0, :, cols] = nn(source, weight[:, cols]).astype(BF)


def source_projection(gathered, local, packed):
    width = gathered.shape[2]
    rows = gathered.shape[0] * (gathered.shape[1] - local)
    parts, shards, _, own, _ = packed.shape
    return pl.pallas_call(
        source_kernel,
        grid=(2,),
        out_shape=jax.ShapeDtypeStruct((2, rows, width), BF),
        in_specs=[
            encoder_rows(gathered, local),
            pl.BlockSpec((parts, shards, 1, own, width), lambda i: (0, 0, 3 + i, 0, 0)),
        ],
        out_specs=pl.BlockSpec((1, rows, width), lambda i: (i, 0, 0)),
        scratch_shapes=[pltpu.VMEM((width, width), BF)],
        compiler_params=params(),
        cost_estimate=cost(4 * rows * width * width, 8 * width * width),
        name="source_projection",
    )(gathered, packed)


def middle_kernel(
    head_count, o_ref, states_ref, gain_two, gain_three, wo_ref, wq_ref, wc_ref, ckv_ref,
    ob_ref, x1_ref, cq_ref, cob_ref, cot_ref, lse_ref, x2_ref, n3_ref, weight, cvt,
):
    rows, width = states_ref.shape
    size = width // head_count
    pair = 2 * size
    for s in range(o_ref.shape[0]):
        inner = o_ref.shape[2]
        ob_ref[:, s * inner : (s + 1) * inner] = o_ref[s]
    whole_weight(wo_ref, weight)

    def add_out(t, _):
        cols = line_tile(t)
        x1_ref[:, cols] = states_ref[:, cols].astype(F32) + nn(ob_ref[...], weight[:, cols])
        return 0

    lax.fori_loop(0, width // TILE, add_out, 0)
    x1 = x1_ref[...]
    n3_ref[...] = (x1 * inverse_rms(x1) * gain_two[...]).astype(BF)
    whole_weight(wq_ref, weight)

    def make_query(t, _):
        cols = line_tile(t)
        cq_ref[:, cols] = nn(n3_ref[...], weight[:, cols]).astype(BF)
        return 0

    lax.fori_loop(0, width // TILE, make_query, 0)

    def attend(p, _):
        cols = line_tile(p, pair)
        keys = ckv_ref[0, :, cols]
        cvt[...] = jnp.transpose(ckv_ref[1, :, cols], (1, 0))
        count = keys.shape[0]
        for half in range(rows // TILE):
            span = slice(half * TILE, (half + 1) * TILE)
            q = cq_ref[span, cols]
            outs = []
            for h in range(2):
                s = nt(keys, head_mask(q, h, 2))
                m = jnp.max(jnp.max(s.reshape(count // 8, 8, TILE), axis=0), axis=0, keepdims=True)
                e = jnp.exp(s - m)
                total = jnp.sum(jnp.sum(e.reshape(count // 8, 8, TILE), axis=0), axis=0, keepdims=True)
                out = nn(cvt[h * size : (h + 1) * size, :], e.astype(BF)) * (1.0 / total)
                lse_ref[p, h : h + 1, span] = m + jnp.log(total)
                outs.append(out)
            both = jnp.concatenate(outs, axis=0)
            cot_ref[p, :, span] = both
            cob_ref[span, cols] = jnp.transpose(both, (1, 0)).astype(BF)
        return 0

    lax.fori_loop(0, width // pair, attend, 0)
    whole_weight(wc_ref, weight)

    def add_cross(t, _):
        cols = line_tile(t)
        x2_ref[:, cols] = x1_ref[:, cols] + nn(cob_ref[...], weight[:, cols])
        return 0

    lax.fori_loop(0, width // TILE, add_cross, 0)
    x2 = x2_ref[...]
    n3_ref[...] = (x2 * inverse_rms(x2) * gain_three[...]).astype(BF)


def middle_forward(o, states, gain_two, gain_three, packed, ckv, head_count):
    rows, width = states.shape
    size = width // head_count
    pairs = head_count // 2
    tokens = lambda dtype: jax.ShapeDtypeStruct((rows, width), dtype)
    shapes = [
        tokens(BF), tokens(F32), tokens(BF), tokens(BF),
        jax.ShapeDtypeStruct((pairs, 2 * size, rows), F32), jax.ShapeDtypeStruct((pairs, 8, rows), F32),
        tokens(F32), tokens(BF),
    ]
    return pl.pallas_call(
        functools.partial(middle_kernel, head_count),
        grid=(1,),
        out_shape=shapes,
        in_specs=[
            whole(o.shape), whole((rows, width)), whole((1, width)), whole((1, width)),
            packed_spec(packed, 0), packed_spec(packed, 1), packed_spec(packed, 2), whole(ckv.shape),
        ],
        out_specs=[whole(s.shape) for s in shapes],
        scratch_shapes=[pltpu.VMEM((width, width), BF), pltpu.VMEM((2 * size, ckv.shape[1]), BF)],
        compiler_params=params(),
        cost_estimate=cost(60 * rows * width * width, 24 * rows * width),
        name="middle_forward",
    )(o, states, gain_two, gain_three, packed, packed, packed, ckv)


def feed_kernel(
    core_ref, n3_ref, cot_ref, x2_ref, gain_ref, w_ref, mine_ref, other_ref,
    hidden_ref, dx2_ref, gain_out_ref, gw_ref, keep_ref, give_ref, n3t, wg, wu, dgate, dup, down,
):
    step = pl.program_id(0)
    half = mine_ref.shape[1]
    own_half = pl.ds(pl.multiple_of(core_ref[0] * half, half), half)
    other_half = pl.ds(pl.multiple_of((1 - core_ref[0]) * half, half), half)
    down[:, own_half] = mine_ref[...]
    down[:, other_half] = other_ref[...]

    @pl.when(step == 0)
    def _():
        n3t[...] = jnp.transpose(n3_ref[...], (1, 0))

    parts, shards, _, rows, _ = w_ref.shape
    for z in range(shards):
        for c in range(parts):
            start = (z * parts + c) * rows
            wg[step, start : start + rows, :] = w_ref[c, z, 0]
            wu[step, start : start + rows, :] = w_ref[c, z, 1]
    n3, cot, wd = n3_ref[...], cot_ref[...], down[...]
    gate, up = nn(n3, wg[step]), nn(n3, wu[step])
    dh = nt(cot, wd)
    t = jnp.tanh(gelu_scale * (gate + 0.044715 * gate * gate * gate))
    gelu = 0.5 * gate * (1.0 + t)
    slope = 0.5 * (1.0 + t) + 0.5 * gate * (1.0 - t * t) * (gelu_scale * (1.0 + 3 * 0.044715 * gate * gate))
    hidden = (gelu * up).astype(BF)
    hidden_ref[...] = hidden
    dgate_low = (dh * up * slope).astype(BF)
    dup_low = (dh * gelu).astype(BF)
    dgate[step] = dgate_low
    dup[step] = dup_low
    down[...] = nn(jnp.transpose(hidden, (1, 0)), cot).astype(BF)
    keep_ref[...] = down[:, own_half]
    give_ref[...] = down[:, other_half]
    everything = slice(None)
    store_grad(gw_ref, 0, everything, nn(n3t[...], dgate_low).astype(BF))
    store_grad(gw_ref, 1, everything, nn(n3t[...], dup_low).astype(BF))

    @pl.when(step == pl.num_programs(0) - 1)
    def _():
        def tile(i, _):
            span = line_tile(i)
            total = None
            for s in range(dgate.shape[0]):
                term = nt(dgate[s], wg[s, span, :]) + nt(dup[s], wu[s, span, :])
                total = term if total is None else total + term
            dx2_ref[:, span] = total
            return 0

        lax.fori_loop(0, dx2_ref.shape[1] // TILE, tile, 0)
        dv, gain_out_ref[...] = norm_back(x2_ref[...], gain_ref[...], dx2_ref[...])
        dx2_ref[...] = cot_ref[...].astype(F32) + dv


def feed_forward(core, n3, cot, x2, gain, wide, mine, other):
    rows, width = n3.shape
    parts, shards, _, own, hidden = wide.shape
    steps = hidden // TILE
    tokens = lambda dtype: jax.ShapeDtypeStruct((rows, width), dtype)
    part = pl.BlockSpec((TILE, width // 2), lambda i: (i, 0))
    piece = pl.BlockSpec((parts, shards, 2, own, TILE), lambda i: (0, 0, 0, 0, i))
    return pl.pallas_call(
        feed_kernel,
        grid=(steps,),
        out_shape=[
            jax.ShapeDtypeStruct((rows, hidden), BF), tokens(F32), jax.ShapeDtypeStruct((1, width), F32),
            jax.ShapeDtypeStruct(wide.shape, BF), jax.ShapeDtypeStruct(mine.shape, BF), jax.ShapeDtypeStruct(mine.shape, BF),
        ],
        in_specs=[
            pl.BlockSpec(memory_space=pltpu.SMEM),
            whole((rows, width)), whole((rows, width)), whole((rows, width)), whole((1, width)), piece, part, part,
        ],
        out_specs=[
            pl.BlockSpec((rows, TILE), lambda i: (0, i)), whole((rows, width)), whole((1, width)),
            piece, part, part,
        ],
        scratch_shapes=[
            pltpu.VMEM((width, rows), BF), pltpu.VMEM((steps, width, TILE), BF), pltpu.VMEM((steps, width, TILE), BF),
            pltpu.VMEM((steps, rows, TILE), BF), pltpu.VMEM((steps, rows, TILE), BF), pltpu.VMEM((TILE, width), BF),
        ],
        compiler_params=params(),
        cost_estimate=cost(28 * rows * width * hidden, 12 * width * hidden),
        name="feed_forward",
    )(core, n3, cot, x2, gain, wide, mine, other)


def output_kernel(core_ref, hidden_ref, x2_ref, mine_ref, other_ref, out_ref):
    half = mine_ref.shape[1]
    own_half = pl.ds(pl.multiple_of(core_ref[0] * half, half), half)
    other_half = pl.ds(pl.multiple_of((1 - core_ref[0]) * half, half), half)
    hidden = hidden_ref[...]
    out_ref[:, own_half] = (x2_ref[:, own_half] + nn(hidden, mine_ref[...])).astype(BF)
    out_ref[:, other_half] = (x2_ref[:, other_half] + nn(hidden, other_ref[...])).astype(BF)


def layer_output(earlier, core, hidden, x2, mine, other, tile=128):
    rows, width = x2.shape
    units = hidden.shape[1]
    return pl.pallas_call(
        leaving_out(output_kernel, len(earlier)),
        grid=(rows // tile,),
        out_shape=jax.ShapeDtypeStruct((rows, width), BF),
        in_specs=unread(earlier) + [
            pl.BlockSpec(memory_space=pltpu.SMEM),
            pl.BlockSpec((tile, units), lambda i: (i, 0)), pl.BlockSpec((tile, width), lambda i: (i, 0)),
            whole(mine.shape), whole(mine.shape),
        ],
        out_specs=pl.BlockSpec((tile, width), lambda i: (i, 0)),
        compiler_params=params(),
        cost_estimate=cost(4 * rows * width * units, 4 * width * units),
        name="layer_output",
    )(*earlier, core, hidden, x2, mine, other)


def middle_back_kernel(
    head_count, dx2_ref, x1_ref, gain_ref, wo_ref, wq_ref, wc_ref, cq_ref, ckv_ref, cot_ref, lse_ref,
    dx1_ref, gain_out_ref, dcq_ref, dckv_ref, dso_ref, weight, dco, ckt, dn,
):
    rows, width = dx2_ref.shape
    size = width // head_count
    pair = 2 * size
    count = ckv_ref.shape[1]
    whole_weight(wc_ref, weight)

    def back_out(t, _):
        dco[:, line_tile(t)] = nt(dx2_ref[...].astype(BF), weight[line_tile(t), :]).astype(BF)
        return 0

    lax.fori_loop(0, width // TILE, back_out, 0)

    def attend(p, _):
        cols = line_tile(p, pair)
        q, do = cq_ref[:, cols], dco[:, cols]
        terms = jnp.transpose(do.astype(F32), (1, 0)) * cot_ref[p]
        ckt[...] = jnp.transpose(ckv_ref[0, :, cols], (1, 0))
        qh = [head_mask(q, h, 2) for h in range(2)]
        doh = [head_mask(do, h, 2) for h in range(2)]
        lse = [lse_ref[p, h : h + 1, :] for h in range(2)]
        delta = [jnp.sum(terms[h * size : (h + 1) * size], axis=0, keepdims=True) for h in range(2)]
        dqt = [None, None]
        for t in range(count // TILE):
            span = slice(t * TILE, (t + 1) * TILE)
            k, v = ckv_ref[0, span, cols], ckv_ref[1, span, cols]
            dk = dv = None
            for h in range(2):
                weights = jnp.exp(nt(k, qh[h]) - lse[h])
                ds = (weights * (nt(v, doh[h]) - delta[h])).astype(BF)
                a, b = nn(weights.astype(BF), doh[h]), nn(ds, qh[h])
                dv = a if dv is None else dv + a
                dk = b if dk is None else dk + b
                c = nn(ckt[h * size : (h + 1) * size, span], ds)
                dqt[h] = c if dqt[h] is None else dqt[h] + c
            dckv_ref[0, span, cols] = dk.astype(BF)
            dckv_ref[1, span, cols] = dv.astype(BF)
        dcq_ref[:, cols] = jnp.transpose(jnp.concatenate(dqt, axis=0), (1, 0)).astype(BF)
        return 0

    lax.fori_loop(0, width // pair, attend, 0)
    whole_weight(wq_ref, weight)

    def back_query(t, _):
        dn[:, line_tile(t)] = nt(dcq_ref[...], weight[line_tile(t), :])
        return 0

    lax.fori_loop(0, width // TILE, back_query, 0)
    dv, gain_out_ref[...] = norm_back(x1_ref[...], gain_ref[...], dn[...])
    dx1_ref[...] = dx2_ref[...] + dv
    whole_weight(wo_ref, weight)
    inner = dso_ref.shape[2]
    per = TILE // inner if inner < TILE else 1
    da = dx1_ref[...].astype(BF)
    for t in range(width // TILE):
        tile = nt(da, weight[t * TILE : (t + 1) * TILE, :]).astype(BF)
        for u in range(per):
            dso_ref[t * per + u] = tile[:, u * inner : (u + 1) * inner]


def middle_back(earlier, dx2, x1, gain, packed, cq, ckv, cot, lse, head_count, parts):
    rows, width = dx2.shape
    size = width // head_count
    count = ckv.shape[1]
    shapes = [
        jax.ShapeDtypeStruct((rows, width), F32), jax.ShapeDtypeStruct((1, width), F32),
        jax.ShapeDtypeStruct((rows, width), BF), jax.ShapeDtypeStruct(ckv.shape, BF),
        jax.ShapeDtypeStruct((parts, rows, width // parts), BF),
    ]
    return pl.pallas_call(
        leaving_out(functools.partial(middle_back_kernel, head_count), len(earlier)),
        grid=(1,),
        out_shape=shapes,
        in_specs=unread(earlier) + [
            whole((rows, width)), whole((rows, width)), whole((1, width)),
            packed_spec(packed, 0), packed_spec(packed, 1), packed_spec(packed, 2),
            whole((rows, width)), whole(ckv.shape), whole(cot.shape), whole(lse.shape),
        ],
        out_specs=[whole(s.shape) for s in shapes],
        scratch_shapes=[
            pltpu.VMEM((width, width), BF), pltpu.VMEM((rows, width), BF),
            pltpu.VMEM((2 * size, count), BF), pltpu.VMEM((rows, width), F32),
        ],
        compiler_params=params(),
        cost_estimate=cost(60 * rows * width * width, 24 * rows * width),
        name="middle_back",
    )(*earlier, dx2, x1, gain, packed, packed, packed, cq, ckv, cot, lse)


def middle_grad_kernel(
    dx2_ref, x1_ref, gain_ref, cob_ref, dcq_ref, dckv_ref, source_ref, ob_ref, dx1_ref, wk_ref, wv_ref,
    g_ref, wk, wv, left, left_source,
):
    width = x1_ref.shape[1]
    parts, shards, _, own, _ = wk_ref.shape
    layout = (parts, shards, 5, own)
    tail = shards * 5 * own
    piece = g_ref.shape[1] - tail
    whole_weight(wk_ref, wk)
    whole_weight(wv_ref, wv)
    for t in range(width // TILE):
        span = slice(t * TILE, (t + 1) * TILE)
        value = (nt(dckv_ref[0], wk[span, :]) + nt(dckv_ref[1], wv[span, :])).astype(BF)
        for c in range(parts):
            g_ref[c, tail : tail + piece, span] = value[c * piece : (c + 1) * piece]

    def product(which, lhs, right):
        def tile(t, _):
            cols = line_tile(t)
            store_rows(g_ref, layout, which, cols, nn(lhs[...], right(cols)).astype(BF))
            return 0

        lax.fori_loop(0, width // TILE, tile, 0)

    left[...] = jnp.transpose(ob_ref[...], (1, 0))
    product(0, left, lambda cols: dx1_ref[:, cols].astype(BF))
    x1 = x1_ref[...]
    left[...] = jnp.transpose((x1 * inverse_rms(x1) * gain_ref[...]).astype(BF), (1, 0))
    product(1, left, lambda cols: dcq_ref[:, cols])
    left[...] = jnp.transpose(cob_ref[...], (1, 0))
    product(2, left, lambda cols: dx2_ref[:, cols].astype(BF))
    left_source[...] = jnp.transpose(source_ref[...].reshape(-1, width), (1, 0))
    product(3, left_source, lambda cols: dckv_ref[0, :, cols])
    product(4, left_source, lambda cols: dckv_ref[1, :, cols])


def middle_grads(dx2, x1, gain, cob, dcq, dckv, gathered, ob, dx1, packed):
    rows, width = dx2.shape
    count = dckv.shape[1]
    parts, shards, _, own, _ = packed.shape
    tokens = whole((rows, width))
    shape = (parts, shards * 5 * own + count // parts, width)
    return pl.pallas_call(
        middle_grad_kernel,
        grid=(1,),
        out_shape=jax.ShapeDtypeStruct(shape, BF),
        in_specs=[
            tokens, tokens, whole((1, width)), tokens, tokens, whole(dckv.shape), encoder_rows(gathered, rows), tokens, tokens,
            packed_spec(packed, 3), packed_spec(packed, 4),
        ],
        out_specs=whole(shape),
        scratch_shapes=[
            pltpu.VMEM((width, width), BF), pltpu.VMEM((width, width), BF),
            pltpu.VMEM((width, rows), BF), pltpu.VMEM((width, count), BF),
        ],
        compiler_params=params(),
        cost_estimate=cost(46 * rows * width * width, 24 * rows * width),
        name="middle_grads",
    )(dx2, x1, gain, cob, dcq, dckv, gathered, ob, dx1, packed, packed)


def final_kernel(d_ref, w_ref, states_ref, gain_ref, dx1_ref, out_ref):
    dn = None
    for s in range(d_ref.shape[0]):
        part = nt(d_ref[s], w_ref[s])
        dn = part if dn is None else dn + part
    dv, _ = norm_back(states_ref[...].astype(F32), gain_ref[...], dn)
    out_ref[...] = dx1_ref[...] + dv


def final_back(dqkv, weights, states, gain, dx1, tile=128):
    parts, rows, inner = dqkv.shape
    width = states.shape[1]
    return pl.pallas_call(
        final_kernel,
        grid=(rows // tile,),
        out_shape=jax.ShapeDtypeStruct((rows, width), F32),
        in_specs=[
            pl.BlockSpec((parts, tile, inner), lambda i: (0, i, 0)),
            whole(weights.shape),
            pl.BlockSpec((tile, width), lambda i: (i, 0)),
            whole((1, width)),
            pl.BlockSpec((tile, width), lambda i: (i, 0)),
        ],
        out_specs=pl.BlockSpec((tile, width), lambda i: (i, 0)),
        compiler_params=params(),
        cost_estimate=cost(6 * rows * width * width, 12 * rows * width),
        name="final_back",
    )(dqkv, weights, states, gain, dx1)


def first_kernel(states_ref, gain_ref, w_ref, out_ref):
    x = states_ref[0].astype(F32)
    n = (x * inverse_rms(x) * gain_ref[...]).astype(BF)
    out_ref[...] = nn(n, w_ref[...]).astype(BF)


def first_projection(gathered, gain, weight, rows):
    parts, _, width = gathered.shape
    cols = weight.shape[1]
    return pl.pallas_call(
        first_kernel,
        grid=(parts,),
        out_shape=jax.ShapeDtypeStruct((parts * rows, cols), BF),
        in_specs=[
            pl.BlockSpec((1, rows, width), lambda i: (i, 0, 0)), whole((1, width)), whole((width, cols)),
        ],
        out_specs=pl.BlockSpec((rows, cols), lambda i: (i, 0)),
        compiler_params=params(),
        cost_estimate=cost(4 * parts * rows * width * cols, 2 * parts * rows * (width + cols)),
        name="first_projection",
    )(gathered, gain, weight)


def last_kernel(states_ref, gain_ref, w_ref, d_ref, gw_ref, gain_out_ref, acc_ref):
    step = pl.program_id(0)
    x = states_ref[0].astype(F32)
    n = (x * inverse_rms(x) * gain_ref[...]).astype(BF)
    g = lax.dot_general(d_ref[...], n, (((0,), (0,)), ((), ())), preferred_element_type=F32)

    @pl.when(step == 0)
    def _():
        acc_ref[...] = g

    @pl.when(step > 0)
    def _():
        acc_ref[...] += g

    @pl.when(step == pl.num_programs(0) - 1)
    def _():
        total = jnp.transpose(acc_ref[...], (1, 0))
        if len(gw_ref.shape) == 2:
            gw_ref[...] = total.astype(BF)
        else:
            shards, piece, wide = gw_ref.shape
            rows = total.shape[0] // shards
            for z in range(shards):
                block = total[z * rows : (z + 1) * rows].astype(BF)
                stacked = jnp.concatenate([block[:, i * 128 : (i + 1) * 128] for i in range(3)], axis=0)
                for b in range(wide // 128):
                    gw_ref[z, :, b * 128 : (b + 1) * 128] = stacked[b * piece : (b + 1) * piece]
        gain_out_ref[...] = jnp.sum(total * w_ref[...].astype(F32), axis=1, keepdims=True)


def last_projection(gathered, gain, weight, grads, rows, shards):
    parts, _, width = gathered.shape
    cols = weight.shape[1]
    shape = (shards, cols // shards, width) if shards else (width, cols)
    return pl.pallas_call(
        last_kernel,
        grid=(parts,),
        out_shape=(jax.ShapeDtypeStruct(shape, BF), jax.ShapeDtypeStruct((width, 1), F32)),
        in_specs=[
            pl.BlockSpec((1, rows, width), lambda i: (i, 0, 0)), whole((1, width)), whole((width, cols)),
            pl.BlockSpec((rows, cols), lambda i: (i, 0)),
        ],
        out_specs=[whole(shape), whole((width, 1))],
        scratch_shapes=[pltpu.VMEM((cols, width), F32)],
        compiler_params=params(),
        cost_estimate=cost(4 * parts * rows * width * cols, 2 * parts * rows * (width + cols)),
        name="last_projection",
    )(gathered, gain, weight, grads)


def unpack_kernel(own, piece, rest_ref, *outs):
    parts, total, width = rest_ref.shape
    first = 5 * own
    rows, inner = outs[6].shape[0], width // parts
    down_at = first + piece + 16
    down, half = total - down_at, width // 2
    for c in range(parts):
        for i in range(5):
            outs[i][c * own : (c + 1) * own, :] = rest_ref[c, i * own : (i + 1) * own, :].astype(F32)
        for i in range(2):
            start = ((c // 2) * 2 + i) * down
            value = rest_ref[c, down_at:total, i * half : (i + 1) * half]
            outs[5][start : start + down, (c % 2) * half : (c % 2 + 1) * half] = value.astype(F32)
        for b in range(width // 128):
            low, end = b * piece, (b + 1) * piece
            while low < end:
                which, row = low // rows, low % rows
                count = min(end - low, rows - row)
                at = first + low - b * piece
                value = rest_ref[c, at : at + count, b * 128 : (b + 1) * 128]
                outs[6 + which][row : row + count, c * inner : (c + 1) * inner] = value.astype(F32)
                low += count


def unpack(rest, own, piece, rows, inner):
    parts, total, width = rest.shape
    down_rows = (total - 5 * own - piece - 16) * parts
    square = jax.ShapeDtypeStruct((rows, width), F32)
    shapes = [square] * 5 + [jax.ShapeDtypeStruct((down_rows, width), F32)] + [square] * 3
    return pl.pallas_call(
        functools.partial(unpack_kernel, own, piece),
        grid=(1,),
        out_shape=shapes,
        in_specs=[whole(rest.shape)],
        out_specs=[whole(v.shape) for v in shapes],
        compiler_params=params(),
        cost_estimate=cost(0, 6 * rest.size),
        name="unpack",
    )(rest)


CTX = ("plane", "core")


def copies(piece):
    return jnp.broadcast_to(piece[None], (lax.axis_size("fsdp"),) + piece.shape)


def spread(piece):
    return lax.all_to_all(copies(piece), "fsdp", 0, 0, tiled=True)


def collect(parts, *earlier):
    parts = lax.all_to_all(parts, "fsdp", 0, 0, tiled=True)
    if earlier:
        parts = after(parts, *earlier)
    return jnp.sum(parts.astype(F32), axis=0).astype(BF)


def collect_far(parts):
    count, mine = lax.axis_size("fsdp"), lax.axis_index("fsdp")
    if count > 4:
        return collect(parts).astype(F32)
    total = take(parts, mine, 0).astype(F32)
    for step in range(1, count):
        for sign in (1, -1):
            message = take(parts, jnp.clip(mine + sign * step, 0, count - 1), 0)
            pairs = [(i, i + sign * step) for i in range(count) if 0 <= i + sign * step < count]
            total = total + lax.ppermute(message, "fsdp", pairs).astype(F32)
    return total


def nothing(*refs):
    pass


def after(value, *earlier):
    return pl.pallas_call(
        nothing,
        out_shape=jax.ShapeDtypeStruct(value.shape, value.dtype),
        in_specs=[pl.BlockSpec(memory_space=pl.ANY)] * (1 + len(earlier)),
        out_specs=pl.BlockSpec(memory_space=pl.ANY),
        input_output_aliases={0: 0},
        name="after",
    )(value, *earlier)


def own_rows(shard):
    rows = shard.shape[0] // lax.axis_size(CTX)
    return lax.dynamic_slice_in_dim(shard, lax.axis_index(CTX) * rows, rows, 0)


def swap(value, axis):
    return lax.ppermute(value, axis, [(0, 1), (1, 0)])


def take(value, index, axis):
    return lax.dynamic_index_in_dim(value, index, axis, keepdims=False)


def gather_down(shard, earlier):
    rows, width = shard.shape
    start = lax.axis_index("core") * (width // 2)
    mine = after(copies(lax.dynamic_slice_in_dim(shard, start, width // 2, 1)), earlier)
    mine = lax.all_to_all(mine, "fsdp", 0, 0, tiled=True).reshape(-1, width // 2)
    return mine, swap(mine, "core")


def reduce_planes(half, later):
    planes, width = lax.axis_size("plane"), half.shape[1]
    if planes != 4:
        return lax.psum_scatter(half, "plane", scatter_dimension=0, tiled=True)
    plane = lax.axis_index("plane")
    quarters = half.reshape(planes, -1, width)
    total = take(quarters, plane, 0).astype(F32)
    for step in range(1, planes):
        message = take(quarters, plane ^ step, 0)
        got = lax.ppermute(message, "plane", [(i, i ^ step) for i in range(planes)])
        total = total + after(got, later).astype(F32)
    return total.astype(BF)


def on_device(
    states, positions, segments, encoded, cotangent,
    self_gain, self_query, self_key, self_value, self_output, bias_table,
    cross_gain, cross_query, cross_key, cross_value, cross_output,
    feed_gain, gate_weight, up_weight, down_weight,
):
    parts, shards = lax.axis_size(CTX), lax.axis_size("fsdp")
    place = lax.axis_index(CTX)
    core = lax.axis_index("core").astype(jnp.int32).reshape(1)
    local, width = states.shape[1:]
    head_count = bias_table.shape[1]
    size = width // head_count
    heads = head_count // parts
    inner = heads * size
    blocks = local // BLK
    shard_width = self_gain.shape[0]
    hidden_width = gate_weight.shape[1]
    own = shard_width // parts
    aligned = own % 16 == 0

    def arranged(pieces):
        if aligned:
            return pieces
        matrices, columns = pieces.shape[2], pieces.shape[4]
        return pieces.transpose(2, 1, 0, 3, 4).reshape(1, 1, matrices, width, columns)

    def scattered(grads):
        if aligned:
            return grads
        matrices, columns = grads.shape[2], grads.shape[4]
        return grads.reshape(matrices, shards, parts, own, columns).transpose(2, 1, 0, 3, 4)

    gathered = lax.all_gather(jnp.concatenate([states[0], encoded[0]], axis=0), CTX, axis=0, tiled=False)
    columns = lax.dynamic_slice_in_dim(
        jnp.stack([self_query, self_key, self_value], axis=1), place * inner, inner, 2
    ).reshape(shard_width, 3 * inner)
    small = jnp.concatenate([self_gain, cross_gain, feed_gain, bias_table.reshape(-1)])
    small_width = small.shape[0]
    small = jnp.pad(small, (0, 16 * 3 * inner - small_width)).reshape(16, 3 * inner)
    first_pos, first_seg = positions[0, ::BLK], segments[0, ::BLK]
    canon = jnp.where(
        first_seg == 0,
        first_pos // BLK,
        PROMPT // BLK + (first_seg - 1) * (CLEN // BLK) + (first_pos - PROMPT) // BLK,
    )
    canon_all = lax.all_gather(canon, CTX, axis=0, tiled=True)
    slots = jnp.argmax(canon_all[None, :] == jnp.arange(blocks * parts)[:, None], axis=1).astype(jnp.int32)
    line = jnp.concatenate([columns, small], axis=0)
    squares = jnp.stack([own_rows(w) for w in (self_output, cross_query, cross_output, cross_key, cross_value)], axis=0)
    squares = after(spread(squares), slots)
    wide = copies(jnp.stack([own_rows(gate_weight), own_rows(up_weight)], axis=0))
    line = after(spread(after(line, squares)), wide)
    qkv_weight = line[:, :shard_width].reshape(width, 3 * inner)
    small = line[:, shard_width:].reshape(shards, -1)[:, :small_width].astype(F32)
    gains = [small[:, i * shard_width : (i + 1) * shard_width].reshape(1, width) for i in range(3)]
    table = small[:, 3 * shard_width :].reshape(BUCKETS, head_count)
    own_table = lax.dynamic_slice_in_dim(table, place * heads, heads, 1).reshape(-1)

    wide = lax.all_to_all(after(wide, line), "fsdp", 0, 0, tiled=True)
    squares = lax.all_gather(squares, CTX, axis=0, tiled=False)

    prompt_tiles = PROMPT // TILE
    qkv = first_projection(gathered, gains[0], qkv_weight, local).reshape(parts * blocks, BLK, 3 * inner)
    o, ot, lse = sa_fwd(slots, own_table, qkv, heads, prompt_tiles)
    o = lax.all_to_all(o.reshape(parts, local, inner), CTX, 0, 0, tiled=True)

    wide = lax.all_gather(after(wide, o), CTX, axis=0, tiled=False)
    squares, wide = arranged(squares), arranged(wide)
    down, other_down = gather_down(down_weight, o)
    ckv = source_projection(gathered, local, squares)
    ob, x1, cq, cob, cot, cross_lse, x2, n3 = middle_forward(
        o, states[0], gains[1], gains[2], squares, ckv, head_count
    )
    qkv_all = lax.all_gather(after(qkv_weight, x2), CTX, axis=0, tiled=False)
    hidden, dx2, feed_gain_part, g_wide, g_down, g_other = feed_forward(
        core, n3, cotangent[0], x2, gains[2], wide, down, other_down
    )
    g_wide = lax.psum_scatter(scattered(g_wide), CTX, scatter_dimension=0, tiled=False)
    g_down = (g_down.astype(F32) + swap(g_other, "core").astype(F32)).astype(BF).reshape(shards, -1, width // 2)
    dx1, cross_gain_part, dcq, dckv, dso = middle_back(
        (qkv_all,), dx2, x1, gains[1], squares, cq, ckv, cot, cross_lse, head_count, parts
    )
    dso = lax.all_to_all(dso, CTX, 0, 0, tiled=True).reshape(parts * blocks, BLK, inner)
    g_squares = middle_grads(dx2, x1, gains[1], cob, after(dcq, g_down), dckv, gathered, ob, dx1, squares)
    if not aligned:
        encoded_part = g_squares[0, 5 * width :].reshape(parts, -1, width)
        g_squares = scattered(g_squares[0, : 5 * width].reshape(1, 1, 5, width, width)).reshape(parts, -1, width)
        g_squares = jnp.concatenate([g_squares, encoded_part], axis=1)
    middle = prompt_tiles + (blocks * parts * BLK // TILE - prompt_tiles) // 4
    g_squares = after(g_squares, dso)
    held = sa_bwd((g_squares,), slots, own_table, qkv, dso, ot, lse, heads, prompt_tiles, 0, middle)
    g_squares = lax.psum_scatter(g_squares, CTX, scatter_dimension=0, tiled=False)
    g_down = collect(after(g_down, dso), held[0])
    dqkv, dtable = sa_bwd(
        (g_wide,), slots, own_table, qkv, dso, ot, lse, heads, prompt_tiles, middle,
        blocks * parts * BLK // TILE, held,
    )
    g_wide = collect(after(g_wide, g_down), dqkv)
    g_down = reduce_planes(g_down, dqkv)
    dqkv_local = lax.all_to_all(after(dqkv, g_wide, g_down).reshape(parts, local, 3 * inner), CTX, 0, 0, tiled=True)
    g_down = jnp.concatenate([g_down[: g_down.shape[0] // 2], g_down[g_down.shape[0] // 2 :]], axis=1)
    grads = dqkv.reshape(parts * local, 3 * inner)
    compact = aligned and inner == 128 and (3 * inner // shards) % 16 == 0
    g_qkv, self_gain_part = last_projection(gathered, gains[0], qkv_weight, grads, local, shards if compact else 0)
    table_part = jnp.zeros((BUCKETS, head_count), F32)
    table_part = lax.dynamic_update_slice_in_dim(table_part, dtable[:, :, 0].T, place * heads, 1)
    sums = [self_gain_part[:, 0] / gains[0][0], cross_gain_part[0], feed_gain_part[0]]
    sums = jnp.concatenate([v.reshape(shards, shard_width) for v in sums] + [table_part.reshape(shards, -1)], axis=1)
    if compact:
        sums = jnp.pad(sums, ((0, 0), (0, 16 * width - small_width))).reshape(shards, 16, width).astype(BF)
        last = jnp.concatenate([g_qkv, sums], axis=1)
    else:
        sums = jnp.pad(sums, ((0, 0), (0, 16 * 3 * inner - small_width))).reshape(shards, 16, 3 * inner).astype(BF)
        last = jnp.concatenate([g_qkv.reshape(shards, shard_width, 3 * inner), sums], axis=1).reshape(shards, -1, width)
    g_squares = after(g_squares, g_wide, g_qkv)
    encoded_grad = g_squares[shards * 5 * own :].astype(F32)
    last_rows = last.shape[1]
    rest = jnp.concatenate([g_squares[: shards * 5 * own].reshape(shards, 5 * own, width), last], axis=1)
    rest = collect_far(rest).astype(BF)
    layer_out = layer_output((dqkv,), core, hidden, x2, down, other_down)
    states_grad = final_back(dqkv_local, qkv_all, states[0], gains[0], dx1)
    g_wide = lax.all_gather(g_wide, CTX, axis=0, tiled=False)
    rest = jnp.concatenate([rest, g_down], axis=0)
    rest = lax.all_gather(after(rest, g_wide, dqkv_local), CTX, axis=0, tiled=False)
    if compact:
        sums_at = 5 * own + g_qkv.shape[1]
        *g_squares, g_down, g_query, g_key, g_value = unpack(rest, own, g_qkv.shape[1], shard_width, inner)
        sums = jnp.sum(rest[:, sums_at].astype(F32), axis=0)
    else:
        last = rest[:, 5 * own : 5 * own + last_rows].reshape(parts, -1, 3 * inner)
        sums = jnp.sum(last[:, shard_width:].reshape(parts, -1).astype(F32), axis=0)
        rest = rest.astype(F32)
        g_squares = rest[:, : 5 * own].reshape(parts, 5, own, width).transpose(1, 0, 2, 3).reshape(5, shard_width, width)
        g_down = rest[:, 5 * own + last_rows :].reshape(parts // 2, 2, -1, 2, width // 2).transpose(0, 3, 2, 1, 4)
        g_down = g_down.reshape(-1, width)
        g_qkv = last[:, :shard_width].astype(F32).reshape(parts, shard_width, 3, inner).transpose(2, 1, 0, 3)
        g_query, g_key, g_value = g_qkv.reshape(3, shard_width, width)
    gain_grads = [sums[i * shard_width : (i + 1) * shard_width] for i in range(3)]
    table_grad = sums[3 * shard_width : small_width].reshape(-1, head_count)
    g_wide = g_wide.astype(F32).transpose(1, 0, 2, 3).reshape(2, shard_width, hidden_width)
    return (
        layer_out[None], states_grad[None], encoded_grad[None],
        gain_grads[0], g_query, g_key, g_value, g_squares[0], table_grad,
        gain_grads[1], g_squares[1], g_squares[3], g_squares[4], g_squares[2],
        gain_grads[2], g_wide[0], g_wide[1], g_down,
    )


def solution(mesh):
    ctx, fsdp = mesh.devices.shape
    split = Mesh(mesh.devices.reshape(ctx // 2, 2, fsdp), ("plane", "core", "fsdp"))
    tokens, matrix, vector = P("fsdp", CTX, None), P("fsdp", None), P("fsdp")
    place = P("fsdp", CTX)
    return jax.shard_map(
        on_device,
        mesh=split,
        in_specs=(tokens, place, place, tokens, tokens)
        + (vector, matrix, matrix, matrix, matrix, matrix)
        + (vector, matrix, matrix, matrix, matrix)
        + (vector, matrix, matrix, matrix),
        out_specs=(tokens, tokens, tokens)
        + (vector, matrix, matrix, matrix, matrix, matrix)
        + (vector, matrix, matrix, matrix, matrix)
        + (vector, matrix, matrix, matrix),
        check_vma=False,
    )
```
